32 devices in a mesh: grp: 2 (over x), len: 16 (over z, y, core).
Axes of the slice: x: 2, y: 2, z: 4, core: 2. Of those that a mesh axis runs over, the one named last changes fastest.
Arguments:
- tin_temp: float32 [64, 512, 1024], P(None, ('grp', 'len')), parts along dimension 1, may hold values from -6 to 6
- flow_code: int32 [64, 512, 1024], P(None, ('grp', 'len')), parts along dimension 1, may hold values from 0 to 3
- speeds: float32 [2, 64], replicated, may hold values from 0.02 to 0.12
- floor_temp: float32 [32, 48, 64, 256], P(('grp', 'len')), parts along dimension 0, may hold values from -6 to 6
- material: int32 [32, 48, 64, 256], P(('grp', 'len')), parts along dimension 0, may hold values from 0 to 2
- conductivity: float32 [3], replicated, may hold values from 0.03 to 0.15
Outputs:
- tin_out: float32 [64, 512, 1024], P(None, ('grp', 'len')), parts along dimension 1
- floor_out: float32 [32, 48, 64, 256], P(('grp', 'len')), parts along dimension 0
The draws below stay inside these ranges and needn't reach their ends.
There are 2 independent parts, one for each index of `grp`. The reference program is written for one: setup_inputs(seed, part) draws one part's arguments, and reference() takes and returns one part's arrays. A program takes and returns all parts, laid end to end along the dimension named above; an argument that names none is the same for every part. Nothing has to cross between parts.
Inputs may be any that keep to these rules, and one draw needn't show every extreme that they name: flow_code % 2 is 0 where the tin cell takes its length upwind value from the lower length index and 1 from the higher; flow_code // 2 likewise across the width. material ids index conductivity.
All inputs are finite; a program needn't handle non-finite values.
Results may differ from the reference program's by a relative error of at most 0.0003.
Values sent between devices are 32-bit elements; how exact they have to be, the bound alone decides.
No kernel may reach another device: no remote copies, remote signals or barrier semaphores. Data moves between devices by JAX's collectives and lax.ppermute only.
A program may use at most 128 MiB of HBM per device.

```python
import jax
import jax.numpy as jnp

NY = 1024
ZT = 64
ZR = 48
TILE_Y = 4
MATS = 3
SWEEPS = 2
NX = 256
TILE_X = 4
CXR = 64
CYR = 256
N_LEN = 16


def plant(drawn, own_key, least, high):
    place = [jax.random.randint(jax.random.fold_in(own_key, axis), (), 0, length) for axis, length in enumerate(drawn.shape)]
    longest = drawn.shape.index(max(drawn.shape))
    neighbour = place[:longest] + [(place[longest] + 1) % drawn.shape[longest]] + place[longest + 1:]
    return drawn.at[tuple(place)].set(least).at[tuple(neighbour)].set(high)


def levels(rng, dims, cuts, least, top_value):
    factor_of = 1.0
    for axis_at, blocks in cuts:
        draws = jax.random.uniform(jax.random.fold_in(jax.random.fold_in(rng, 6), axis_at), (blocks,), jnp.float32, least / len(cuts), top_value / len(cuts))
        factor_of = factor_of * jnp.repeat(jnp.exp(draws), dims[axis_at] // blocks).reshape((-1,) + (1,) * (len(dims) - 1 - axis_at))
    return factor_of


def scatter_about(own_key, shape, deviation, limit, cuts=(), dtype=jnp.bfloat16):
    values = deviation * jax.random.normal(own_key, shape, jnp.float32)
    if cuts:
        values = values * levels(own_key, shape, cuts, -0.22, 0.18)
    return jnp.clip(values, -limit, limit).astype(dtype)


def setup_inputs(seed: int = 0, part: int = 0) -> dict:
    seeds = jax.random.split(jax.random.key(seed), 7)
    part_keys = jax.random.split(jax.random.fold_in(seeds[6], part), 7)
    tin_temp = scatter_about(part_keys[0], (ZT, NX, NY), 1.0, 6.0, ((1, 16),), jnp.float32)
    flow_code = plant(jax.random.randint(part_keys[1], (ZT, NX, NY), 0, 4), jax.random.fold_in(part_keys[1], 1), 0, 3).astype(jnp.int32)
    speeds = jnp.clip(jax.random.uniform(seeds[2], (2, ZT), jnp.float32, 0.02, 0.12), 0.02, 0.12)
    floor_temp = scatter_about(part_keys[3], (N_LEN, ZR, CXR, CYR), 1.0, 6.0, ((0, 16),), jnp.float32)
    material = plant(jax.random.randint(part_keys[4], (N_LEN, ZR, CXR, CYR), 0, MATS), jax.random.fold_in(part_keys[4], 1), 0, MATS - 1).astype(jnp.int32)
    conductivity = jnp.clip(jax.random.uniform(seeds[5], (MATS,), jnp.float32, 0.03, 0.15), 0.03, 0.15)
    return {"tin_temp": tin_temp, "flow_code": flow_code, "speeds": speeds, "floor_temp": floor_temp, "material": material, "conductivity": conductivity}


KT = 0.1
HT = 0.2
HR = 0.2


def lookup(material, conductivity):
    result = jnp.zeros(material.shape, jnp.float32)
    for material_id in range(conductivity.shape[0]):
        result = result + jnp.where(material == material_id, conductivity[material_id], 0.0)
    return result


def tin_update(tin_field, padded, flow_code, speeds, top_plane):
    x_minus = padded[:, :-2, 1:-1]
    x_plus = padded[:, 2:, 1:-1]
    y_minus = padded[:, 1:-1, :-2]
    y_plus = padded[:, 1:-1, 2:]
    layer_above = jnp.concatenate([tin_field[1:], tin_field[-1:]], 0)
    layer_below = jnp.concatenate([tin_field[:1], tin_field[:-1]], 0)
    spread = x_minus + x_plus + y_minus + y_plus + layer_above + layer_below - 6.0 * tin_field
    speed_x = speeds[0][:, None, None]
    speed_y = speeds[1][:, None, None]
    carried = jnp.where(flow_code % 2 == 0, speed_x * (x_minus - tin_field), speed_x * (x_plus - tin_field))
    carried = carried + jnp.where(flow_code // 2 == 0, speed_y * (y_minus - tin_field), speed_y * (y_plus - tin_field))
    layer_ids = jnp.arange(tin_field.shape[0])[:, None, None]
    contact = jnp.where(layer_ids == 0, HT * (top_plane[None] - tin_field[0:1]), 0.0)
    return tin_field + KT * spread + carried + contact


def floor_update(floor_field, conduct, along_x, conduct_x, along_y, conduct_y, bottom_tin):
    lateral = 0.5 * (conduct + conduct_x[:, :-2]) * (along_x[:, :-2] - floor_field)
    lateral = lateral + 0.5 * (conduct + conduct_x[:, 2:]) * (along_x[:, 2:] - floor_field)
    lateral = lateral + 0.5 * (conduct + conduct_y[:, :, :-2]) * (along_y[:, :, :-2] - floor_field)
    lateral = lateral + 0.5 * (conduct + conduct_y[:, :, 2:]) * (along_y[:, :, 2:] - floor_field)
    field_above = jnp.concatenate([floor_field[:1], floor_field[:-1]], 0)
    conduct_above = jnp.concatenate([conduct[:1], conduct[:-1]], 0)
    field_below = jnp.concatenate([floor_field[1:], jnp.zeros_like(floor_field[:1])], 0)
    conduct_below = jnp.concatenate([conduct[1:], jnp.zeros_like(conduct[:1])], 0)
    vertical = 0.5 * (conduct + conduct_above) * (field_above - floor_field)
    vertical = vertical + 0.5 * (conduct + conduct_below) * (field_below - floor_field)
    layer_ids = jnp.arange(floor_field.shape[0])[:, None, None]
    contact = jnp.where(layer_ids == 0, HR * (bottom_tin[None] - floor_field[0:1]), 0.0)
    return floor_field + lateral + vertical + contact


def to_grid(tile_array):
    shaped = tile_array.reshape(TILE_X, TILE_Y, ZR, CXR, CYR)
    return shaped.transpose(2, 0, 3, 1, 4).reshape(ZR, NX, NY)


def to_tiles(grid_array):
    shaped = grid_array.reshape(ZR, TILE_X, CXR, TILE_Y, CYR)
    return shaped.transpose(1, 3, 0, 2, 4).reshape(N_LEN, ZR, CXR, CYR)


def reference(tin_temp, flow_code, speeds, floor_temp, material, conductivity):
    tin_field = tin_temp
    floor_field = to_grid(floor_temp)
    conduct = lookup(to_grid(material), conductivity)
    pad_x = ((0, 0), (1, 1), (0, 0))
    pad_y = ((0, 0), (0, 0), (1, 1))
    conduct_x = jnp.pad(conduct, pad_x)
    conduct_y = jnp.pad(conduct, pad_y)
    for repeat in range(SWEEPS):
        bottom_tin = tin_field[0]
        top_plane = floor_field[0]
        padded = jnp.pad(tin_field, ((0, 0), (1, 1), (1, 1)))
        tin_next = tin_update(tin_field, padded, flow_code, speeds, top_plane)
        floor_next = floor_update(floor_field, conduct, jnp.pad(floor_field, pad_x), conduct_x,
                                  jnp.pad(floor_field, pad_y), conduct_y, bottom_tin)
        tin_field = tin_next
        floor_field = floor_next
    return tin_field, to_tiles(floor_field)
```

```python
import functools

import jax
import jax.numpy as jnp
from jax import lax
from jax.experimental import pallas as pl
from jax.experimental.pallas import tpu as pltpu
from jax.sharding import PartitionSpec as P

TILE_Y = 4
KT = 0.1
HT = 0.2
HR = 0.2
LANES = 128
SUBL = 8
F32 = jnp.float32
ANY = pl.BlockSpec(memory_space=pl.ANY)
VMEM = pl.BlockSpec(memory_space=pltpu.VMEM)
SMEM = pl.BlockSpec(memory_space=pltpu.SMEM)
PARAMS = pltpu.CompilerParams(vmem_limit_bytes=48 * 1024 * 1024)


def shape(dims, dtype=F32):
    return jax.ShapeDtypeStruct(dims, dtype)


def cost(flops, nbytes):
    return pl.CostEstimate(flops=flops, bytes_accessed=nbytes, transcendentals=0)


def place():
    pos = lax.axis_index("len")
    group, column = pos // TILE_Y, pos % TILE_Y
    return group, column, pos % 2 == 1, group % 2 == 1


def iotas():
    rows = lax.broadcasted_iota(jnp.int32, (SUBL, LANES), 0)
    lanes = lax.broadcasted_iota(jnp.int32, (SUBL, LANES), 1)
    return rows, lanes


def swaps(kind):
    count = lax.axis_size("len")
    partner = {
        "e1": lambda i: i ^ 1,
        "e2": lambda i: i + 1 if i % 2 else i - 1,
        "x2": lambda i: i ^ 2,
        "x3": lambda i: i ^ 3,
        "z1": lambda i: i ^ TILE_Y,
        "z2": lambda i: i + TILE_Y if (i // TILE_Y) % 2 else i - TILE_Y,
    }[kind]
    return [(i, partner(i)) for i in range(count) if 0 <= partner(i) < count]


def swap(value, kind):
    return lax.ppermute(value, "len", swaps(kind))


def select_copy(cond, first, second, sem):
    @pl.when(cond)
    def _():
        pltpu.make_async_copy(*first, sem).start()

    @pl.when(jnp.logical_not(cond))
    def _():
        pltpu.make_async_copy(*second, sem).start()


def half_lookup(ids, cond):
    value = jnp.full(ids.shape, 0.5 * cond[0], F32)
    for i in range(1, cond.shape[0]):
        value = jnp.where(ids == i, 0.5 * cond[i], value)
    return value


def pack_rows_kernel(u, g, m, cond, e1, e2, x2, z1, z2, mrow, sem):
    group, column, odd, godd = place()
    nx, cx = u.shape[1], g.shape[1]
    nr, width = g.shape[0], g.shape[2]
    first, last = 0, nx - 1
    select_copy(odd, (u.at[:, last, :], e2), (u.at[:, first, :], e2), sem.at[0])
    select_copy(odd, (u.at[:, first, :], e1), (u.at[:, last, :], e1), sem.at[1])
    top = (g.at[:, 0, :], z1.at[:nr]), (g.at[:, cx - 1, :], z1.at[:nr])
    select_copy(godd, top[0], top[1], sem.at[2])
    top = (g.at[:, 0, :], z2.at[:nr]), (g.at[:, cx - 1, :], z2.at[:nr])
    select_copy(godd, top[1], top[0], sem.at[3])
    rows = [(m.at[:, r, :], mrow.at[s]) for r, s in ((0, 0), (cx - 1, 1))]
    for i, (src, dst) in enumerate(rows):
        pltpu.make_async_copy(src, dst, sem.at[4 + i]).start()
    other = column ^ 2
    lane = pl.multiple_of(other * width, LANES)
    row = pl.multiple_of(other * nx, SUBL)
    pltpu.make_async_copy(u.at[0, :, pl.ds(lane, width)], x2.at[:nx], sem.at[6]).start()
    pltpu.make_async_copy(g.at[0, pl.ds(row, nx), :], x2.at[nx:], sem.at[7]).start()
    for i, (src, dst) in enumerate(rows):
        pltpu.make_async_copy(src, dst, sem.at[4 + i]).wait()
    low, high = half_lookup(mrow[0], cond), half_lookup(mrow[1], cond)
    z1[nr:, :] = jnp.where(godd, low, high)
    z2[nr:, :] = jnp.where(godd, high, low)
    pltpu.make_async_copy(u.at[:, 0, :], e2, sem.at[0]).wait()
    pltpu.make_async_copy(u.at[:, 0, :], e1, sem.at[1]).wait()
    pltpu.make_async_copy(g.at[:, 0, :], z1.at[:nr], sem.at[2]).wait()
    pltpu.make_async_copy(g.at[:, 0, :], z2.at[:nr], sem.at[3]).wait()
    pltpu.make_async_copy(u.at[0, :, :width], x2.at[:nx], sem.at[6]).wait()
    pltpu.make_async_copy(g.at[0, :nx, :], x2.at[nx:], sem.at[7]).wait()


def put_columns(aux, cols):
    half = cols.shape[0] // 2
    aux[half:, :LANES] = cols[:half]
    aux[half:, LANES:] = cols[half:]


def pack_cols_kernel(u, g, m, cond, x1, x3, gv, mv, own_b, own_p, acc, sem):
    group, column, odd, godd = place()
    nx = u.shape[1]
    nr, cx, width = g.shape
    planes = [
        pltpu.make_async_copy(u.at[0], own_b, sem.at[0]),
        pltpu.make_async_copy(g.at[0], own_p, sem.at[1]),
    ]
    chunks = 4
    step = nr // chunks
    loads = []
    for c in range(chunks):
        at = pl.ds(c * step, step)
        loads.append(
            [
                pltpu.make_async_copy(g.at[at], gv.at[at], sem.at[2 + 2 * c]),
                pltpu.make_async_copy(m.at[at], mv.at[at], sem.at[3 + 2 * c]),
            ]
        )
    for copy in [c for pair in loads for c in pair] + planes:
        copy.start()
    rows, lanes = iotas()
    tiles = cx // SUBL
    right = width - LANES
    shift = LANES // 2
    sides = ((0, 0), (right, 1))
    carry = [jnp.zeros((SUBL, LANES), F32)] * (2 * tiles) + [
        jnp.zeros((SUBL, LANES), jnp.int32)
    ] * (2 * tiles)
    for c in range(chunks):
        for copy in loads[c]:
            copy.wait()

        def body(z, carry):
            carry = list(carry)
            at_g, at_k = lanes == z, lanes == z + shift
            for s, (lane, extra) in enumerate(sides):
                for t in range(tiles):
                    gt = gv[z, t * SUBL : (t + 1) * SUBL, lane : lane + LANES]
                    mt = mv[z, t * SUBL : (t + 1) * SUBL, lane : lane + LANES]
                    i = s * tiles + t
                    carry[i] = jnp.where(at_g, pltpu.roll(gt, z + extra, 1), carry[i])
                    i += 2 * tiles
                    carry[i] = jnp.where(
                        at_k, pltpu.roll(mt, z + shift + extra, 1), carry[i]
                    )
            return tuple(carry)

        carry = lax.fori_loop(c * step, (c + 1) * step, body, tuple(carry))
    is_k = lanes >= shift
    for s in range(2):
        for t in range(tiles):
            gt, mt = carry[s * tiles + t], carry[(2 + s) * tiles + t]
            acc[s, t * SUBL : (t + 1) * SUBL, :] = jnp.where(
                is_k, half_lookup(mt, cond), gt
            )
    put_columns(x1, jnp.where(odd, acc[0], acc[1]))
    inner = (column > 0) & (column < TILE_Y - 1)
    put_columns(x3, jnp.where(inner, jnp.where(odd, acc[1], acc[0]), 0.0))
    for copy in planes:
        copy.wait()
    put_planes(x1, own_b, own_p, column ^ 1)
    put_planes(x3, own_b, own_p, column ^ 3)


def put_planes(dst, b_plane, p_plane, other):
    nx, width = b_plane.shape[0], p_plane.shape[1]
    lane = pl.multiple_of(other * width, LANES)
    row = pl.multiple_of(other * nx, SUBL)
    dst[:nx, :] = b_plane[:, pl.ds(lane, width)]
    dst[nx : 2 * nx, :] = p_plane[pl.ds(row, nx), :]


def floor_kernel(
    emit, g, m, top_b, cond, cols1, cols3, z1, z2, x2, *rest
):
    nr, cx, width = g.shape
    nx = top_b.shape[1]
    if emit:
        out, gtop, cl, cr, o1, o2, kc, kr = rest[:8]
        rest = rest[8:]
    else:
        kc_in, kr_in, out = rest[:3]
        rest = rest[3:]
    gv, mv, kv, ov, fzv, gcol, grow, bv, sem = rest[:9]
    group, column, odd, godd = place()
    tiles, wide = cx // SUBL, width // LANES
    chunks = 6
    step = nr // chunks
    half = cx // 2
    def load(c):
        at = pl.ds(c * step, step)
        return (
            pltpu.make_async_copy(g.at[at], gv.at[at], sem.at[2 * c]),
            pltpu.make_async_copy(m.at[at], mv.at[at], sem.at[2 * c + 1]),
        )

    for copy in load(0):
        copy.start()
    base = 2 * chunks
    lane = pl.multiple_of(column * width, LANES)
    row = lambda other: pl.ds(pl.multiple_of(other * nx, SUBL), nx)
    pieces = [
        pltpu.make_async_copy(
            top_b.at[0, :, pl.ds(lane, width)], bv.at[row(column)], sem.at[base]
        ),
        pltpu.make_async_copy(cols1.at[:nx], bv.at[row(column ^ 1)], sem.at[base + 1]),
        pltpu.make_async_copy(x2.at[:nx], bv.at[row(column ^ 2)], sem.at[base + 2]),
        pltpu.make_async_copy(cols3.at[:nx], bv.at[row(column ^ 3)], sem.at[base + 3]),
    ]
    for copy in pieces:
        copy.start()
    for c in range(1, chunks):
        for copy in load(c):
            copy.start()
    for j in range(2):
        at, to = slice(j * LANES, (j + 1) * LANES), slice(j * half, (j + 1) * half)
        one, three = cols1[half:, at], cols3[half:, at]
        gcol[0, to, :] = jnp.where(odd, one, three)
        gcol[1, to, :] = jnp.where(odd, three, one)
    one, two = z1[...], z2[...]
    low, high = jnp.where(godd, one, two), jnp.where(godd, two, one)
    grow[0, :, :], grow[1, :, :] = low[:nr], high[:nr]
    if emit:
        kc[...] = gcol[...]
        kr[0, :, :], kr[1, :, :] = low[nr:], high[nr:]
        kcol, krow = kc, kr
    else:
        kcol, krow = kc_in, kr_in
    rows, lanes = iotas()
    r_first, r_last = rows == 0, rows == SUBL - 1
    l_first, l_last = lanes == 0, lanes == LANES - 1
    shift = LANES // 2
    fzv[...] = jnp.zeros_like(fzv)
    gv[nr, :, :] = jnp.zeros((cx, width), F32)
    kv[nr, :, :] = jnp.zeros((cx, width), F32)
    scal = [0.5 * cond[i] for i in range(cond.shape[0])]

    def convert(c):
        def body(z, _):
            for t in range(tiles):
                for j in range(wide):
                    at = (z, slice(t * SUBL, (t + 1) * SUBL), slice(j * LANES, (j + 1) * LANES))
                    ids = mv[at]
                    value = jnp.full(ids.shape, scal[0], F32)
                    for i in range(1, len(scal)):
                        value = jnp.where(ids == i, scal[i], value)
                    kv[at] = value
            return 0

        lax.fori_loop(c * step, (c + 1) * step, body, 0)

    def layer(start, offset):
        z = start + offset

        def tile(ref, t):
            return [
                ref[z, t * SUBL : (t + 1) * SUBL, j * LANES : (j + 1) * LANES]
                for j in range(wide)
            ]

        def row_of(ref, s):
            block = ref[s, pl.ds(start, SUBL), :][offset : offset + 1]
            return [
                jnp.broadcast_to(block[:, j * LANES : (j + 1) * LANES], (SUBL, LANES))
                for j in range(wide)
            ]

        glow, ghigh, klow, khigh = row_of(grow, 0), row_of(grow, 1), row_of(krow, 0), row_of(krow, 1)
        up = lambda vs: [pltpu.roll(v, SUBL - 1, 0) for v in vs]
        gt, kt = tile(gv, 0), tile(kv, 0)
        gu, ku = up(gt), up(kt)
        prev = [(k + kl) * (g_ - gl) for k, kl, g_, gl in zip(kt, klow, gt, glow)]
        for t in range(tiles):
            rs = slice(t * SUBL, (t + 1) * SUBL)
            if t + 1 < tiles:
                gn, kn = tile(gv, t + 1), tile(kv, t + 1)
                gun, kun = up(gn), up(kn)
            else:
                gun, kun = ghigh, khigh
            gcl = pltpu.roll(gcol[0, rs, :], lax.rem(LANES - z, LANES), 1)
            gcr = pltpu.roll(gcol[1, rs, :], LANES - 1 - z, 1)
            kcl = pltpu.roll(kcol[0, rs, :], lax.rem(LANES + shift - z, LANES), 1)
            kcr = pltpu.roll(kcol[1, rs, :], lax.rem(LANES + shift - 1 - z, LANES), 1)
            gl = [pltpu.roll(v, LANES - 1, 1) for v in gt] + [gcr]
            kl = [pltpu.roll(v, LANES - 1, 1) for v in kt] + [kcr]
            west = (kt[0] + kcl) * (gt[0] - gcl)
            new_prev = []
            for j in range(wide):
                g_, k_ = gt[j], kt[j]
                xp = jnp.where(r_last, gun[j], gu[j])
                kx = jnp.where(r_last, kun[j], ku[j])
                fx = (k_ + kx) * (xp - g_)
                fxd = pltpu.roll(fx, 1, 0)
                fxm = jnp.where(r_first, prev[j], fxd)
                new_prev.append(fxd)
                yp = jnp.where(l_last, gl[j + 1], gl[j])
                ky = jnp.where(l_last, kl[j + 1], kl[j])
                fy = (k_ + ky) * (yp - g_)
                fyd = pltpu.roll(fy, 1, 1)
                fym = jnp.where(l_first, west, fyd)
                west = fyd
                at = slice(j * LANES, (j + 1) * LANES)
                fz = (k_ + kv[z + 1, rs, at]) * (gv[z + 1, rs, at] - g_)
                total = g_ + (fx - fxm) + (fy - fym) + (fz - fzv[rs, at])
                fzv[rs, at] = fz
                ov[z, rs, at] = total
            prev = new_prev
            if t + 1 < tiles:
                gt, kt, gu, ku = gn, kn, gun, kun

    def emit_layer(z):
        at_z = lanes == z
        for t in range(tiles):
            rs = slice(t * SUBL, (t + 1) * SUBL)
            cl[rs, :] = jnp.where(at_z, pltpu.roll(ov[z, rs, :LANES], z, 1), cl[rs, :])
            cr[rs, :] = jnp.where(
                at_z, pltpu.roll(ov[z, rs, width - LANES :], z + 1, 1), cr[rs, :]
            )

    if emit:
        cl[...] = jnp.zeros_like(cl)
        cr[...] = jnp.zeros_like(cr)

    def store(c):
        at = pl.ds(c * step, step)
        return pltpu.make_async_copy(ov.at[at], out.at[at], sem.at[base + 4 + c])

    def store_rows(c):
        at = pl.ds(pl.multiple_of(c * step, SUBL), step)
        low, high = ov.at[at, 0, :], ov.at[at, cx - 1, :]
        select_copy(godd, (low, o1.at[at]), (high, o1.at[at]), sem.at[base + 10 + c])
        select_copy(godd, (high, o2.at[at]), (low, o2.at[at]), sem.at[base + 16 + c])

    for copy in load(0):
        copy.wait()
    convert(0)

    def chunk(c, _):
        @pl.when(c + 1 < chunks)
        def _():
            for copy in load(c + 1):
                copy.wait()
            convert(c + 1)

        start = pl.multiple_of(c * step, SUBL)
        for offset in range(step):
            layer(start, offset)

        @pl.when(c == 0)
        def _():
            for copy in pieces:
                copy.wait()
            ov[0, :, :] = ov[0] + HR * (bv[...] - gv[0])
            if emit:
                gtop[...] = ov[0]

        store(c).start()
        if emit:
            store_rows(c)

            def body(z, _):
                emit_layer(z)
                return 0

            lax.fori_loop(start, start + step, body, 0)
        return 0

    lax.fori_loop(0, chunks, chunk, 0)
    for c in range(chunks):
        store(c).wait()
        if emit:
            at = pl.ds(c * step, step)
            pltpu.make_async_copy(ov.at[at, 0, :], o1.at[at], sem.at[base + 10 + c]).wait()
            pltpu.make_async_copy(ov.at[at, 0, :], o2.at[at], sem.at[base + 16 + c]).wait()


def floor_sweep(emit, g, m, top_b, cond, cols1, cols3, z1, z2, x2, halos=()):
    nr, cx, width = g.shape
    outs = [shape(g.shape)]
    specs = [ANY]
    if emit:
        outs += [
            shape((cx, width)),
            shape((cx, LANES)),
            shape((cx, LANES)),
            shape((nr, width)),
            shape((nr, width)),
            shape((2, cx, LANES)),
            shape((2, nr, width)),
        ]
        specs += [VMEM] * 7
    return pl.pallas_call(
        functools.partial(floor_kernel, emit),
        out_shape=outs,
        in_specs=[ANY, ANY, ANY, SMEM, VMEM, VMEM, VMEM, VMEM, VMEM] + [VMEM] * len(halos),
        out_specs=specs,
        scratch_shapes=[
            pltpu.VMEM((nr + 1, cx, width), F32),
            pltpu.VMEM(g.shape, jnp.int32),
            pltpu.VMEM((nr + 1, cx, width), F32),
            pltpu.VMEM(g.shape, F32),
            pltpu.VMEM((cx, width), F32),
            pltpu.VMEM((2, cx, LANES), F32),
            pltpu.VMEM((2, nr, width), F32),
            pltpu.VMEM((cx, width), F32),
            pltpu.SemaphoreType.DMA((34,)),
        ],
        compiler_params=PARAMS,
        cost_estimate=cost(30 * g.size, 12 * g.size),
        name="floor_sweep",
    )(g, m, top_b, cond, cols1, cols3, z1, z2, x2, *halos)


def tin_kernel(emit, u, f, e1, e2, x1, x2, x3, top_p, speeds, *rest):
    zt, nx, ny = u.shape
    width = x2.shape[1]
    if emit:
        gtop, cl, cr, out, o1, o2, ox1, ox2, ox3 = rest[:9]
        rest = rest[9:]
    else:
        out = rest[0]
        rest = rest[1:]
    uv, fv, ov, halo, pv, sem = rest
    group, column, odd, godd = place()
    chunks = 8
    step = zt // chunks

    def load(c):
        at = pl.ds(c * step, step)
        return (
            pltpu.make_async_copy(u.at[at], uv.at[at], sem.at[2 * c]),
            pltpu.make_async_copy(f.at[at], fv.at[at], sem.at[2 * c + 1]),
        )

    base = 2 * chunks
    for copy in load(0):
        copy.start()
    select_copy(odd, (e1, halo.at[0]), (e2, halo.at[0]), sem.at[base])
    select_copy(odd, (e2, halo.at[1]), (e1, halo.at[1]), sem.at[base + 1])
    rows_at = pl.ds(pl.multiple_of(column * nx, SUBL), nx)
    lanes_at = lambda other: pl.ds(pl.multiple_of(other * width, LANES), width)
    pieces = [
        pltpu.make_async_copy(top_p.at[0, rows_at, :], pv.at[:, lanes_at(column)], sem.at[base + 2])
    ]
    for k, ref in ((1, x1), (2, x2), (3, x3)):
        pieces.append(
            pltpu.make_async_copy(
                ref.at[nx : 2 * nx, :], pv.at[:, lanes_at(column ^ k)], sem.at[base + 2 + k]
            )
        )
    for copy in pieces:
        copy.start()
    for c in range(1, chunks):
        for copy in load(c):
            copy.start()
    rows, lanes = iotas()
    r_first, r_last = rows == 0, rows == SUBL - 1
    l_first, l_last = lanes == 0, lanes == LANES - 1
    tiles, wide = nx // SUBL, ny // LANES
    zero = jnp.zeros((SUBL, LANES), F32)

    def layer(start, offset):
        z = start + offset
        sx, sy = speeds[0, z], speeds[1, z]
        centre = 1.0 - 6.0 * KT - sx - sy - jnp.where(z == 0, HT, 0.0)
        above, below = jnp.minimum(z + 1, zt - 1), jnp.maximum(z - 1, 0)

        def get(ref, z_, t, j):
            return ref[z_, t * SUBL : (t + 1) * SUBL, j * LANES : (j + 1) * LANES]

        def row_of(s, at):
            block = halo[s, pl.ds(start, SUBL), at]
            return jnp.broadcast_to(block[offset : offset + 1], (SUBL, LANES))

        left = [zero] * tiles
        now = [get(uv, z, t, 0) for t in range(tiles)]
        turned = [pltpu.roll(v, LANES - 1, 1) for v in now]
        for j in range(wide):
            at = slice(j * LANES, (j + 1) * LANES)
            if j + 1 < wide:
                nxt = [get(uv, z, t, j + 1) for t in range(tiles)]
                nxt_turned = [pltpu.roll(v, LANES - 1, 1) for v in nxt]
            else:
                nxt, nxt_turned = None, [zero] * tiles
            low, high = row_of(0, at), row_of(1, at)
            downs = [low] + [pltpu.roll(v, 1, 0) for v in now]
            ups = [pltpu.roll(v, SUBL - 1, 0) for v in now] + [high]
            for t in range(tiles):
                v = now[t]
                xm = jnp.where(r_first, downs[t], downs[t + 1])
                xp = jnp.where(r_last, ups[t + 1], ups[t])
                turn = pltpu.roll(v, 1, 1)
                ym = jnp.where(l_first, left[t], turn)
                yp = jnp.where(l_last, nxt_turned[t], turned[t])
                left[t] = turn
                code = get(fv, z, t, j)
                xs = jnp.where((code & 1) == 0, xm, xp)
                ys = jnp.where(code < 2, ym, yp)
                spread = (xm + xp) + (ym + yp) + (get(uv, above, t, j) + get(uv, below, t, j))
                ov[z, t * SUBL : (t + 1) * SUBL, at] = (
                    (centre * v + KT * spread) + (sx * xs + sy * ys)
                )
            now, turned = nxt, nxt_turned

    def store(c):
        at = pl.ds(c * step, step)
        return pltpu.make_async_copy(ov.at[at], out.at[at], sem.at[base + 6 + c])

    def store_rows(c):
        at = pl.ds(pl.multiple_of(c * step, SUBL), step)
        low, high = ov.at[at, 0, :], ov.at[at, nx - 1, :]
        select_copy(odd, (low, o1.at[at]), (high, o1.at[at]), sem.at[base + 14 + c])
        select_copy(odd, (high, o2.at[at]), (low, o2.at[at]), sem.at[base + 22 + c])

    for copy in load(0):
        copy.wait()
    pltpu.make_async_copy(e2, halo.at[0], sem.at[base]).wait()
    pltpu.make_async_copy(e2, halo.at[1], sem.at[base + 1]).wait()

    def chunk(c, _):
        @pl.when(c + 1 < chunks)
        def _():
            for copy in load(c + 1):
                copy.wait()

        start = pl.multiple_of(c * step, SUBL)
        for offset in range(step):
            layer(start, offset)

        @pl.when(c == 0)
        def _():
            for copy in pieces:
                copy.wait()
            ov[0, :, :] = ov[0] + HT * pv[...]

        store(c).start()
        if emit:
            store_rows(c)
        return 0

    lax.fori_loop(0, chunks, chunk, 0)
    if emit:
        put_columns(ox1, jnp.where(odd, cl[...], cr[...]))
        inner = (column > 0) & (column < TILE_Y - 1)
        put_columns(ox3, jnp.where(inner, jnp.where(odd, cr[...], cl[...]), 0.0))
        plane = ov.at[0]
        put_planes(ox1, plane, gtop, column ^ 1)
        put_planes(ox2, plane, gtop, column ^ 2)
        put_planes(ox3, plane, gtop, column ^ 3)
    for c in range(chunks):
        store(c).wait()
        if emit:
            at = pl.ds(c * step, step)
            pltpu.make_async_copy(ov.at[at, 0, :], o1.at[at], sem.at[base + 14 + c]).wait()
            pltpu.make_async_copy(ov.at[at, 0, :], o2.at[at], sem.at[base + 22 + c]).wait()


def tin_sweep(emit, u, f, e1, e2, x1, x2, x3, top_p, speeds, own=()):
    zt, nx, ny = u.shape
    width = x2.shape[1]
    outs, specs = [shape(u.shape)], [ANY]
    if emit:
        outs += [shape(v.shape) for v in (e1, e2, x1, x2, x3)]
        specs += [VMEM] * 5
    return pl.pallas_call(
        functools.partial(tin_kernel, emit),
        out_shape=outs,
        in_specs=[ANY] * 8 + [SMEM] + [VMEM] * len(own),
        out_specs=specs,
        scratch_shapes=[
            pltpu.VMEM(u.shape, F32),
            pltpu.VMEM(u.shape, jnp.int32),
            pltpu.VMEM(u.shape, F32),
            pltpu.VMEM((2, zt, ny), F32),
            pltpu.VMEM((nx, ny), F32),
            pltpu.SemaphoreType.DMA((46,)),
        ],
        compiler_params=PARAMS,
        cost_estimate=cost(30 * u.size, 12 * u.size),
        name="tin_sweep",
    )(u, f, e1, e2, x1, x2, x3, top_p, speeds, *own)


def local(tin_temp, flow_code, speeds, floor_temp, material, conductivity):
    u, f, g, m = tin_temp, flow_code, floor_temp[0], material[0]
    zt, nx, ny = u.shape
    nr, cx, width = g.shape
    e1, e2, x2, z1, z2 = pl.pallas_call(
        pack_rows_kernel,
        out_shape=[
            shape((zt, ny)),
            shape((zt, ny)),
            shape((2 * nx, width)),
            shape((2 * nr, width)),
            shape((2 * nr, width)),
        ],
        in_specs=[ANY, ANY, ANY, SMEM],
        out_specs=[VMEM] * 5,
        scratch_shapes=[pltpu.VMEM((2, nr, width), jnp.int32), pltpu.SemaphoreType.DMA((8,))],
        compiler_params=PARAMS,
        cost_estimate=cost(0, 1 << 20),
        name="pack_rows",
    )(u, g, m, conductivity)
    e2 = swap(e2, "e2")
    z1, z2 = swap(z1, "z1"), swap(z2, "z2")
    x1, x3 = pl.pallas_call(
        pack_cols_kernel,
        out_shape=[shape((cx, 2 * LANES)), shape((cx, 2 * LANES))],
        in_specs=[ANY, ANY, ANY, SMEM],
        out_specs=[VMEM] * 2,
        scratch_shapes=[
            pltpu.VMEM(g.shape, F32),
            pltpu.VMEM(g.shape, jnp.int32),
            pltpu.VMEM((nx, ny), F32),
            pltpu.VMEM((cx, width), F32),
            pltpu.VMEM((2, cx, LANES), F32),
            pltpu.SemaphoreType.DMA((10,)),
        ],
        compiler_params=PARAMS,
        cost_estimate=cost(0, 8 * g.size),
        name="pack_cols",
    )(u, g, m, conductivity)
    e1 = swap(e1, "e1")
    x1, x2, x3 = swap(x1, "e1"), swap(x2, "x2"), swap(x3, "x3")
    g1, gtop, cl, cr, z1, z2, kc, kr = floor_sweep(
        True, g, m, u, conductivity, x1, x3, z1, z2, x2
    )
    z1, z2 = swap(z1, "z1"), swap(z2, "z2")
    u1, e1, e2, y1, y2, y3 = tin_sweep(
        True, u, f, e1, e2, x1, x2, x3, g, speeds, (gtop, cl, cr)
    )
    e2 = swap(e2, "e2")
    y1, y2, y3 = swap(y1, "e1"), swap(y2, "x2"), swap(y3, "x3")
    e1 = swap(e1, "e1")
    (g2,) = floor_sweep(False, g1, m, u1, conductivity, y1, y3, z1, z2, y2, (kc, kr))
    (u2,) = tin_sweep(False, u1, f, e1, e2, y1, y2, y3, g1, speeds)
    return u2, g2[None]


def solution(mesh):
    placed = (
        P(None, ("grp", "len"), None),
        P(None, ("grp", "len"), None),
        P(),
        P(("grp", "len"), None, None, None),
        P(("grp", "len"), None, None, None),
        P(),
    )
    return jax.shard_map(
        local,
        mesh=mesh,
        in_specs=placed,
        out_specs=(P(None, ("grp", "len"), None), P(("grp", "len"), None, None, None)),
        check_vma=False,
    )
```

```python
import functools

import jax
import jax.numpy as jnp
from jax import lax
from jax.experimental import pallas as pl
from jax.experimental.pallas import tpu as pltpu
from jax.sharding import PartitionSpec as P

TILE_Y = 4
KT = 0.1
HT = 0.2
HR = 0.2
LANES = 128
SUBL = 8
F32 = jnp.float32
ANY = pl.BlockSpec(memory_space=pl.ANY)
VMEM = pl.BlockSpec(memory_space=pltpu.VMEM)
SMEM = pl.BlockSpec(memory_space=pltpu.SMEM)


def params(mib):
    return pltpu.CompilerParams(vmem_limit_bytes=mib * 1024 * 1024)


def shape(dims, dtype=F32):
    return pltpu.VMEM(dims, dtype)


def far(dims, dtype=F32):
    return pltpu.HBM(dims, dtype)


def in_hbm(*arrays):
    return [pltpu.with_memory_space_constraint(a, pltpu.HBM) for a in arrays]


def in_vmem(*arrays):
    return [pltpu.with_memory_space_constraint(a, pltpu.VMEM) for a in arrays]


def cost(flops, nbytes):
    return pl.CostEstimate(flops=flops, bytes_accessed=nbytes, transcendentals=0)


def place():
    pos = lax.axis_index("len")
    group, column = pos // TILE_Y, pos % TILE_Y
    return group, column, pos % 2 == 1, group % 2 == 1


def iotas():
    rows = lax.broadcasted_iota(jnp.int32, (SUBL, LANES), 0)
    lanes = lax.broadcasted_iota(jnp.int32, (SUBL, LANES), 1)
    return rows, lanes


def swaps(kind):
    count = lax.axis_size("len")
    partner = {
        "e1": lambda i: i ^ 1,
        "e2": lambda i: i + 1 if i % 2 else i - 1,
        "x2": lambda i: i ^ 2,
        "x3": lambda i: i ^ 3,
        "z1": lambda i: i ^ TILE_Y,
        "z2": lambda i: i + TILE_Y if (i // TILE_Y) % 2 else i - TILE_Y,
    }[kind]
    return [(i, partner(i)) for i in range(count) if 0 <= partner(i) < count]


def swap(value, kind):
    return lax.ppermute(value, "len", swaps(kind))


def select_copy(cond, first, second, sem):
    @pl.when(cond)
    def _():
        pltpu.make_async_copy(*first, sem).start()

    @pl.when(jnp.logical_not(cond))
    def _():
        pltpu.make_async_copy(*second, sem).start()


def half_lookup(ids, cond):
    value = jnp.full(ids.shape, 0.5 * cond[0], F32)
    for i in range(1, cond.shape[0]):
        value = jnp.where(ids == i, 0.5 * cond[i], value)
    return value


def wait_bytes(src, dst, sem):
    pltpu.make_async_copy(src, dst, sem).wait()


def pack_rows_kernel(u, floor, ids, cond, e2, x2, z1, z2, mrow, sem):
    g, m = floor.at[0], ids.at[0]
    group, column, odd, godd = place()
    nx, cx = u.shape[1], g.shape[1]
    nr, width = g.shape[0], g.shape[2]
    select_copy(odd, (u.at[:, nx - 1, :], e2), (u.at[:, 0, :], e2), sem.at[0])
    low, high = g.at[:, 0, :], g.at[:, cx - 1, :]
    select_copy(godd, (low, z1.at[:nr]), (high, z1.at[:nr]), sem.at[1])
    select_copy(godd, (high, z2.at[:nr]), (low, z2.at[:nr]), sem.at[2])
    rows = [(m.at[:, r, :], mrow.at[s]) for r, s in ((0, 0), (cx - 1, 1))]
    for i, (src, dst) in enumerate(rows):
        pltpu.make_async_copy(src, dst, sem.at[3 + i]).start()
    other = column ^ 2
    lane = pl.multiple_of(other * width, LANES)
    row = pl.multiple_of(other * nx, SUBL)
    planes = (
        pltpu.make_async_copy(u.at[0, :, pl.ds(lane, width)], x2.at[:nx], sem.at[5]),
        pltpu.make_async_copy(g.at[0, pl.ds(row, nx), :], x2.at[nx:], sem.at[6]),
    )
    for copy in planes:
        copy.start()
    for i, (src, dst) in enumerate(rows):
        wait_bytes(src, dst, sem.at[3 + i])
    k_low, k_high = half_lookup(mrow[0], cond), half_lookup(mrow[1], cond)
    z1[nr:, :] = jnp.where(godd, k_low, k_high)
    z2[nr:, :] = jnp.where(godd, k_high, k_low)
    wait_bytes(u.at[:, 0, :], e2, sem.at[0])
    wait_bytes(low, z1.at[:nr], sem.at[1])
    wait_bytes(low, z2.at[:nr], sem.at[2])
    for copy in planes:
        copy.wait()


def put_columns(aux, cols):
    half = cols.shape[0] // 2
    aux[half:, :LANES] = cols[:half]
    aux[half:, LANES:] = cols[half:]


def get_columns(aux):
    half = aux.shape[0] // 2
    return jnp.concatenate([aux[half:, :LANES], aux[half:, LANES:]], 0)


def put_planes(dst, b_plane, p_plane, other):
    nx, width = b_plane.shape[0], p_plane.shape[1]
    lane = pl.multiple_of(other * width, LANES)
    row = pl.multiple_of(other * nx, SUBL)
    dst[:nx, :] = b_plane[:, pl.ds(lane, width)]
    dst[nx : 2 * nx, :] = p_plane[pl.ds(row, nx), :]


def keep_columns(own, z, at_z, at_y, rs, left, right, shift):
    lanes = lax.broadcasted_iota(jnp.int32, (SUBL, LANES), 1)
    both = pltpu.roll(jnp.where(lanes == 0, left, right), z + shift, 1)
    own[0, rs, :] = jnp.where(at_z, both, own[0, rs, :])
    own[1, rs, :] = jnp.where(at_y, both, own[1, rs, :])


def prepare_kernel(
    u, floor, ids, cond, _, e1, x3, own, gv, ce, cw, cn, cz, mv, kv, b_plane, sem
):
    g, m = floor.at[0], ids.at[0]
    group, column, odd, godd = place()
    zt, nx, ny = u.shape
    nr, cx, width = g.shape
    chunks = 6
    step = nr // chunks

    def load(c):
        at = pl.ds(c * step, step)
        return (
            pltpu.make_async_copy(m.at[at], mv.at[at], sem.at[2 * c]),
            pltpu.make_async_copy(g.at[at], gv.at[at], sem.at[2 * c + 1]),
        )

    base = 2 * chunks
    plane = pltpu.make_async_copy(u.at[0], b_plane, sem.at[base])
    for copy in load(0):
        copy.start()
    rows_out = e1.at[:, :ny]
    select_copy(odd, (u.at[:, 0, :], rows_out), (u.at[:, nx - 1, :], rows_out), sem.at[base + 1])
    plane.start()
    for c in range(1, chunks):
        for copy in load(c):
            copy.start()
    rows, lanes = iotas()
    r_last, l_first, l_last = rows == SUBL - 1, lanes == 0, lanes == LANES - 1
    tiles, wide = cx // SUBL, width // LANES
    shift = LANES // 2
    scal = [0.5 * cond[i] for i in range(cond.shape[0])]
    own[...] = jnp.zeros_like(own)

    def lookup(ids):
        value = jnp.full(ids.shape, scal[0], F32)
        for i in range(1, len(scal)):
            value = jnp.where(ids == i, scal[i], value)
        return value

    def layer(z):
        at_z, at_y = lanes == z, lanes == lax.rem(z + LANES - 1, LANES)
        at_kz, at_ky = lanes == z + shift, lanes == z + shift - 1
        before = jnp.maximum(z - 1, 0)
        spans = [slice(j * LANES, (j + 1) * LANES) for j in range(wide)]

        def tile(t):
            rs = slice(t * SUBL, (t + 1) * SUBL)
            ks = [lookup(mv[z, rs, at]) for at in spans]
            return ks, [pltpu.roll(k, SUBL - 1, 0) for k in ks]

        ks, ups = tile(0)
        for t in range(tiles):
            rs = slice(t * SUBL, (t + 1) * SUBL)
            if t + 1 < tiles:
                kn, un = tile(t + 1)
            east = [pltpu.roll(k, LANES - 1, 1) for k in ks]
            west = [pltpu.roll(k, 1, 1) for k in ks]
            for j, at in enumerate(spans):
                k = ks[j]
                kv[z, rs, at] = k
                cz[before, rs, at] = kv[before, rs, at] + k
                if t + 1 < tiles:
                    cn[z, rs, at] = k + jnp.where(r_last, un[j], ups[j])
                else:
                    cn[z, rs, at] = jnp.where(r_last, 0.0, k + ups[j])
                if j + 1 < wide:
                    ce[z, rs, at] = k + jnp.where(l_last, east[j + 1], east[j])
                else:
                    ce[z, rs, at] = jnp.where(l_last, 0.0, k + east[j])
                if j > 0:
                    cw[z, rs, at] = k + jnp.where(l_first, west[j - 1], west[j])
                else:
                    cw[z, rs, at] = jnp.where(l_first, 0.0, k + west[j])
            keep_columns(own, z, at_z, at_y, rs, gv[z, rs, spans[0]], gv[z, rs, spans[-1]], 0)
            keep_columns(own, z, at_kz, at_ky, rs, ks[0], ks[-1], shift)
            if t + 1 < tiles:
                ks, ups = kn, un

    def chunk(c, _):
        for copy in load(c):
            copy.wait()
        start = c * step

        def body(i, _):
            layer(start + 2 * i)
            layer(start + 2 * i + 1)
            return 0

        return lax.fori_loop(0, step // 2, body, 0)

    lax.fori_loop(0, chunks, chunk, 0)
    cz[nr - 1, :, :] = kv[nr - 1]
    own[1, :, :] = pltpu.roll(own[1], 1, 1)
    left, right = own[0], own[1]
    aux = e1.at[:, ny:]
    put_columns(aux, jnp.where(odd, left, right))
    inner = (column > 0) & (column < TILE_Y - 1)
    put_columns(x3, jnp.where(inner, jnp.where(odd, right, left), 0.0))
    plane.wait()
    put_planes(aux, b_plane, gv.at[0], column ^ 1)
    put_planes(x3, b_plane, gv.at[0], column ^ 3)
    wait_bytes(u.at[:, 0, :], rows_out, sem.at[base + 1])


def floor_kernel(
    emit, g, ce, cw, cn, cz, u, x1, x2, x3, z1, z2, y1, y2, own, *rest
):
    nr, cx, width = g.shape
    nx, ny = u.shape[1], u.shape[2]
    if emit:
        out, own_new, o1, o2, kc, kr = rest[:6]
        ov, rest = out, rest[6:]
    else:
        kc, kr, out, ov = rest[:4]
        rest = rest[4:]
    fzv, tcol, trow, bv, sem = rest
    group, column, odd, godd = place()
    tiles, wide = cx // SUBL, width // LANES
    step = SUBL
    chunks = nr // step
    shift = LANES // 2
    aux = x1.at[:, ny:]
    one, three = get_columns(aux), get_columns(x3)
    for s, halo in ((0, jnp.where(odd, one, three)), (1, jnp.where(odd, three, one))):
        if emit:
            kc[s, :, :] = pltpu.roll(own[s] + halo, shift, 1)
        tcol[s, :, :] = kc[s] * (halo - own[s])
    for s, (mine, halo) in enumerate(((z1, y1), (z2, y2))):
        if emit:
            kr[s, :, :] = mine[nr:, :] + halo[nr:, :]
        side = kr[s] * (halo[:nr, :] - mine[:nr, :])
        trow[jnp.where(godd, s, 1 - s), :, :] = side
    row = lambda other: pl.ds(pl.multiple_of(other * nx, SUBL), nx)
    bv[row(column), :] = u[0, :, pl.ds(pl.multiple_of(column * width, LANES), width)]
    for k, ref in ((1, aux), (2, x2), (3, x3)):
        bv[row(column ^ k), :] = ref[:nx, :]
    rows, lanes = iotas()
    r_first, r_last = rows == 0, rows == SUBL - 1
    l_first, l_last = lanes == 0, lanes == LANES - 1
    fzv[...] = jnp.zeros_like(fzv)
    if emit:
        own_new[...] = jnp.zeros_like(own_new)
    spans = [slice(j * LANES, (j + 1) * LANES) for j in range(wide)]

    def layer(start, offset):
        z = start + offset
        back = lax.rem(LANES - z, LANES)
        if emit:
            at_z, at_y = lanes == z, lanes == lax.rem(z + LANES - 1, LANES)
        above = z + 1
        if offset == step - 1:
            above = jnp.minimum(above, nr - 1)
            scale = jnp.where(z + 1 < nr, 1.0, 0.0)

        def tile(t):
            rs = slice(t * SUBL, (t + 1) * SUBL)
            gs = [g[z, rs, at] for at in spans]
            return gs, [pltpu.roll(v, SUBL - 1, 0) for v in gs]

        def row_of(s):
            block = trow[s, pl.ds(start, SUBL), :][offset : offset + 1]
            return [jnp.broadcast_to(block[:, at], (SUBL, LANES)) for at in spans]

        low, high = row_of(0), row_of(1)
        gs, ups = tile(0)
        prev = [-v for v in low]
        for t in range(tiles):
            rs = slice(t * SUBL, (t + 1) * SUBL)
            if t + 1 < tiles:
                gn, un = tile(t + 1)
            east = [pltpu.roll(v, LANES - 1, 1) for v in gs]
            west = [pltpu.roll(v, 1, 1) for v in gs]
            t_west = pltpu.roll(tcol[0, rs, :], back, 1)
            t_east = pltpu.roll(tcol[1, rs, :], LANES - 1 - z, 1)
            for j, at in enumerate(spans):
                v = gs[j]
                if t + 1 < tiles:
                    fx = cn[z, rs, at] * (jnp.where(r_last, un[j], ups[j]) - v)
                else:
                    fx = jnp.where(r_last, high[j], cn[z, rs, at] * (ups[j] - v))
                turned = pltpu.roll(fx, 1, 0)
                fxm = jnp.where(r_first, prev[j], turned)
                prev[j] = turned
                yp = jnp.where(l_last, east[j + 1], east[j]) if j + 1 < wide else east[j]
                ym = jnp.where(l_first, west[j - 1], west[j]) if j > 0 else west[j]
                side = ce[z, rs, at] * (yp - v) + cw[z, rs, at] * (ym - v)
                if j == 0:
                    side = side + jnp.where(l_first, t_west, 0.0)
                if j + 1 == wide:
                    side = side + jnp.where(l_last, t_east, 0.0)
                nxt = g[above, rs, at]
                if offset == step - 1:
                    nxt = scale * nxt
                fz = cz[z, rs, at] * (nxt - v)
                total = v + ((fx - fxm) + side + (fz - fzv[rs, at]))
                fzv[rs, at] = fz
                ov[z, rs, at] = total
            if t + 1 < tiles:
                gs, ups = gn, un

    def columns(z):
        at_z, at_y = lanes == z, lanes == lax.rem(z + LANES - 1, LANES)
        for t in range(tiles):
            rs = slice(t * SUBL, (t + 1) * SUBL)
            keep_columns(own_new, z, at_z, at_y, rs, ov[z, rs, spans[0]], ov[z, rs, spans[-1]], 0)

    def store(c):
        at = pl.ds(c * step, step)
        return pltpu.make_async_copy(ov.at[at], out.at[at], sem.at[c])

    def store_rows(c):
        at = pl.ds(pl.multiple_of(c * step, SUBL), step)
        low, high = ov.at[at, 0, :], ov.at[at, cx - 1, :]
        select_copy(godd, (low, o1.at[at]), (high, o1.at[at]), sem.at[chunks + c])
        select_copy(godd, (high, o2.at[at]), (low, o2.at[at]), sem.at[2 * chunks + c])

    def chunk(c, _):
        start = pl.multiple_of(c * step, SUBL)
        for offset in range(step):
            layer(start, offset)

        @pl.when(c == 0)
        def _():
            ov[0, :, :] = ov[0] + HR * (bv[...] - g[0])

        if emit:
            store_rows(c)
            for offset in range(step):
                columns(start + offset)
        else:
            store(c).start()
        return 0

    lax.fori_loop(0, chunks, chunk, 0)
    if emit:
        own_new[1, :, :] = pltpu.roll(own_new[1], 1, 1)
    for c in range(chunks):
        if emit:
            at = pl.ds(c * step, step)
            wait_bytes(ov.at[at, 0, :], o1.at[at], sem.at[chunks + c])
            wait_bytes(ov.at[at, 0, :], o2.at[at], sem.at[2 * chunks + c])
        else:
            store(c).wait()


def floor_sweep(emit, g, coefs, u, x1, x2, x3, z1, z2, y1, y2, own, halos=()):
    nr, cx, width = g.shape
    scratch = [
        pltpu.VMEM((cx, width), F32),
        pltpu.VMEM((2, cx, LANES), F32),
        pltpu.VMEM((2, nr, width), F32),
        pltpu.VMEM((cx, width), F32),
        pltpu.SemaphoreType.DMA((3 * nr // SUBL,)),
    ]
    if emit:
        outs = [
            shape(g.shape),
            shape(own.shape),
            shape((nr, width)),
            shape((nr, width)),
            shape(own.shape),
            shape((2, nr, width)),
        ]
        specs = [VMEM] * 6
    else:
        outs, specs = [far(g.shape)], [ANY]
        scratch = [pltpu.VMEM(g.shape, F32)] + scratch
    return pl.pallas_call(
        functools.partial(floor_kernel, emit),
        out_shape=outs,
        in_specs=[VMEM] * (14 + len(halos)),
        out_specs=specs,
        scratch_shapes=scratch,
        compiler_params=params(2 if emit else 6),
        cost_estimate=cost(30 * g.size, 12 * g.size),
        name="floor_sweep",
    )(*in_vmem(g, *coefs, u, x1, x2, x3, z1, z2, y1, y2, own, *halos))


def tin_kernel(emit, u, f, e1, e2, x2, x3, g, speeds, *rest):
    zt, nx, ny = u.shape
    width = x2.shape[1]
    if emit:
        g_new, own, out, o1, o2, ox2, ox3 = rest[:7]
        ov, rest = out, rest[7:]
    else:
        out, ov = rest[:2]
        rest = rest[2:]
    pv, sem = rest
    group, column, odd, godd = place()
    step = SUBL
    chunks = zt // step
    lanes_at = lambda other: pl.ds(pl.multiple_of(other * width, LANES), width)
    pv[:, lanes_at(column)] = g[0, pl.ds(pl.multiple_of(column * nx, SUBL), nx), :]
    for k, ref in ((1, e1.at[:, ny:]), (2, x2), (3, x3)):
        pv[:, lanes_at(column ^ k)] = ref[nx : 2 * nx, :]
    rows, lanes = iotas()
    r_first, r_last = rows == 0, rows == SUBL - 1
    l_first, l_last = lanes == 0, lanes == LANES - 1
    tiles, wide = nx // SUBL, ny // LANES
    zero = jnp.zeros((SUBL, LANES), F32)

    def layer(start, offset):
        z = start + offset
        sx, sy = speeds[0, z], speeds[1, z]
        centre = 1.0 - 6.0 * KT - sx - sy - jnp.where(z == 0, HT, 0.0)
        above, below = jnp.minimum(z + 1, zt - 1), jnp.maximum(z - 1, 0)

        def get(ref, z_, t, j):
            return ref[z_, t * SUBL : (t + 1) * SUBL, j * LANES : (j + 1) * LANES]

        left = [zero] * tiles
        now = [get(u, z, t, 0) for t in range(tiles)]
        turned = [pltpu.roll(v, LANES - 1, 1) for v in now]
        for j in range(wide):
            at = slice(j * LANES, (j + 1) * LANES)
            if j + 1 < wide:
                nxt = [get(u, z, t, j + 1) for t in range(tiles)]
                nxt_turned = [pltpu.roll(v, LANES - 1, 1) for v in nxt]
            else:
                nxt, nxt_turned = None, [zero] * tiles
            one = e1[pl.ds(start, SUBL), at][offset : offset + 1]
            two = e2[pl.ds(start, SUBL), at][offset : offset + 1]
            low = jnp.broadcast_to(jnp.where(odd, one, two), (SUBL, LANES))
            high = jnp.broadcast_to(jnp.where(odd, two, one), (SUBL, LANES))
            downs = [low] + [pltpu.roll(v, 1, 0) for v in now]
            ups = [pltpu.roll(v, SUBL - 1, 0) for v in now] + [high]
            for t in range(tiles):
                v = now[t]
                xm = jnp.where(r_first, downs[t], downs[t + 1])
                xp = jnp.where(r_last, ups[t + 1], ups[t])
                turn = pltpu.roll(v, 1, 1)
                ym = jnp.where(l_first, left[t], turn)
                yp = jnp.where(l_last, nxt_turned[t], turned[t])
                left[t] = turn
                code = get(f, z, t, j)
                xs = jnp.where((code & 1) == 0, xm, xp)
                ys = jnp.where(code < 2, ym, yp)
                spread = (xm + xp) + (ym + yp) + (get(u, above, t, j) + get(u, below, t, j))
                ov[z, t * SUBL : (t + 1) * SUBL, at] = (
                    (centre * v + KT * spread) + (sx * xs + sy * ys)
                )
            now, turned = nxt, nxt_turned

    def store(c):
        at = pl.ds(c * step, step)
        return pltpu.make_async_copy(ov.at[at], out.at[at], sem.at[c])

    def store_rows(c):
        at = pl.ds(pl.multiple_of(c * step, SUBL), step)
        low, high = ov.at[at, 0, :], ov.at[at, nx - 1, :]
        to1, to2 = o1.at[at, :ny], o2.at[at]
        select_copy(odd, (low, to1), (high, to1), sem.at[c])
        select_copy(odd, (high, to2), (low, to2), sem.at[chunks + c])

    def chunk(c, _):
        start = pl.multiple_of(c * step, SUBL)
        for offset in range(step):
            layer(start, offset)

        @pl.when(c == 0)
        def _():
            ov[0, :, :] = ov[0] + HT * pv[...]

        if emit:
            store_rows(c)
        else:
            store(c).start()
        return 0

    lax.fori_loop(0, chunks, chunk, 0)
    if emit:
        aux = o1.at[:, ny:]
        put_columns(aux, jnp.where(odd, own[0], own[1]))
        inner = (column > 0) & (column < TILE_Y - 1)
        put_columns(ox3, jnp.where(inner, jnp.where(odd, own[1], own[0]), 0.0))
        for k, ref in ((1, aux), (2, ox2), (3, ox3)):
            put_planes(ref, ov.at[0], g_new.at[0], column ^ k)
    for c in range(chunks):
        if emit:
            at = pl.ds(c * step, step)
            wait_bytes(ov.at[at, 0, :], o1.at[at, :ny], sem.at[c])
            wait_bytes(ov.at[at, 0, :], o2.at[at], sem.at[chunks + c])
        else:
            store(c).wait()


def tin_sweep(emit, u, f, e1, e2, x2, x3, g, speeds, own=()):
    zt, nx, ny = u.shape
    scratch = [pltpu.VMEM((nx, ny), F32), pltpu.SemaphoreType.DMA((2 * zt // SUBL,))]
    if emit:
        outs = [shape(v.shape) for v in (u, e1, e2, x2, x3)]
        specs = [VMEM] * 5
    else:
        outs, specs = [far(u.shape)], [ANY]
        scratch = [pltpu.VMEM(u.shape, F32)] + scratch
    return pl.pallas_call(
        functools.partial(tin_kernel, emit),
        out_shape=outs,
        in_specs=[VMEM] * 7 + [SMEM] + [VMEM] * len(own),
        out_specs=specs,
        scratch_shapes=scratch,
        compiler_params=params(2 if emit else 6),
        cost_estimate=cost(30 * u.size, 12 * u.size),
        name="tin_sweep",
    )(*in_vmem(u, f, e1, e2, x2, x3, g), speeds, *in_vmem(*own))


def local(tin_temp, flow_code, speeds, floor_temp, material, conductivity):
    u, f, g, m = tin_temp, flow_code, floor_temp[0], material[0]
    zt, nx, ny = u.shape
    nr, cx, width = g.shape
    e2, x2, z1, z2 = pl.pallas_call(
        pack_rows_kernel,
        out_shape=[
            shape((zt, ny)),
            shape((2 * nx, width)),
            shape((2 * nr, width)),
            shape((2 * nr, width)),
        ],
        in_specs=[ANY, ANY, ANY, SMEM],
        out_specs=[VMEM] * 4,
        scratch_shapes=[pltpu.VMEM((2, nr, width), jnp.int32), pltpu.SemaphoreType.DMA((7,))],
        compiler_params=params(2),
        cost_estimate=cost(0, 1 << 20),
        name="pack_rows",
    )(*in_hbm(u, floor_temp, material), conductivity)
    e2, x2 = swap(e2, "e2"), swap(x2, "x2")
    y1, y2 = swap(z1, "z1"), swap(z2, "z2")
    e1, x3, own, gv, *coefs = pl.pallas_call(
        prepare_kernel,
        out_shape=[
            shape((zt, ny + 2 * LANES)),
            shape((cx, 2 * LANES)),
            shape((2, cx, LANES)),
        ]
        + [shape(g.shape)] * 5,
        in_specs=[ANY, ANY, ANY, SMEM, ANY],
        out_specs=[VMEM] * 8,
        scratch_shapes=[
            pltpu.VMEM(g.shape, jnp.int32),
            pltpu.VMEM(g.shape, F32),
            pltpu.VMEM((nx, ny), F32),
            pltpu.SemaphoreType.DMA((14,)),
        ],
        compiler_params=params(10),
        cost_estimate=cost(0, 8 * g.size),
        name="prepare",
    )(*in_hbm(u, floor_temp, material), conductivity, z1)
    e1, x3 = swap(e1, "e1"), swap(x3, "x3")
    g1, own1, z1, z2, kc, kr = floor_sweep(
        True, gv, coefs, u, e1, x2, x3, z1, z2, y1, y2, own
    )
    y1, y2 = swap(z1, "z1"), swap(z2, "z2")
    u1, e1, e2, x2, x3 = tin_sweep(
        True, u, f, e1, e2, x2, x3, gv, speeds, (g1, own1)
    )
    e2 = swap(e2, "e2")
    e1, x2, x3 = swap(e1, "e1"), swap(x2, "x2"), swap(x3, "x3")
    (g2,) = floor_sweep(
        False, g1, coefs, u1, e1, x2, x3, z1, z2, y1, y2, own1, (kc, kr)
    )
    (u2,) = tin_sweep(False, u1, f, e1, e2, x2, x3, g1, speeds)
    return u2, g2[None]


def solution(mesh):
    placed = (
        P(None, ("grp", "len"), None),
        P(None, ("grp", "len"), None),
        P(),
        P(("grp", "len"), None, None, None),
        P(("grp", "len"), None, None, None),
        P(),
    )
    return jax.shard_map(
        local,
        mesh=mesh,
        in_specs=placed,
        out_specs=(P(None, ("grp", "len"), None), P(("grp", "len"), None, None, None)),
        check_vma=False,
    )
```

```python
import functools

import jax
import jax.numpy as jnp
from jax import lax
from jax.experimental import pallas as pl
from jax.experimental.pallas import tpu as pltpu
from jax.sharding import PartitionSpec as P

TILE_Y = 4
KT = 0.1
HT = 0.2
HR = 0.2
LANES = 128
SUBL = 8
F32 = jnp.float32
ANY = pl.BlockSpec(memory_space=pl.ANY)
VMEM = pl.BlockSpec(memory_space=pltpu.VMEM)
SMEM = pl.BlockSpec(memory_space=pltpu.SMEM)


def params(mib):
    return pltpu.CompilerParams(vmem_limit_bytes=mib * 1024 * 1024)


def shape(dims, dtype=F32):
    return pltpu.VMEM(dims, dtype)


def far(dims, dtype=F32):
    return pltpu.HBM(dims, dtype)


def in_hbm(*arrays):
    return [pltpu.with_memory_space_constraint(a, pltpu.HBM) for a in arrays]


def in_vmem(*arrays):
    return [pltpu.with_memory_space_constraint(a, pltpu.VMEM) for a in arrays]


def cost(flops, nbytes):
    return pl.CostEstimate(flops=flops, bytes_accessed=nbytes, transcendentals=0)


def place():
    pos = lax.axis_index("len")
    group, column = pos // TILE_Y, pos % TILE_Y
    return group, column, pos % 2 == 1, group % 2 == 1


def iotas():
    rows = lax.broadcasted_iota(jnp.int32, (SUBL, LANES), 0)
    lanes = lax.broadcasted_iota(jnp.int32, (SUBL, LANES), 1)
    return rows, lanes


def partner(kind, pos):
    return {
        "e1": lambda: pos ^ 1,
        "e2": lambda: pos + 1 if pos % 2 else pos - 1,
        "x2": lambda: pos ^ 2,
        "z1": lambda: pos ^ TILE_Y,
        "z2": lambda: pos + TILE_Y if (pos // TILE_Y) % 2 else pos - TILE_Y,
    }[kind]()


def swap(value, kind):
    count, parts = lax.axis_size("len"), lax.axis_size("grp")
    pairs = []
    for part in range(parts):
        for pos in range(count):
            to, other = part, partner(kind, pos)
            if not 0 <= other < count:
                to, other = (part ^ 1, pos) if kind == "e2" else (part, pos ^ 1)
            if 0 <= to < parts:
                pairs.append((part * count + pos, to * count + other))
    return lax.ppermute(value, ("grp", "len"), pairs)


def select_copy(cond, first, second, sem):
    @pl.when(cond)
    def _():
        pltpu.make_async_copy(*first, sem).start()

    @pl.when(jnp.logical_not(cond))
    def _():
        pltpu.make_async_copy(*second, sem).start()


def half_lookup(ids, cond):
    value = jnp.full(ids.shape, 0.5 * cond[0], F32)
    for i in range(1, cond.shape[0]):
        value = jnp.where(ids == i, 0.5 * cond[i], value)
    return value


def wait_bytes(src, dst, sem):
    pltpu.make_async_copy(src, dst, sem).wait()


def put_columns(aux, cols):
    half = cols.shape[0] // 2
    aux[half:, :LANES] = cols[:half]
    aux[half:, LANES:] = cols[half:]


def get_columns(aux):
    half = aux.shape[0] // 2
    return jnp.concatenate([aux[half:, :LANES], aux[half:, LANES:]], 0)


def put_planes(dst, b_plane, p_plane, other):
    nx, width = b_plane.shape[0], p_plane.shape[1]
    lane = pl.multiple_of(other * width, LANES)
    row = pl.multiple_of(other * nx, SUBL)
    dst[:nx, :] = b_plane[:, pl.ds(lane, width)]
    dst[nx : 2 * nx, :] = p_plane[pl.ds(row, nx), :]


def keep_columns(own, slots, start, step, rs, edges):
    lanes = lax.broadcasted_iota(jnp.int32, (SUBL, LANES), 1)
    left, right = own[0, rs, :], own[1, rs, :]
    for offset in range(step):
        z = start + offset + slots
        first, last = edges(offset)
        both = pltpu.roll(jnp.where(lanes == 0, first, last), z, 1)
        left = jnp.where(lanes == z, both, left)
        right = jnp.where(lanes == lax.rem(z + LANES - 1, LANES), both, right)
    own[0, rs, :] = left
    own[1, rs, :] = right


def put_parts(e1_aux, x2, own, b_plane, p_plane, column, odd):
    nx = b_plane.shape[0]
    left, right = own[0], own[1]
    put_columns(e1_aux, jnp.where(odd, left, right))
    put_planes(e1_aux, b_plane, p_plane, column ^ 1)
    put_planes(x2, b_plane, p_plane, column ^ 2)
    aux = x2.at[2 * nx :]
    inner = (column > 0) & (column < TILE_Y - 1)
    put_columns(aux, jnp.where(inner, jnp.where(odd, right, left), 0.0))
    put_planes(aux, b_plane, p_plane, column ^ 3)


def pack_kernel(
    u, floor, ids, cond, e1, e2, x2, z1, z2, own, gv, mv, own_m, b_plane, mrow, sem
):
    g, m = floor.at[0], ids.at[0]
    group, column, odd, godd = place()
    nx, ny = u.shape[1], u.shape[2]
    nr, cx, width = g.shape
    step = SUBL
    chunks = nr // step
    shift = LANES // 2

    def load(c):
        at = pl.ds(c * step, step)
        return (
            pltpu.make_async_copy(g.at[at], gv.at[at], sem.at[2 * c]),
            pltpu.make_async_copy(m.at[at], mv.at[at], sem.at[2 * c + 1]),
        )

    base = 2 * chunks
    for copy in load(0):
        copy.start()
    plane = pltpu.make_async_copy(u.at[0], b_plane, sem.at[base])
    plane.start()
    low, high = g.at[:, 0, :], g.at[:, cx - 1, :]
    mrows = [
        pltpu.make_async_copy(m.at[:, r, :], mrow.at[s], sem.at[base + 1 + s])
        for r, s in ((0, 0), (cx - 1, 1))
    ]
    for copy in mrows + [copy for c in range(1, chunks) for copy in load(c)]:
        copy.start()
    select_copy(godd, (low, z1.at[:nr]), (high, z1.at[:nr]), sem.at[base + 3])
    select_copy(godd, (high, z2.at[:nr]), (low, z2.at[:nr]), sem.at[base + 4])
    rows_out = e1.at[:, :ny]
    select_copy(odd, (u.at[:, nx - 1, :], e2), (u.at[:, 0, :], e2), sem.at[base + 5])
    select_copy(odd, (u.at[:, 0, :], rows_out), (u.at[:, nx - 1, :], rows_out), sem.at[base + 6])
    own[...] = jnp.zeros_like(own)
    own_m[...] = jnp.zeros_like(own_m)

    def chunk(c, _):
        for copy in load(c):
            copy.wait()
        start = c * step
        for t in range(cx // SUBL):
            rs = slice(t * SUBL, (t + 1) * SUBL)

            def edges(ref):
                return lambda offset: (
                    ref[start + offset, rs, :LANES],
                    ref[start + offset, rs, width - LANES :],
                )

            keep_columns(own, 0, start, step, rs, edges(gv))
            keep_columns(own_m, shift, start, step, rs, edges(mv))
        return 0

    lax.fori_loop(0, chunks, chunk, 0)
    is_k = lax.broadcasted_iota(jnp.int32, (cx, LANES), 1) >= shift
    for s in range(2):
        codes = pltpu.roll(own_m[s], s, 1)
        own[s, :, :] = jnp.where(is_k, half_lookup(codes, cond), pltpu.roll(own[s], s, 1))
    plane.wait()
    put_parts(e1.at[:, ny:], x2, own, b_plane, gv.at[0], column, odd)
    for copy in mrows:
        copy.wait()
    k_low, k_high = half_lookup(mrow[0], cond), half_lookup(mrow[1], cond)
    z1[nr:, :] = jnp.where(godd, k_low, k_high)
    z2[nr:, :] = jnp.where(godd, k_high, k_low)
    wait_bytes(low, z1.at[:nr], sem.at[base + 3])
    wait_bytes(low, z2.at[:nr], sem.at[base + 4])
    wait_bytes(u.at[:, 0, :], e2, sem.at[base + 5])
    wait_bytes(u.at[:, 0, :], rows_out, sem.at[base + 6])


def coefficients_kernel(m, cond, u, f, ce, cw, cn, cz, urows, frows, kv, sem):
    nr, cx, width = m.shape
    nx = u.shape[1]
    picks = [(u.at[:, r, :], urows.at[i]) for i, r in enumerate((0, 1, nx - 2, nx - 1))]
    picks += [(f.at[:, r, :], frows.at[i]) for i, r in enumerate((0, nx - 1))]
    picks = [pltpu.make_async_copy(a, b, sem.at[i]) for i, (a, b) in enumerate(picks)]
    for copy in picks:
        copy.start()
    rows, lanes = iotas()
    r_last, l_first, l_last = rows == SUBL - 1, lanes == 0, lanes == LANES - 1
    tiles, wide = cx // SUBL, width // LANES
    spans = [slice(j * LANES, (j + 1) * LANES) for j in range(wide)]
    step = SUBL

    def layer(z):
        before = jnp.maximum(z - 1, 0)

        def tile(t):
            rs = slice(t * SUBL, (t + 1) * SUBL)
            ks = [half_lookup(m[z, rs, at], cond) for at in spans]
            return ks, [pltpu.roll(k, SUBL - 1, 0) for k in ks]

        ks, ups = tile(0)
        for t in range(tiles):
            rs = slice(t * SUBL, (t + 1) * SUBL)
            if t + 1 < tiles:
                kn, un = tile(t + 1)
            east = [pltpu.roll(k, LANES - 1, 1) for k in ks]
            west = [pltpu.roll(k, 1, 1) for k in ks]
            for j, at in enumerate(spans):
                k = ks[j]
                kv[z, rs, at] = k
                cz[before, rs, at] = kv[before, rs, at] + k
                if t + 1 < tiles:
                    cn[z, rs, at] = k + jnp.where(r_last, un[j], ups[j])
                else:
                    cn[z, rs, at] = jnp.where(r_last, 0.0, k + ups[j])
                if j + 1 < wide:
                    ce[z, rs, at] = k + jnp.where(l_last, east[j + 1], east[j])
                else:
                    ce[z, rs, at] = jnp.where(l_last, 0.0, k + east[j])
                if j > 0:
                    cw[z, rs, at] = k + jnp.where(l_first, west[j - 1], west[j])
                else:
                    cw[z, rs, at] = jnp.where(l_first, 0.0, k + west[j])
            if t + 1 < tiles:
                ks, ups = kn, un

    def chunk(c, _):
        for offset in range(step):
            layer(c * step + offset)
        return 0

    lax.fori_loop(0, nr // step, chunk, 0)
    cz[nr - 1, :, :] = kv[nr - 1]
    for copy in picks:
        copy.wait()


def floor_kernel(
    emit, g, ce, cw, cn, cz, u, x1, x2, x3, z1, z2, y1, y2, own, *rest
):
    nr, cx, width = g.shape
    nx, ny = u.shape[1], u.shape[2]
    if emit:
        out, own_new, o1, o2, kc, kr = rest[:6]
        ov, rest = out, rest[6:]
    else:
        kc, kr, out, ov = rest[:4]
        rest = rest[4:]
    fzv, tcol, trow, bv, sem = rest
    group, column, odd, godd = place()
    tiles, wide = cx // SUBL, width // LANES
    step = SUBL
    chunks = nr // step
    shift = LANES // 2
    aux, x3 = x1.at[:, ny:], x3.at[2 * nx :]
    groups = lax.axis_size("len") // TILE_Y
    known = (group ^ 1) < groups, jnp.where(godd, group + 1 < groups, group > 0)
    one, three = get_columns(aux), get_columns(x3)
    for s, halo in ((0, jnp.where(odd, one, three)), (1, jnp.where(odd, three, one))):
        if emit:
            kc[s, :, :] = pltpu.roll(own[s] + halo, shift, 1)
        tcol[s, :, :] = kc[s] * (halo - own[s])
    for s, (mine, halo) in enumerate(((z1, y1), (z2, y2))):
        halo = jnp.where(known[s], halo[...], 0.0)
        if emit:
            kr[s, :, :] = mine[nr:, :] + halo[nr:, :]
        side = kr[s] * (halo[:nr, :] - mine[:nr, :])
        trow[jnp.where(godd, s, 1 - s), :, :] = side
    row = lambda other: pl.ds(pl.multiple_of(other * nx, SUBL), nx)
    bv[row(column), :] = u[0, :, pl.ds(pl.multiple_of(column * width, LANES), width)]
    for k, ref in ((1, aux), (2, x2), (3, x3)):
        bv[row(column ^ k), :] = ref[:nx, :]
    rows, lanes = iotas()
    r_first, r_last = rows == 0, rows == SUBL - 1
    l_first, l_last = lanes == 0, lanes == LANES - 1
    fzv[...] = jnp.zeros_like(fzv)
    if emit:
        own_new[...] = jnp.zeros_like(own_new)
    spans = [slice(j * LANES, (j + 1) * LANES) for j in range(wide)]

    def layer(start, offset):
        z = start + offset
        back = lax.rem(LANES - z, LANES)
        above = z + 1
        if offset == step - 1:
            above = jnp.minimum(above, nr - 1)
            scale = jnp.where(z + 1 < nr, 1.0, 0.0)

        def tile(t):
            rs = slice(t * SUBL, (t + 1) * SUBL)
            gs = [g[z, rs, at] for at in spans]
            return gs, [pltpu.roll(v, SUBL - 1, 0) for v in gs]

        def row_of(s):
            block = trow[s, pl.ds(start, SUBL), :][offset : offset + 1]
            return [jnp.broadcast_to(block[:, at], (SUBL, LANES)) for at in spans]

        low, high = row_of(0), row_of(1)
        gs, ups = tile(0)
        prev = [-v for v in low]
        for t in range(tiles):
            rs = slice(t * SUBL, (t + 1) * SUBL)
            if t + 1 < tiles:
                gn, un = tile(t + 1)
            east = [pltpu.roll(v, LANES - 1, 1) for v in gs]
            west = [pltpu.roll(v, 1, 1) for v in gs]
            t_west = pltpu.roll(tcol[0, rs, :], back, 1)
            t_east = pltpu.roll(tcol[1, rs, :], LANES - 1 - z, 1)
            for j, at in enumerate(spans):
                v = gs[j]
                if t + 1 < tiles:
                    fx = cn[z, rs, at] * (jnp.where(r_last, un[j], ups[j]) - v)
                else:
                    fx = jnp.where(r_last, high[j], cn[z, rs, at] * (ups[j] - v))
                turned = pltpu.roll(fx, 1, 0)
                fxm = jnp.where(r_first, prev[j], turned)
                prev[j] = turned
                yp = jnp.where(l_last, east[j + 1], east[j]) if j + 1 < wide else east[j]
                ym = jnp.where(l_first, west[j - 1], west[j]) if j > 0 else west[j]
                side = ce[z, rs, at] * (yp - v) + cw[z, rs, at] * (ym - v)
                if j == 0:
                    side = side + jnp.where(l_first, t_west, 0.0)
                if j + 1 == wide:
                    side = side + jnp.where(l_last, t_east, 0.0)
                nxt = g[above, rs, at]
                if offset == step - 1:
                    nxt = scale * nxt
                fz = cz[z, rs, at] * (nxt - v)
                total = v + ((fx - fxm) + side + (fz - fzv[rs, at]))
                fzv[rs, at] = fz
                ov[z, rs, at] = total
            if t + 1 < tiles:
                gs, ups = gn, un

    def columns(start):
        for t in range(tiles):
            rs = slice(t * SUBL, (t + 1) * SUBL)
            edges = lambda offset: (
                ov[start + offset, rs, spans[0]],
                ov[start + offset, rs, spans[-1]],
            )
            keep_columns(own_new, 0, start, step, rs, edges)

    def store(c):
        at = pl.ds(c * step, step)
        return pltpu.make_async_copy(ov.at[at], out.at[at], sem.at[c])

    def store_rows(c):
        at = pl.ds(pl.multiple_of(c * step, SUBL), step)
        low, high = ov.at[at, 0, :], ov.at[at, cx - 1, :]
        select_copy(godd, (low, o1.at[at]), (high, o1.at[at]), sem.at[chunks + c])
        select_copy(godd, (high, o2.at[at]), (low, o2.at[at]), sem.at[2 * chunks + c])

    def chunk(c, _):
        start = pl.multiple_of(c * step, SUBL)
        for offset in range(step):
            layer(start, offset)

        @pl.when(c == 0)
        def _():
            ov[0, :, :] = ov[0] + HR * (bv[...] - g[0])

        if emit:
            store_rows(c)
            columns(start)
        else:
            store(c).start()
        return 0

    lax.fori_loop(0, chunks, chunk, 0)
    if emit:
        own_new[1, :, :] = pltpu.roll(own_new[1], 1, 1)
    for c in range(chunks):
        if emit:
            at = pl.ds(c * step, step)
            wait_bytes(ov.at[at, 0, :], o1.at[at], sem.at[chunks + c])
            wait_bytes(ov.at[at, 0, :], o2.at[at], sem.at[2 * chunks + c])
        else:
            store(c).wait()


def floor_sweep(emit, g, coefs, u, x1, x2, x3, z1, z2, y1, y2, own, halos=()):
    nr, cx, width = g.shape
    scratch = [
        pltpu.VMEM((cx, width), F32),
        pltpu.VMEM((2, cx, LANES), F32),
        pltpu.VMEM((2, nr, width), F32),
        pltpu.VMEM((cx, width), F32),
        pltpu.SemaphoreType.DMA((3 * nr // SUBL,)),
    ]
    if emit:
        outs = [
            shape(g.shape),
            shape(own.shape),
            shape((nr, width)),
            shape((nr, width)),
            shape(own.shape),
            shape((2, nr, width)),
        ]
        specs = [VMEM] * 6
    else:
        outs, specs = [far(g.shape)], [ANY]
        scratch = [pltpu.VMEM(g.shape, F32)] + scratch
    return pl.pallas_call(
        functools.partial(floor_kernel, emit),
        out_shape=outs,
        in_specs=[VMEM] * (14 + len(halos)),
        out_specs=specs,
        scratch_shapes=scratch,
        compiler_params=params(2 if emit else 6),
        cost_estimate=cost(0, 16 << 20),
        name="floor_sweep",
    )(*in_vmem(g, *coefs, u, x1, x2, x3, z1, z2, y1, y2, own, *halos))


def tin_layer(u, f, e1, e2, speeds, start, offset, out):
    zt, nx, ny = u.shape
    _, _, odd, _ = place()
    pos = lax.axis_index("len")
    alone = (pos == 0) | (pos == lax.axis_size("len") - 1)
    rows, lanes = iotas()
    r_first, r_last = rows == 0, rows == SUBL - 1
    l_first, l_last = lanes == 0, lanes == LANES - 1
    tiles, wide = nx // SUBL, ny // LANES
    zero = jnp.zeros((SUBL, LANES), F32)
    z = start + offset
    sx, sy = speeds[0, z], speeds[1, z]
    centre = 1.0 - 6.0 * KT - sx - sy - jnp.where(z == 0, HT, 0.0)
    above, below = jnp.minimum(z + 1, zt - 1), jnp.maximum(z - 1, 0)

    def get(ref, z_, t, j):
        return ref[z_, t * SUBL : (t + 1) * SUBL, j * LANES : (j + 1) * LANES]

    left = [zero] * tiles
    now = [get(u, z, t, 0) for t in range(tiles)]
    turned = [pltpu.roll(v, LANES - 1, 1) for v in now]
    for j in range(wide):
        at = slice(j * LANES, (j + 1) * LANES)
        if j + 1 < wide:
            nxt = [get(u, z, t, j + 1) for t in range(tiles)]
            nxt_turned = [pltpu.roll(v, LANES - 1, 1) for v in nxt]
        else:
            nxt, nxt_turned = None, [zero] * tiles
        one = e1[pl.ds(start, SUBL), at][offset : offset + 1]
        two = jnp.where(alone, 0.0, e2[pl.ds(start, SUBL), at][offset : offset + 1])
        low = jnp.broadcast_to(jnp.where(odd, one, two), (SUBL, LANES))
        high = jnp.broadcast_to(jnp.where(odd, two, one), (SUBL, LANES))
        downs = [low] + [pltpu.roll(v, 1, 0) for v in now]
        ups = [pltpu.roll(v, SUBL - 1, 0) for v in now] + [high]
        for t in range(tiles):
            v = now[t]
            xm = jnp.where(r_first, downs[t], downs[t + 1])
            xp = jnp.where(r_last, ups[t + 1], ups[t])
            turn = pltpu.roll(v, 1, 1)
            ym = jnp.where(l_first, left[t], turn)
            yp = jnp.where(l_last, nxt_turned[t], turned[t])
            left[t] = turn
            code = get(f, z, t, j)
            xs = jnp.where((code & 1) == 0, xm, xp)
            ys = jnp.where(code < 2, ym, yp)
            spread = (xm + xp) + (ym + yp) + (get(u, above, t, j) + get(u, below, t, j))
            out[t * SUBL : (t + 1) * SUBL, at] = (centre * v + KT * spread) + (sx * xs + sy * ys)
        now, turned = nxt, nxt_turned


def gather_floor_top(pv, e1, x2, x3, g):
    nx, ny = pv.shape
    width = x2.shape[1]
    column = place()[1]
    lanes_at = lambda other: pl.ds(pl.multiple_of(other * width, LANES), width)
    pv[:, lanes_at(column)] = g[0, pl.ds(pl.multiple_of(column * nx, SUBL), nx), :]
    for k, ref in ((1, e1.at[:, ny:]), (2, x2), (3, x3.at[2 * nx :])):
        pv[:, lanes_at(column ^ k)] = ref[nx : 2 * nx, :]


def edge_kernel(u, f, urows, frows, x2, x3, e1, e2, g, g_new, own, speeds, ox2, o1, o2, pv, plane):
    zt, nx, ny = u.shape
    group, column, odd, _ = place()
    pos = lax.axis_index("len")
    alone = (pos == 0) | (pos == lax.axis_size("len") - 1)
    gather_floor_top(pv, e1, x2, x3, g)
    tin_layer(u, f, e1, e2, speeds, 0, 0, plane)
    plane[...] = plane[...] + HT * pv[...]
    put_parts(o1.at[:, ny:], ox2, own, plane, g_new.at[0], column, odd)
    rows, lanes = iotas()
    r_first, r_last = rows == 0, rows == SUBL - 1
    l_first, l_last = lanes == 0, lanes == LANES - 1
    wide, blocks = ny // LANES, zt // SUBL
    zero = jnp.zeros((SUBL, LANES), F32)

    def block(b, _):
        start = pl.multiple_of(b * SUBL, SUBL)
        here = pl.ds(start, SUBL)
        before = pl.ds(pl.multiple_of(jnp.maximum(start - SUBL, 0), SUBL), SUBL)
        after = pl.ds(pl.multiple_of(jnp.minimum(start + SUBL, zt - SUBL), SUBL), SUBL)
        bottom, top = b == 0, b == blocks - 1
        sx = sy = zero
        for i in range(SUBL):
            sx = jnp.where(rows == i, speeds[0, start + i], sx)
            sy = jnp.where(rows == i, speeds[1, start + i], sy)
        contact = jnp.where(r_first & bottom, HT, 0.0)
        centre = 1.0 - 6.0 * KT - sx - sy - contact
        outs = []
        for s, (edge, inner, side) in enumerate(((0, 1, 0), (3, 2, nx - 1))):
            vs = [urows[edge, here, j * LANES : (j + 1) * LANES] for j in range(wide)]
            east = [pltpu.roll(v, LANES - 1, 1) for v in vs] + [zero]
            west = [zero] + [pltpu.roll(v, 1, 1) for v in vs]
            for j in range(wide):
                at = slice(j * LANES, (j + 1) * LANES)
                v, code, inside = vs[j], frows[s, here, at], urows[inner, here, at]
                one, two = e1[here, at], jnp.where(alone, 0.0, e2[here, at])
                outside = jnp.where(odd, two, one) if s else jnp.where(odd, one, two)
                xm, xp = (inside, outside) if s else (outside, inside)
                ym = jnp.where(l_first, west[j], west[j + 1])
                yp = jnp.where(l_last, east[j + 1], east[j])
                above, below = urows[edge, after, at], urows[edge, before, at]
                above = jnp.where(top, pltpu.roll(v, 1, 0), above)
                below = jnp.where(bottom, pltpu.roll(v, SUBL - 1, 0), below)
                above = jnp.where(r_last, pltpu.roll(above, SUBL - 1, 0), pltpu.roll(v, SUBL - 1, 0))
                below = jnp.where(r_first, pltpu.roll(below, 1, 0), pltpu.roll(v, 1, 0))
                xs = jnp.where((code & 1) == 0, xm, xp)
                ys = jnp.where(code < 2, ym, yp)
                spread = (xm + xp) + (ym + yp) + (above + below)
                new = (centre * v + KT * spread) + (sx * xs + sy * ys)
                new = new + contact * jnp.broadcast_to(pv[side : side + 1, at], (SUBL, LANES))
                outs.append(new)
        for j in range(wide):
            at = slice(j * LANES, (j + 1) * LANES)
            low, high = outs[j], outs[wide + j]
            o1[here, at] = jnp.where(odd, low, high)
            o2[here, at] = jnp.where(odd, high, low)
        return 0

    lax.fori_loop(0, blocks, block, 0)


def edge_sweep(u, f, urows, frows, x2, x3, e1, e2, g, g_new, own, speeds):
    plane = pltpu.VMEM(u.shape[1:], F32)
    return pl.pallas_call(
        edge_kernel,
        out_shape=[shape(v.shape) for v in (x2, e1, e2)],
        in_specs=[VMEM] * 11 + [SMEM],
        out_specs=[VMEM] * 3,
        scratch_shapes=[plane, plane],
        compiler_params=params(2),
        cost_estimate=cost(0, 4 << 20),
        name="edge",
    )(*in_vmem(u, f, urows, frows, x2, x3, e1, e2, g, g_new, own), speeds)


def tin_kernel(final, u, f, x2, x3, e1, e2, g, speeds, out, *rest):
    zt, nx, ny = u.shape
    if final:
        ov, rest = rest[0], rest[1:]
    else:
        ov = out
    pv, sem = rest
    step = SUBL
    gather_floor_top(pv, e1, x2, x3, g)

    def store(c):
        at = pl.ds(c * step, step)
        return pltpu.make_async_copy(ov.at[at], out.at[at], sem.at[c])

    def chunk(c, _):
        start = pl.multiple_of(c * step, SUBL)
        for offset in range(step):
            tin_layer(u, f, e1, e2, speeds, start, offset, ov.at[start + offset])

        @pl.when(c == 0)
        def _():
            ov[0, :, :] = ov[0] + HT * pv[...]

        if final:
            store(c).start()
        return 0

    lax.fori_loop(0, zt // step, chunk, 0)
    if final:
        for c in range(zt // step):
            store(c).wait()


def tin_sweep(final, u, f, x2, x3, e1, e2, g, speeds):
    zt, nx, ny = u.shape
    scratch = [pltpu.VMEM((nx, ny), F32), pltpu.SemaphoreType.DMA((zt // SUBL,))]
    if final:
        out, spec, scratch = far(u.shape), ANY, [pltpu.VMEM(u.shape, F32)] + scratch
    else:
        out, spec = shape(u.shape), VMEM
    return pl.pallas_call(
        functools.partial(tin_kernel, final),
        out_shape=out,
        in_specs=[VMEM] * 7 + [SMEM],
        out_specs=spec,
        scratch_shapes=scratch,
        compiler_params=params(6 if final else 2),
        cost_estimate=cost(0, 20 << 20),
        name="tin_sweep",
    )(*in_vmem(u, f, x2, x3, e1, e2, g), speeds)


def local(tin_temp, flow_code, speeds, floor_temp, material, conductivity):
    u, f, g, m = tin_temp, flow_code, floor_temp[0], material[0]
    zt, nx, ny = u.shape
    nr, cx, width = g.shape
    e1, e2, x2, z1, z2, own, gv, mv = pl.pallas_call(
        pack_kernel,
        out_shape=[
            shape((zt, ny + 2 * LANES)),
            shape((zt, ny)),
            shape((2 * nx + cx, width)),
            shape((2 * nr, width)),
            shape((2 * nr, width)),
            shape((2, cx, LANES)),
            shape(g.shape),
            shape(g.shape, jnp.int32),
        ],
        in_specs=[ANY, ANY, ANY, SMEM],
        out_specs=[VMEM] * 8,
        scratch_shapes=[
            pltpu.VMEM((2, cx, LANES), jnp.int32),
            pltpu.VMEM((nx, ny), F32),
            pltpu.VMEM((2, nr, width), jnp.int32),
            pltpu.SemaphoreType.DMA((2 * nr // SUBL + 7,)),
        ],
        compiler_params=params(2),
        cost_estimate=cost(0, 12 << 20),
        name="pack",
    )(*in_hbm(u, floor_temp, material), conductivity)
    x2 = swap(x2, "x2")
    y1, y2 = swap(z1, "z1"), swap(z2, "z2")
    e1, e2 = swap(e1, "e1"), swap(e2, "e2")
    *coefs, urows, frows = pl.pallas_call(
        coefficients_kernel,
        out_shape=[shape(g.shape)] * 4
        + [shape((4, zt, ny)), shape((2, zt, ny), jnp.int32)],
        in_specs=[VMEM, SMEM, ANY, ANY],
        out_specs=[VMEM] * 6,
        scratch_shapes=[pltpu.VMEM(g.shape, F32), pltpu.SemaphoreType.DMA((6,))],
        compiler_params=params(6),
        cost_estimate=cost(0, 16 << 20),
        name="coefficients",
    )(*in_vmem(mv), conductivity, *in_hbm(u, f))
    x2, coefs[0] = lax.optimization_barrier((x2, coefs[0]))
    x3 = swap(x2, "e1")
    g1, own1, z1, z2, kc, kr = floor_sweep(
        True, gv, coefs, u, e1, x2, x3, z1, z2, y1, y2, own
    )
    w2, w1, d2 = edge_sweep(u, f, urows, frows, x2, x3, e1, e2, gv, g1, own1, speeds)
    w2 = swap(w2, "x2")
    y1, y2 = swap(z1, "z1"), swap(z2, "z2")
    w1, d2 = swap(w1, "e1"), swap(d2, "e2")
    u1 = tin_sweep(False, u, f, x2, x3, e1, e2, gv, speeds)
    w2, u1 = lax.optimization_barrier((w2, u1))
    w3 = swap(w2, "e1")
    (g2,) = floor_sweep(
        False, g1, coefs, u1, w1, w2, w3, z1, z2, y1, y2, own1, (kc, kr)
    )
    u2 = tin_sweep(True, u1, f, w2, w3, w1, d2, g1, speeds)
    return u2, g2[None]


def solution(mesh):
    placed = (
        P(None, ("grp", "len"), None),
        P(None, ("grp", "len"), None),
        P(),
        P(("grp", "len"), None, None, None),
        P(("grp", "len"), None, None, None),
        P(),
    )
    return jax.shard_map(
        local,
        mesh=mesh,
        in_specs=placed,
        out_specs=(P(None, ("grp", "len"), None), P(("grp", "len"), None, None, None)),
        check_vma=False,
    )
```

```python
import functools

import jax
import jax.numpy as jnp
from jax import lax
from jax.experimental import pallas as pl
from jax.experimental.pallas import tpu as pltpu
from jax.sharding import PartitionSpec as P

TILE_Y = 4
KT = 0.1
HT = 0.2
HR = 0.2
LANES = 128
SUBL = 8
F32 = jnp.float32
ANY = pl.BlockSpec(memory_space=pl.ANY)
VMEM = pl.BlockSpec(memory_space=pltpu.VMEM)


def params(mib):
    return pltpu.CompilerParams(vmem_limit_bytes=mib * 1024 * 1024)


def shape(dims, dtype=F32):
    return pltpu.VMEM(dims, dtype)


def far(dims, dtype=F32):
    return pltpu.HBM(dims, dtype)


def in_hbm(*arrays):
    return [pltpu.with_memory_space_constraint(a, pltpu.HBM) for a in arrays]


def in_vmem(*arrays):
    return [pltpu.with_memory_space_constraint(a, pltpu.VMEM) for a in arrays]


def cost(flops, nbytes):
    return pl.CostEstimate(flops=flops, bytes_accessed=nbytes, transcendentals=0)


def place():
    pos = lax.axis_index("len")
    group, column = pos // TILE_Y, pos % TILE_Y
    return group, column, pos % 2 == 1, group % 2 == 1


def iotas():
    rows = lax.broadcasted_iota(jnp.int32, (SUBL, LANES), 0)
    lanes = lax.broadcasted_iota(jnp.int32, (SUBL, LANES), 1)
    return rows, lanes


def partner(kind, pos):
    return {
        "e1": lambda: pos ^ 1,
        "e2": lambda: pos + 1 if pos % 2 else pos - 1,
        "x2": lambda: pos ^ 2,
        "x3": lambda: pos ^ 3,
        "z1": lambda: pos ^ TILE_Y,
        "z2": lambda: pos + TILE_Y if (pos // TILE_Y) % 2 else pos - TILE_Y,
    }[kind]()


def swap(value, kind):
    count, parts = lax.axis_size("len"), lax.axis_size("grp")
    pairs = []
    for part in range(parts):
        for pos in range(count):
            to, other = part, partner(kind, pos)
            if not 0 <= other < count:
                to, other = (part ^ 1, pos) if kind == "e2" else (part, pos ^ 1)
            if 0 <= to < parts:
                pairs.append((part * count + pos, to * count + other))
    return lax.ppermute(value, ("grp", "len"), pairs)


def select_copy(cond, first, second, sem):
    @pl.when(cond)
    def _():
        pltpu.make_async_copy(*first, sem).start()

    @pl.when(jnp.logical_not(cond))
    def _():
        pltpu.make_async_copy(*second, sem).start()


def half_coded(codes, halves):
    value = jnp.zeros(codes.shape, F32)
    for i in range(halves.shape[0]):
        value = jnp.where(codes == i + 1.0, halves[i, 0:1, 0:1], value)
    return value


def wait_bytes(src, dst, sem):
    pltpu.make_async_copy(src, dst, sem).wait()


def put_columns(aux, cols):
    half = cols.shape[0] // 2
    aux[half:, :LANES] = cols[:half]
    aux[half:, LANES:] = cols[half:]


def get_columns(aux):
    half = aux.shape[0] // 2
    return jnp.concatenate([aux[half:, :LANES], aux[half:, LANES:]], 0)


def put_planes(dst, b_plane, p_plane, other):
    nx, width = b_plane.shape[0], p_plane.shape[1]
    lane = pl.multiple_of(other * width, LANES)
    row = pl.multiple_of(other * nx, SUBL)
    dst[:nx, :] = b_plane[:, pl.ds(lane, width)]
    dst[nx : 2 * nx, :] = p_plane[pl.ds(row, nx), :]


def keep_columns(own, slots, start, step, rs, edges):
    lanes = lax.broadcasted_iota(jnp.int32, (SUBL, LANES), 1)
    left, right = own[0, rs, :], own[1, rs, :]
    for offset in range(step):
        z = start + offset + slots
        first, last = edges(offset)
        both = pltpu.roll(jnp.where(lanes == 0, first, last), z, 1)
        left = jnp.where(lanes == z, both, left)
        right = jnp.where(lanes == lax.rem(z + LANES - 1, LANES), both, right)
    own[0, rs, :] = left
    own[1, rs, :] = right


def put_parts(e1_aux, x2, x3, own, b_plane, p_plane, column, odd):
    nx = b_plane.shape[0]
    left, right = own[0], own[1]
    put_columns(e1_aux, jnp.where(odd, left, right))
    put_planes(e1_aux, b_plane, p_plane, column ^ 1)
    put_planes(x2, b_plane, p_plane, column ^ 2)
    inner = (column > 0) & (column < TILE_Y - 1)
    put_columns(x3, jnp.where(inner, jnp.where(odd, right, left), 0.0))
    put_planes(x3, b_plane, p_plane, column ^ 3)


def pack_kernel(
    u, floor, ids, speeds, cond, e1, e2, x2, x3, z1, z2, own, gv, mv, rates, halves,
    own_m, b_plane, mrow, speeds_v, cond_v, sem
):
    g, m = floor.at[0], ids.at[0]
    group, column, odd, godd = place()
    nx, ny = u.shape[1], u.shape[2]
    nr, cx, width = g.shape
    step = SUBL
    chunks = nr // step
    shift = LANES // 2

    def load(c):
        at = pl.ds(c * step, step)
        return (
            pltpu.make_async_copy(g.at[at], gv.at[at], sem.at[2 * c]),
            pltpu.make_async_copy(m.at[at], mv.at[at], sem.at[2 * c + 1]),
        )

    base = 2 * chunks
    for copy in load(0):
        copy.start()
    plane = pltpu.make_async_copy(u.at[0], b_plane, sem.at[base])
    plane.start()
    low, high = g.at[:, 0, :], g.at[:, cx - 1, :]
    mrows = [
        pltpu.make_async_copy(m.at[:, r, :], mrow.at[s], sem.at[base + 1 + s])
        for r, s in ((0, 0), (cx - 1, 1))
    ]
    for copy in mrows + [copy for c in range(1, chunks) for copy in load(c)]:
        copy.start()
    select_copy(godd, (low, z1.at[:nr]), (high, z1.at[:nr]), sem.at[base + 3])
    select_copy(godd, (high, z2.at[:nr]), (low, z2.at[:nr]), sem.at[base + 4])
    small = (
        pltpu.make_async_copy(speeds, speeds_v, sem.at[base + 7]),
        pltpu.make_async_copy(cond, cond_v, sem.at[base + 8]),
    )
    for copy in small:
        copy.start()
    rows_out = e1.at[:, :ny]
    select_copy(odd, (u.at[:, nx - 1, :], e2), (u.at[:, 0, :], e2), sem.at[base + 5])
    select_copy(odd, (u.at[:, 0, :], rows_out), (u.at[:, nx - 1, :], rows_out), sem.at[base + 6])
    own[...] = jnp.zeros_like(own)
    own_m[...] = jnp.zeros_like(own_m)

    def chunk(c, _):
        for copy in load(c):
            copy.wait()
        start = c * step
        for t in range(cx // SUBL):
            rs = slice(t * SUBL, (t + 1) * SUBL)

            def edges(ref):
                return lambda offset: (
                    ref[start + offset, rs, :LANES],
                    ref[start + offset, rs, width - LANES :],
                )

            keep_columns(own, 0, start, step, rs, edges(gv))
            keep_columns(own_m, shift, start, step, rs, edges(mv))
        return 0

    lax.fori_loop(0, chunks, chunk, 0)
    is_k = lax.broadcasted_iota(jnp.int32, (cx, LANES), 1) >= shift
    for s in range(2):
        codes = pltpu.roll(own_m[s], s, 1)
        own[s, :, :] = jnp.where(is_k, codes.astype(F32) + 1.0, pltpu.roll(own[s], s, 1))
    plane.wait()
    put_parts(e1.at[:, ny:], x2, x3, own, b_plane, gv.at[0], column, odd)
    for copy in mrows:
        copy.wait()
    m_low, m_high = mrow[0].astype(F32) + 1.0, mrow[1].astype(F32) + 1.0
    z1[nr:, :] = jnp.where(godd, m_low, m_high)
    z2[nr:, :] = jnp.where(godd, m_high, m_low)
    for copy in small:
        copy.wait()
    zt = u.shape[0]
    diagonal = lax.broadcasted_iota(jnp.int32, (zt, zt), 0) == lax.broadcasted_iota(
        jnp.int32, (zt, zt), 1
    )
    for s in range(2):
        spread = jnp.where(diagonal, jnp.broadcast_to(speeds_v[s : s + 1, :], (zt, zt)), 0.0)
        along = jnp.sum(spread, axis=1, keepdims=True)
        rates[s, :, :] = jnp.broadcast_to(along, (zt, LANES))
    for i in range(halves.shape[0]):
        halves[i, :, :] = jnp.broadcast_to(0.5 * cond_v[0:1, i : i + 1], (SUBL, LANES))
    wait_bytes(low, z1.at[:nr], sem.at[base + 3])
    wait_bytes(low, z2.at[:nr], sem.at[base + 4])
    wait_bytes(u.at[:, 0, :], e2, sem.at[base + 5])
    wait_bytes(u.at[:, 0, :], rows_out, sem.at[base + 6])


def coefficients_kernel(m, halves, u, f, ce, cw, cn, cz, urows, frows, kv, sem):
    nr, cx, width = m.shape
    nx = u.shape[1]
    picks = [(u.at[:, r, :], urows.at[i]) for i, r in enumerate((1, nx - 2))]
    picks += [(f.at[:, r, :], frows.at[i]) for i, r in enumerate((0, nx - 1))]
    picks = [pltpu.make_async_copy(a, b, sem.at[i]) for i, (a, b) in enumerate(picks)]
    for copy in picks:
        copy.start()
    rows, lanes = iotas()
    r_last, l_first, l_last = rows == SUBL - 1, lanes == 0, lanes == LANES - 1
    tiles, wide = cx // SUBL, width // LANES
    spans = [slice(j * LANES, (j + 1) * LANES) for j in range(wide)]
    step = SUBL
    values = [halves[i] for i in range(halves.shape[0])]

    def lookup(ids):
        value = values[0]
        for i in range(1, len(values)):
            value = jnp.where(ids == i, values[i], value)
        return value

    def layer(z):
        before = jnp.maximum(z - 1, 0)

        def tile(t):
            rs = slice(t * SUBL, (t + 1) * SUBL)
            ks = [lookup(m[z, rs, at]) for at in spans]
            return ks, [pltpu.roll(k, SUBL - 1, 0) for k in ks]

        ks, ups = tile(0)
        for t in range(tiles):
            rs = slice(t * SUBL, (t + 1) * SUBL)
            if t + 1 < tiles:
                kn, un = tile(t + 1)
            east = [pltpu.roll(k, LANES - 1, 1) for k in ks]
            west = [pltpu.roll(k, 1, 1) for k in ks]
            for j, at in enumerate(spans):
                k = ks[j]
                kv[z, rs, at] = k
                cz[before, rs, at] = kv[before, rs, at] + k
                if t + 1 < tiles:
                    cn[z, rs, at] = k + jnp.where(r_last, un[j], ups[j])
                else:
                    cn[z, rs, at] = jnp.where(r_last, 0.0, k + ups[j])
                if j + 1 < wide:
                    ce[z, rs, at] = k + jnp.where(l_last, east[j + 1], east[j])
                else:
                    ce[z, rs, at] = jnp.where(l_last, 0.0, k + east[j])
                if j > 0:
                    cw[z, rs, at] = k + jnp.where(l_first, west[j - 1], west[j])
                else:
                    cw[z, rs, at] = jnp.where(l_first, 0.0, k + west[j])
            if t + 1 < tiles:
                ks, ups = kn, un

    def chunk(c, _):
        for offset in range(step):
            layer(c * step + offset)
        return 0

    lax.fori_loop(0, nr // step, chunk, 0)
    cz[nr - 1, :, :] = kv[nr - 1]
    for copy in picks:
        copy.wait()


def floor_kernel(
    emit, g, ce, cw, cn, cz, u, x1, x2, x3, z1, z2, y1, y2, own, *rest
):
    nr, cx, width = g.shape
    nx, ny = u.shape[1], u.shape[2]
    if emit:
        halves, out, own_new, o1, o2, kc, kr = rest[:7]
        ov, rest = out, rest[7:]
    else:
        kc, kr, out, ov = rest[:4]
        rest = rest[4:]
    fzv, tcol, trow, bv, sem = rest
    group, column, odd, godd = place()
    tiles, wide = cx // SUBL, width // LANES
    step = SUBL
    chunks = nr // step
    shift = LANES // 2
    aux = x1.at[:, ny:]
    groups = lax.axis_size("len") // TILE_Y
    known = (group ^ 1) < groups, jnp.where(godd, group + 1 < groups, group > 0)
    one, three = get_columns(aux), get_columns(x3)
    for s, halo in ((0, jnp.where(odd, one, three)), (1, jnp.where(odd, three, one))):
        if emit:
            both = half_coded(own[s], halves) + half_coded(halo, halves)
            kc[s, :, :] = pltpu.roll(both, shift, 1)
        tcol[s, :, :] = kc[s] * (halo - own[s])
    for s, (mine, halo) in enumerate(((z1, y1), (z2, y2))):
        halo = jnp.where(known[s], halo[...], 0.0)
        if emit:
            kr[s, :, :] = half_coded(mine[nr:, :], halves) + half_coded(halo[nr:, :], halves)
        side = kr[s] * (halo[:nr, :] - mine[:nr, :])
        trow[jnp.where(godd, s, 1 - s), :, :] = side
    row = lambda other: pl.ds(pl.multiple_of(other * nx, SUBL), nx)
    bv[row(column), :] = u[0, :, pl.ds(pl.multiple_of(column * width, LANES), width)]
    for k, ref in ((1, aux), (2, x2), (3, x3)):
        bv[row(column ^ k), :] = ref[:nx, :]
    rows, lanes = iotas()
    r_first, r_last = rows == 0, rows == SUBL - 1
    l_first, l_last = lanes == 0, lanes == LANES - 1
    fzv[...] = jnp.zeros_like(fzv)
    if emit:
        own_new[...] = jnp.zeros_like(own_new)
    spans = [slice(j * LANES, (j + 1) * LANES) for j in range(wide)]

    def layer(start, offset):
        z = start + offset
        back = lax.rem(LANES - z, LANES)
        above = z + 1
        if offset == step - 1:
            above = jnp.minimum(above, nr - 1)
            scale = jnp.where(z + 1 < nr, 1.0, 0.0)

        def tile(t):
            rs = slice(t * SUBL, (t + 1) * SUBL)
            gs = [g[z, rs, at] for at in spans]
            return gs, [pltpu.roll(v, SUBL - 1, 0) for v in gs]

        def row_of(s):
            block = trow[s, pl.ds(start, SUBL), :][offset : offset + 1]
            return [jnp.broadcast_to(block[:, at], (SUBL, LANES)) for at in spans]

        low, high = row_of(0), row_of(1)
        gs, ups = tile(0)
        prev = [-v for v in low]
        for t in range(tiles):
            rs = slice(t * SUBL, (t + 1) * SUBL)
            if t + 1 < tiles:
                gn, un = tile(t + 1)
            east = [pltpu.roll(v, LANES - 1, 1) for v in gs]
            west = [pltpu.roll(v, 1, 1) for v in gs]
            t_west = pltpu.roll(tcol[0, rs, :], back, 1)
            t_east = pltpu.roll(tcol[1, rs, :], LANES - 1 - z, 1)
            for j, at in enumerate(spans):
                v = gs[j]
                if t + 1 < tiles:
                    fx = cn[z, rs, at] * (jnp.where(r_last, un[j], ups[j]) - v)
                else:
                    fx = jnp.where(r_last, high[j], cn[z, rs, at] * (ups[j] - v))
                turned = pltpu.roll(fx, 1, 0)
                fxm = jnp.where(r_first, prev[j], turned)
                prev[j] = turned
                yp = jnp.where(l_last, east[j + 1], east[j]) if j + 1 < wide else east[j]
                ym = jnp.where(l_first, west[j - 1], west[j]) if j > 0 else west[j]
                side = ce[z, rs, at] * (yp - v) + cw[z, rs, at] * (ym - v)
                if j == 0:
                    side = side + jnp.where(l_first, t_west, 0.0)
                if j + 1 == wide:
                    side = side + jnp.where(l_last, t_east, 0.0)
                nxt = g[above, rs, at]
                if offset == step - 1:
                    nxt = scale * nxt
                fz = cz[z, rs, at] * (nxt - v)
                total = v + ((fx - fxm) + side + (fz - fzv[rs, at]))
                fzv[rs, at] = fz
                ov[z, rs, at] = total
            if t + 1 < tiles:
                gs, ups = gn, un

    def columns(start):
        for t in range(tiles):
            rs = slice(t * SUBL, (t + 1) * SUBL)
            edges = lambda offset: (
                ov[start + offset, rs, spans[0]],
                ov[start + offset, rs, spans[-1]],
            )
            keep_columns(own_new, 0, start, step, rs, edges)

    def store(c):
        at = pl.ds(c * step, step)
        return pltpu.make_async_copy(ov.at[at], out.at[at], sem.at[c])

    def store_rows(c):
        at = pl.ds(pl.multiple_of(c * step, SUBL), step)
        low, high = ov.at[at, 0, :], ov.at[at, cx - 1, :]
        select_copy(godd, (low, o1.at[at]), (high, o1.at[at]), sem.at[chunks + c])
        select_copy(godd, (high, o2.at[at]), (low, o2.at[at]), sem.at[2 * chunks + c])

    def chunk(c, _):
        start = pl.multiple_of(c * step, SUBL)
        for offset in range(step):
            layer(start, offset)

        @pl.when(c == 0)
        def _():
            ov[0, :, :] = ov[0] + HR * (bv[...] - g[0])

        if emit:
            store_rows(c)
            columns(start)
        else:
            store(c).start()
        return 0

    lax.fori_loop(0, chunks, chunk, 0)
    if emit:
        own_new[1, :, :] = pltpu.roll(own_new[1], 1, 1)
    if emit:
        for c in range(chunks):
            at = pl.ds(c * step, step)
            wait_bytes(ov.at[at, 0, :], o1.at[at], sem.at[chunks + c])
            wait_bytes(ov.at[at, 0, :], o2.at[at], sem.at[2 * chunks + c])
        return []
    return [store(c) for c in range(chunks)]


def floor_scratch(dims):
    nr, cx, width = dims
    return [
        pltpu.VMEM((cx, width), F32),
        pltpu.VMEM((2, cx, LANES), F32),
        pltpu.VMEM((2, nr, width), F32),
        pltpu.VMEM((cx, width), F32),
        pltpu.SemaphoreType.DMA((3 * nr // SUBL,)),
    ]


def floor_first(g, coefs, u, x1, x2, x3, z1, z2, y1, y2, own, halves):
    nr, cx, width = g.shape

    def kernel(*refs):
        floor_kernel(True, *refs)

    return pl.pallas_call(
        kernel,
        out_shape=[
            shape(g.shape),
            shape(own.shape),
            shape((nr, width)),
            shape((nr, width)),
            shape(own.shape),
            shape((2, nr, width)),
        ],
        in_specs=[VMEM] * 15,
        out_specs=[VMEM] * 6,
        scratch_shapes=floor_scratch(g.shape),
        compiler_params=params(2),
        cost_estimate=cost(0, 16 << 20),
        name="floor_first",
    )(*in_vmem(g, *coefs, u, x1, x2, x3, z1, z2, y1, y2, own, halves))


def fill_halo(halo, e1, e2):
    odd, pos, ny = place()[2], lax.axis_index("len"), halo.shape[2]
    alone = (pos == 0) | (pos == lax.axis_size("len") - 1)
    one, two = e1[:, :ny], jnp.where(alone, 0.0, e2[...])
    halo[0, :, :] = jnp.where(odd, one, two)
    halo[1, :, :] = jnp.where(odd, two, one)


def tin_layer(u, f, halo, rates, start, offset, out):
    zt, nx, ny = u.shape
    rows, lanes = iotas()
    r_first, r_last = rows == 0, rows == SUBL - 1
    l_first, l_last = lanes == 0, lanes == LANES - 1
    tiles, wide = nx // SUBL, ny // LANES
    zero = jnp.zeros((SUBL, LANES), F32)
    z = start + offset
    sx, sy = (
        jnp.broadcast_to(rates[s, pl.ds(start, SUBL), :][offset : offset + 1], (SUBL, LANES))
        for s in range(2)
    )
    centre = 1.0 - 6.0 * KT - sx - sy
    if offset == 0:
        centre = centre - jnp.where(z == 0, HT, 0.0)
    above, below = jnp.minimum(z + 1, zt - 1), jnp.maximum(z - 1, 0)

    def get(ref, z_, t, j):
        return ref[z_, t * SUBL : (t + 1) * SUBL, j * LANES : (j + 1) * LANES]

    left = [zero] * tiles
    now = [get(u, z, t, 0) for t in range(tiles)]
    turned = [pltpu.roll(v, LANES - 1, 1) for v in now]
    for j in range(wide):
        at = slice(j * LANES, (j + 1) * LANES)
        if j + 1 < wide:
            nxt = [get(u, z, t, j + 1) for t in range(tiles)]
            nxt_turned = [pltpu.roll(v, LANES - 1, 1) for v in nxt]
        else:
            nxt, nxt_turned = None, [zero] * tiles
        low, high = (
            jnp.broadcast_to(halo[s, pl.ds(start, SUBL), at][offset : offset + 1], (SUBL, LANES))
            for s in range(2)
        )
        downs = [low] + [pltpu.roll(v, 1, 0) for v in now]
        ups = [pltpu.roll(v, SUBL - 1, 0) for v in now] + [high]
        for t in range(tiles):
            v = now[t]
            xm = jnp.where(r_first, downs[t], downs[t + 1])
            xp = jnp.where(r_last, ups[t + 1], ups[t])
            turn = pltpu.roll(v, 1, 1)
            ym = jnp.where(l_first, left[t], turn)
            yp = jnp.where(l_last, nxt_turned[t], turned[t])
            left[t] = turn
            code = get(f, z, t, j)
            xs = jnp.where((code & 1) == 0, xm, xp)
            ys = jnp.where(code < 2, ym, yp)
            spread = (xm + xp) + (ym + yp) + (get(u, above, t, j) + get(u, below, t, j))
            out[t * SUBL : (t + 1) * SUBL, at] = (centre * v + KT * spread) + (sx * xs + sy * ys)
        now, turned = nxt, nxt_turned


def gather_floor_top(pv, e1, x2, x3, g):
    nx, ny = pv.shape
    width = x2.shape[1]
    column = place()[1]
    lanes_at = lambda other: pl.ds(pl.multiple_of(other * width, LANES), width)
    pv[:, lanes_at(column)] = g[0, pl.ds(pl.multiple_of(column * nx, SUBL), nx), :]
    for k, ref in ((1, e1.at[:, ny:]), (2, x2), (3, x3)):
        pv[:, lanes_at(column ^ k)] = ref[nx : 2 * nx, :]


def edge_kernel(
    u, f, mine1, mine2, urows, frows, x2, x3, e1, e2, g, g_new, own, rates, ox2, ox3, o1, o2, pv, plane, halo
):
    zt, nx, ny = u.shape
    group, column, odd, _ = place()
    gather_floor_top(pv, e1, x2, x3, g)
    fill_halo(halo, e1, e2)
    tin_layer(u, f, halo, rates, 0, 0, plane)
    plane[...] = plane[...] + HT * pv[...]
    put_parts(o1.at[:, ny:], ox2, ox3, own, plane, g_new.at[0], column, odd)
    rows, lanes = iotas()
    r_first, r_last = rows == 0, rows == SUBL - 1
    l_first, l_last = lanes == 0, lanes == LANES - 1
    wide, blocks = ny // LANES, zt // SUBL
    zero = jnp.zeros((SUBL, LANES), F32)

    def block(b, _):
        start = pl.multiple_of(b * SUBL, SUBL)
        here = pl.ds(start, SUBL)
        before = pl.ds(pl.multiple_of(jnp.maximum(start - SUBL, 0), SUBL), SUBL)
        after = pl.ds(pl.multiple_of(jnp.minimum(start + SUBL, zt - SUBL), SUBL), SUBL)
        bottom, top = b == 0, b == blocks - 1
        sx, sy = rates[0, here, :], rates[1, here, :]
        contact = jnp.where(r_first & bottom, HT, 0.0)
        centre = 1.0 - 6.0 * KT - sx - sy - contact
        outs = []
        def own_row(s, rows_, at):
            one, two = mine1[rows_, at], mine2[rows_, at]
            return jnp.where(odd, two, one) if s else jnp.where(odd, one, two)

        for s, side in ((0, 0), (1, nx - 1)):
            vs = [own_row(s, here, slice(j * LANES, (j + 1) * LANES)) for j in range(wide)]
            east = [pltpu.roll(v, LANES - 1, 1) for v in vs] + [zero]
            west = [zero] + [pltpu.roll(v, 1, 1) for v in vs]
            for j in range(wide):
                at = slice(j * LANES, (j + 1) * LANES)
                v, code, inside, outside = vs[j], frows[s, here, at], urows[s, here, at], halo[s, here, at]
                xm, xp = (inside, outside) if s else (outside, inside)
                ym = jnp.where(l_first, west[j], west[j + 1])
                yp = jnp.where(l_last, east[j + 1], east[j])
                above, below = own_row(s, after, at), own_row(s, before, at)
                above = jnp.where(top, pltpu.roll(v, 1, 0), above)
                below = jnp.where(bottom, pltpu.roll(v, SUBL - 1, 0), below)
                above = jnp.where(r_last, pltpu.roll(above, SUBL - 1, 0), pltpu.roll(v, SUBL - 1, 0))
                below = jnp.where(r_first, pltpu.roll(below, 1, 0), pltpu.roll(v, 1, 0))
                xs = jnp.where((code & 1) == 0, xm, xp)
                ys = jnp.where(code < 2, ym, yp)
                spread = (xm + xp) + (ym + yp) + (above + below)
                new = (centre * v + KT * spread) + (sx * xs + sy * ys)
                new = new + contact * jnp.broadcast_to(pv[side : side + 1, at], (SUBL, LANES))
                outs.append(new)
        for j in range(wide):
            at = slice(j * LANES, (j + 1) * LANES)
            low, high = outs[j], outs[wide + j]
            o1[here, at] = jnp.where(odd, low, high)
            o2[here, at] = jnp.where(odd, high, low)
        return 0

    lax.fori_loop(0, blocks, block, 0)


def edge_sweep(u, f, mine1, mine2, urows, frows, x2, x3, e1, e2, g, g_new, own, rates):
    plane = pltpu.VMEM(u.shape[1:], F32)
    return pl.pallas_call(
        edge_kernel,
        out_shape=[shape(v.shape) for v in (x2, x3, e1, e2)],
        in_specs=[VMEM] * 14,
        out_specs=[VMEM] * 4,
        scratch_shapes=[plane, plane, pltpu.VMEM((2, *e2.shape), F32)],
        compiler_params=params(2),
        cost_estimate=cost(0, 4 << 20),
        name="edge",
    )(*in_vmem(u, f, mine1, mine2, urows, frows, x2, x3, e1, e2, g, g_new, own, rates))


def tin_kernel(final, u, f, x2, x3, e1, e2, g, rates, out, ov, pv, halo, sem):
    zt, nx, ny = u.shape
    step = SUBL
    gather_floor_top(pv, e1, x2, x3, g)
    fill_halo(halo, e1, e2)

    def store(c):
        at = pl.ds(c * step, step)
        return pltpu.make_async_copy(ov.at[at], out.at[at], sem.at[c])

    def chunk(c, _):
        start = pl.multiple_of(c * step, SUBL)
        for offset in range(step):
            tin_layer(u, f, halo, rates, start, offset, ov.at[start + offset])

        @pl.when(c == 0)
        def _():
            ov[0, :, :] = ov[0] + HT * pv[...]

        if final:
            store(c).start()
        return 0

    lax.fori_loop(0, zt // step, chunk, 0)
    return [store(c) for c in range(zt // step)] if final else []


def tin_scratch(dims):
    zt, nx, ny = dims
    return [
        pltpu.VMEM((nx, ny), F32),
        pltpu.VMEM((2, zt, ny), F32),
        pltpu.SemaphoreType.DMA((zt // SUBL,)),
    ]


def tin_first(u, f, x2, x3, e1, e2, g, rates):
    def kernel(u, f, x2, x3, e1, e2, g, rates, out, *scratch):
        tin_kernel(False, u, f, x2, x3, e1, e2, g, rates, out, out, *scratch)

    return pl.pallas_call(
        kernel,
        out_shape=shape(u.shape),
        in_specs=[VMEM] * 8,
        out_specs=VMEM,
        scratch_shapes=tin_scratch(u.shape),
        compiler_params=params(2),
        cost_estimate=cost(0, 20 << 20),
        name="tin_first",
    )(*in_vmem(u, f, x2, x3, e1, e2, g, rates))


def last_sweep(u, f, x2, x3, x1, e2, g, rates, coefs, z1, z2, y1, y2, own, kc, kr):
    def kernel(
        u, f, x2, x3, x1, e2, g, ce, cw, cn, cz, z1, z2, y1, y2, own, kc, kr, rates,
        u_out, g_out, uv, gv, *scratch
    ):
        stores = tin_kernel(
            True, u, f, x2, x3, x1, e2, g, rates, u_out, uv, *scratch[:3]
        )
        stores += floor_kernel(
            False, g, ce, cw, cn, cz, u, x1, x2, x3, z1, z2, y1, y2, own, kc, kr, g_out, gv,
            *scratch[3:]
        )
        for copy in stores:
            copy.wait()

    return pl.pallas_call(
        kernel,
        out_shape=[far(u.shape), far(g.shape)],
        in_specs=[VMEM] * 19,
        out_specs=[ANY] * 2,
        scratch_shapes=[pltpu.VMEM(u.shape, F32), pltpu.VMEM(g.shape, F32)]
        + tin_scratch(u.shape)
        + floor_scratch(g.shape),
        compiler_params=params(10),
        cost_estimate=cost(0, 36 << 20),
        name="last_sweep",
    )(*in_vmem(u, f, x2, x3, x1, e2, g, *coefs, z1, z2, y1, y2, own, kc, kr, rates))


def local(tin_temp, flow_code, speeds, floor_temp, material, conductivity):
    u, f, g, m = tin_temp, flow_code, floor_temp[0], material[0]
    zt, nx, ny = u.shape
    nr, cx, width = g.shape
    e1, e2, x2, x3, z1, z2, own, gv, mv, rates, halves = pl.pallas_call(
        pack_kernel,
        out_shape=[
            shape((zt, ny + 2 * LANES)),
            shape((zt, ny)),
            shape((2 * nx, width)),
            shape((cx, 2 * LANES)),
            shape((2 * nr, width)),
            shape((2 * nr, width)),
            shape((2, cx, LANES)),
            shape(g.shape),
            shape(g.shape, jnp.int32),
            shape((2, zt, LANES)),
            shape((conductivity.shape[0], SUBL, LANES)),
        ],
        in_specs=[ANY] * 5,
        out_specs=[VMEM] * 11,
        scratch_shapes=[
            pltpu.VMEM((2, cx, LANES), jnp.int32),
            pltpu.VMEM((nx, ny), F32),
            pltpu.VMEM((2, nr, width), jnp.int32),
            pltpu.VMEM(speeds.shape, F32),
            pltpu.VMEM((1, conductivity.shape[0]), F32),
            pltpu.SemaphoreType.DMA((2 * nr // SUBL + 9,)),
        ],
        compiler_params=params(2),
        cost_estimate=cost(0, 12 << 20),
        name="pack",
    )(*in_hbm(u, floor_temp, material, speeds, conductivity[None]))
    mine1, mine2 = e1, e2
    e1, e2 = swap(e1, "e1"), swap(e2, "e2")
    e1, x3 = lax.optimization_barrier((e1, x3))
    x2, x3 = swap(x2, "x2"), swap(x3, "x3")
    y1, y2 = swap(z1, "z1"), swap(z2, "z2")
    *coefs, urows, frows = pl.pallas_call(
        coefficients_kernel,
        out_shape=[shape(g.shape)] * 4
        + [shape((2, zt, ny)), shape((2, zt, ny), jnp.int32)],
        in_specs=[VMEM, VMEM, ANY, ANY],
        out_specs=[VMEM] * 6,
        scratch_shapes=[pltpu.VMEM(g.shape, F32), pltpu.SemaphoreType.DMA((4,))],
        compiler_params=params(6),
        cost_estimate=cost(0, 16 << 20),
        name="coefficients",
    )(*in_vmem(mv, halves), *in_hbm(u, f))
    g1, own1, z1, z2, kc, kr = floor_first(
        gv, coefs, u, e1, x2, x3, z1, z2, y1, y2, own, halves
    )
    w2, w3, w1, d2 = edge_sweep(
        u, f, mine1, mine2, urows, frows, x2, x3, e1, e2, gv, g1, own1, rates
    )
    w1, d2 = swap(w1, "e1"), swap(d2, "e2")
    w1, w3 = lax.optimization_barrier((w1, w3))
    w2, w3 = swap(w2, "x2"), swap(w3, "x3")
    y1, y2 = swap(z1, "z1"), swap(z2, "z2")
    u1 = tin_first(u, f, x2, x3, e1, e2, gv, rates)
    u2, g2 = last_sweep(
        u1, f, w2, w3, w1, d2, g1, rates, coefs, z1, z2, y1, y2, own1, kc, kr
    )
    return u2, g2[None]


def solution(mesh):
    placed = (
        P(None, ("grp", "len"), None),
        P(None, ("grp", "len"), None),
        P(),
        P(("grp", "len"), None, None, None),
        P(("grp", "len"), None, None, None),
        P(),
    )
    return jax.shard_map(
        local,
        mesh=mesh,
        in_specs=placed,
        out_specs=(P(None, ("grp", "len"), None), P(("grp", "len"), None, None, None)),
        check_vma=False,
    )
```

```python
import functools

import jax
import jax.numpy as jnp
from jax import lax
from jax.experimental import pallas as pl
from jax.experimental.pallas import tpu as pltpu
from jax.sharding import PartitionSpec as P

TILE_Y = 4
KT = 0.1
HT = 0.2
HR = 0.2
LANES = 128
SUBL = 8
F32 = jnp.float32
ANY = pl.BlockSpec(memory_space=pl.ANY)
VMEM = pl.BlockSpec(memory_space=pltpu.VMEM)


def params(mib):
    return pltpu.CompilerParams(vmem_limit_bytes=mib * 1024 * 1024)


def shape(dims, dtype=F32):
    return pltpu.VMEM(dims, dtype)


def far(dims, dtype=F32):
    return pltpu.HBM(dims, dtype)


def in_hbm(*arrays):
    return [pltpu.with_memory_space_constraint(a, pltpu.HBM) for a in arrays]


def in_vmem(*arrays):
    return [pltpu.with_memory_space_constraint(a, pltpu.VMEM) for a in arrays]


def cost(flops, nbytes):
    return pl.CostEstimate(flops=flops, bytes_accessed=nbytes, transcendentals=0)


def place():
    pos = lax.axis_index("len")
    group, column = pos // TILE_Y, pos % TILE_Y
    return group, column, pos % 2 == 1, group % 2 == 1


def iotas():
    rows = lax.broadcasted_iota(jnp.int32, (SUBL, LANES), 0)
    lanes = lax.broadcasted_iota(jnp.int32, (SUBL, LANES), 1)
    return rows, lanes


def partner(kind, pos):
    return {
        "e1": lambda: pos ^ 1,
        "e2": lambda: pos + 1 if pos % 2 else pos - 1,
        "x2": lambda: pos ^ 2,
        "x3": lambda: pos ^ 3,
        "z1": lambda: pos ^ TILE_Y,
        "z2": lambda: pos + TILE_Y if (pos // TILE_Y) % 2 else pos - TILE_Y,
    }[kind]()


def swap(value, kind):
    count, parts = lax.axis_size("len"), lax.axis_size("grp")
    pairs = []
    for part in range(parts):
        for pos in range(count):
            to, other = part, partner(kind, pos)
            if not 0 <= other < count:
                to, other = (part ^ 1, pos) if kind == "e2" else (part, pos ^ 1)
            if 0 <= to < parts:
                pairs.append((part * count + pos, to * count + other))
    return lax.ppermute(value, ("grp", "len"), pairs)


def select_copy(cond, first, second, sem):
    @pl.when(cond)
    def _():
        pltpu.make_async_copy(*first, sem).start()

    @pl.when(jnp.logical_not(cond))
    def _():
        pltpu.make_async_copy(*second, sem).start()


def half_coded(codes, halves):
    value = jnp.zeros(codes.shape, F32)
    for i in range(halves.shape[0]):
        value = jnp.where(codes == i + 1.0, halves[i, 0:1, 0:1], value)
    return value


def wait_bytes(src, dst, sem):
    pltpu.make_async_copy(src, dst, sem).wait()


def put_columns(aux, cols):
    half = cols.shape[0] // 2
    aux[half:, :LANES] = cols[:half]
    aux[half:, LANES:] = cols[half:]


def get_columns(aux):
    half = aux.shape[0] // 2
    return jnp.concatenate([aux[half:, :LANES], aux[half:, LANES:]], 0)


def put_planes(dst, b_plane, p_plane, other):
    nx, width = b_plane.shape[0], p_plane.shape[1]
    lane = pl.multiple_of(other * width, LANES)
    row = pl.multiple_of(other * nx, SUBL)
    dst[:nx, :] = b_plane[:, pl.ds(lane, width)]
    dst[nx : 2 * nx, :] = p_plane[pl.ds(row, nx), :]


def keep_columns(own, slots, start, step, rs, edges):
    lanes = lax.broadcasted_iota(jnp.int32, (SUBL, LANES), 1)
    left, right = own[0, rs, :], own[1, rs, :]
    for offset in range(step):
        z = start + offset + slots
        first, last = edges(offset)
        both = pltpu.roll(jnp.where(lanes == 0, first, last), z, 1)
        left = jnp.where(lanes == z, both, left)
        right = jnp.where(lanes == lax.rem(z + LANES - 1, LANES), both, right)
    own[0, rs, :] = left
    own[1, rs, :] = right


def put_parts(e1_aux, x2, x3, own, b_plane, p_plane, column, odd):
    nx = b_plane.shape[0]
    left, right = own[0], own[1]
    put_columns(e1_aux, jnp.where(odd, left, right))
    put_planes(e1_aux, b_plane, p_plane, column ^ 1)
    put_planes(x2, b_plane, p_plane, column ^ 2)
    inner = (column > 0) & (column < TILE_Y - 1)
    put_columns(x3, jnp.where(inner, jnp.where(odd, right, left), 0.0))
    put_planes(x3, b_plane, p_plane, column ^ 3)


def pack_kernel(
    u, floor, ids, speeds, cond, e1, e2, x2, x3, z1, z2, own, gv, mv, rates, halves,
    own_m, b_plane, mrow, speeds_v, cond_v, sem
):
    g, m = floor.at[0], ids.at[0]
    group, column, odd, godd = place()
    nx, ny = u.shape[1], u.shape[2]
    nr, cx, width = g.shape
    step = SUBL
    chunks = nr // step
    shift = LANES // 2

    def load(c):
        at = pl.ds(c * step, step)
        return (
            pltpu.make_async_copy(g.at[at], gv.at[at], sem.at[2 * c]),
            pltpu.make_async_copy(m.at[at], mv.at[at], sem.at[2 * c + 1]),
        )

    base = 2 * chunks
    for copy in load(0):
        copy.start()
    plane = pltpu.make_async_copy(u.at[0], b_plane, sem.at[base])
    plane.start()
    low, high = g.at[:, 0, :], g.at[:, cx - 1, :]
    mrows = [
        pltpu.make_async_copy(m.at[:, r, :], mrow.at[s], sem.at[base + 1 + s])
        for r, s in ((0, 0), (cx - 1, 1))
    ]
    for copy in mrows + [copy for c in range(1, chunks) for copy in load(c)]:
        copy.start()
    select_copy(godd, (low, z1.at[:nr]), (high, z1.at[:nr]), sem.at[base + 3])
    select_copy(godd, (high, z2.at[:nr]), (low, z2.at[:nr]), sem.at[base + 4])
    small = (
        pltpu.make_async_copy(speeds, speeds_v, sem.at[base + 7]),
        pltpu.make_async_copy(cond, cond_v, sem.at[base + 8]),
    )
    for copy in small:
        copy.start()
    rows_out = e1.at[:, :ny]
    select_copy(odd, (u.at[:, nx - 1, :], e2), (u.at[:, 0, :], e2), sem.at[base + 5])
    select_copy(odd, (u.at[:, 0, :], rows_out), (u.at[:, nx - 1, :], rows_out), sem.at[base + 6])
    own[...] = jnp.zeros_like(own)
    own_m[...] = jnp.zeros_like(own_m)

    def chunk(c, _):
        for copy in load(c):
            copy.wait()
        start = c * step
        for t in range(cx // SUBL):
            rs = slice(t * SUBL, (t + 1) * SUBL)

            def edges(ref):
                return lambda offset: (
                    ref[start + offset, rs, :LANES],
                    ref[start + offset, rs, width - LANES :],
                )

            keep_columns(own, 0, start, step, rs, edges(gv))
            keep_columns(own_m, shift, start, step, rs, edges(mv))
        return 0

    lax.fori_loop(0, chunks, chunk, 0)
    is_k = lax.broadcasted_iota(jnp.int32, (cx, LANES), 1) >= shift
    for s in range(2):
        codes = pltpu.roll(own_m[s], s, 1)
        own[s, :, :] = jnp.where(is_k, codes.astype(F32) + 1.0, pltpu.roll(own[s], s, 1))
    plane.wait()
    put_parts(e1.at[:, ny:], x2, x3, own, b_plane, gv.at[0], column, odd)
    for copy in mrows:
        copy.wait()
    m_low, m_high = mrow[0].astype(F32) + 1.0, mrow[1].astype(F32) + 1.0
    z1[nr:, :] = jnp.where(godd, m_low, m_high)
    z2[nr:, :] = jnp.where(godd, m_high, m_low)
    for copy in small:
        copy.wait()
    zt = u.shape[0]
    diagonal = lax.broadcasted_iota(jnp.int32, (zt, zt), 0) == lax.broadcasted_iota(
        jnp.int32, (zt, zt), 1
    )
    for s in range(2):
        spread = jnp.where(diagonal, jnp.broadcast_to(speeds_v[s : s + 1, :], (zt, zt)), 0.0)
        along = jnp.sum(spread, axis=1, keepdims=True)
        rates[s, :, :] = jnp.broadcast_to(along, (zt, LANES))
    for i in range(halves.shape[0]):
        halves[i, :, :] = jnp.broadcast_to(0.5 * cond_v[0:1, i : i + 1], (SUBL, LANES))
    wait_bytes(low, z1.at[:nr], sem.at[base + 3])
    wait_bytes(low, z2.at[:nr], sem.at[base + 4])
    wait_bytes(u.at[:, 0, :], e2, sem.at[base + 5])
    wait_bytes(u.at[:, 0, :], rows_out, sem.at[base + 6])


def inner_kernel(m, g, halves, u, f, out, ce, cw, cn, cz, urows, frows, kv, fzv, sem):
    nr, cx, width = m.shape
    nx = u.shape[1]
    picks = [(u.at[:, r, :], urows.at[i]) for i, r in enumerate((1, nx - 2))]
    picks += [(f.at[:, r, :], frows.at[i]) for i, r in enumerate((0, nx - 1))]
    picks = [pltpu.make_async_copy(a, b, sem.at[i]) for i, (a, b) in enumerate(picks)]
    for copy in picks:
        copy.start()
    rows, lanes = iotas()
    r_first, r_last = rows == 0, rows == SUBL - 1
    l_first, l_last = lanes == 0, lanes == LANES - 1
    tiles, wide = cx // SUBL, width // LANES
    spans = [slice(j * LANES, (j + 1) * LANES) for j in range(wide)]
    step = SUBL
    values = [halves[i] for i in range(halves.shape[0])]
    zero = jnp.zeros((SUBL, LANES), F32)

    def lookup(ids):
        value = values[0]
        for i in range(1, len(values)):
            value = jnp.where(ids == i, values[i], value)
        return value

    for t in range(tiles):
        rs = slice(t * SUBL, (t + 1) * SUBL)
        for at in spans:
            kv[0, rs, at] = lookup(m[0, rs, at])
    fzv[...] = jnp.zeros_like(fzv)
    turn = lambda vs, by, axis: [pltpu.roll(v, by, axis) for v in vs]

    def layer(start, offset):
        z = start + offset
        above, here, there = z + 1, offset % 2, (offset + 1) % 2
        last = offset == step - 1
        if last:
            above = jnp.minimum(above, nr - 1)
            scale = jnp.where(z + 1 < nr, 1.0, 0.0)

        def tile(t):
            rs = slice(t * SUBL, (t + 1) * SUBL)
            gs = [g[z, rs, at] for at in spans]
            ks = [kv[here, rs, at] for at in spans]
            return gs, ks, turn(gs, SUBL - 1, 0), turn(ks, SUBL - 1, 0)

        now = tile(0)
        prev = [zero] * wide
        for t in range(tiles):
            rs = slice(t * SUBL, (t + 1) * SUBL)
            gs, ks, g_up, k_up = now
            if t + 1 < tiles:
                now = tile(t + 1)
            ge, gw = turn(gs, LANES - 1, 1), turn(gs, 1, 1)
            ke, kw = turn(ks, LANES - 1, 1), turn(ks, 1, 1)
            for j, at in enumerate(spans):
                v, k = gs[j], ks[j]
                k_next, v_next = lookup(m[above, rs, at]), g[above, rs, at]
                if last:
                    k_next, v_next = scale * k_next, scale * v_next
                kv[there, rs, at] = k_next
                below = k + k_next
                if t + 1 < tiles:
                    north = k + jnp.where(r_last, now[3][j], k_up[j])
                    xp = jnp.where(r_last, now[2][j], g_up[j])
                else:
                    north, xp = jnp.where(r_last, 0.0, k + k_up[j]), g_up[j]
                if j + 1 < wide:
                    east = k + jnp.where(l_last, ke[j + 1], ke[j])
                    yp = jnp.where(l_last, ge[j + 1], ge[j])
                else:
                    east, yp = jnp.where(l_last, 0.0, k + ke[j]), ge[j]
                if j > 0:
                    west = k + jnp.where(l_first, kw[j - 1], kw[j])
                    ym = jnp.where(l_first, gw[j - 1], gw[j])
                else:
                    west, ym = jnp.where(l_first, 0.0, k + kw[j]), gw[j]
                ce[z, rs, at], cw[z, rs, at] = east, west
                cn[z, rs, at], cz[z, rs, at] = north, below
                fx = north * (xp - v)
                turned = pltpu.roll(fx, 1, 0)
                fxm = jnp.where(r_first, prev[j], turned)
                prev[j] = turned
                fz = below * (v_next - v)
                side = east * (yp - v) + west * (ym - v)
                out[z, rs, at] = v + ((fx - fxm) + side + (fz - fzv[rs, at]))
                fzv[rs, at] = fz

    def chunk(c, _):
        start = pl.multiple_of(c * step, SUBL)
        for offset in range(step):
            layer(start, offset)
        return 0

    lax.fori_loop(0, nr // step, chunk, 0)
    for copy in picks:
        copy.wait()


def floor_sides(halves, u, x1, x2, x3, z1, z2, y1, y2, own, kc, kr, tcol, trow, bv):
    nr = kr.shape[1]
    nx, ny = u.shape[1], u.shape[2]
    width = bv.shape[1]
    group, column, odd, godd = place()
    shift = LANES // 2
    aux = x1.at[:, ny:]
    groups = lax.axis_size("len") // TILE_Y
    known = (group ^ 1) < groups, jnp.where(godd, group + 1 < groups, group > 0)
    one, three = get_columns(aux), get_columns(x3)
    for s, halo in ((0, jnp.where(odd, one, three)), (1, jnp.where(odd, three, one))):
        if halves is not None:
            both = half_coded(own[s], halves) + half_coded(halo, halves)
            kc[s, :, :] = pltpu.roll(both, shift, 1)
        tcol[s, :, :] = kc[s] * (halo - own[s])
    for s, (mine, halo) in enumerate(((z1, y1), (z2, y2))):
        halo = jnp.where(known[s], halo[...], 0.0)
        if halves is not None:
            kr[s, :, :] = half_coded(mine[nr:, :], halves) + half_coded(halo[nr:, :], halves)
        side = kr[s] * (halo[:nr, :] - mine[:nr, :])
        trow[jnp.where(godd, s, 1 - s), :, :] = side
    row = lambda other: pl.ds(pl.multiple_of(other * nx, SUBL), nx)
    bv[row(column), :] = u[0, :, pl.ds(pl.multiple_of(column * width, LANES), width)]
    for k, ref in ((1, aux), (2, x2), (3, x3)):
        bv[row(column ^ k), :] = ref[:nx, :]


def floor_kernel(
    g, ce, cw, cn, cz, u, x1, x2, x3, z1, z2, y1, y2, own, kc, kr, out, ov, fzv, tcol, trow, bv, sem
):
    nr, cx, width = g.shape
    tiles, wide = cx // SUBL, width // LANES
    step = SUBL
    chunks = nr // step
    floor_sides(None, u, x1, x2, x3, z1, z2, y1, y2, own, kc, kr, tcol, trow, bv)
    rows, lanes = iotas()
    r_first, r_last = rows == 0, rows == SUBL - 1
    l_first, l_last = lanes == 0, lanes == LANES - 1
    fzv[...] = jnp.zeros_like(fzv)
    spans = [slice(j * LANES, (j + 1) * LANES) for j in range(wide)]

    def layer(start, offset):
        z = start + offset
        back = lax.rem(LANES - z, LANES)
        above = z + 1
        if offset == step - 1:
            above = jnp.minimum(above, nr - 1)
            scale = jnp.where(z + 1 < nr, 1.0, 0.0)

        def tile(t):
            rs = slice(t * SUBL, (t + 1) * SUBL)
            gs = [g[z, rs, at] for at in spans]
            return gs, [pltpu.roll(v, SUBL - 1, 0) for v in gs]

        def row_of(s):
            block = trow[s, pl.ds(start, SUBL), :][offset : offset + 1]
            return [jnp.broadcast_to(block[:, at], (SUBL, LANES)) for at in spans]

        low, high = row_of(0), row_of(1)
        gs, ups = tile(0)
        prev = [-v for v in low]
        for t in range(tiles):
            rs = slice(t * SUBL, (t + 1) * SUBL)
            if t + 1 < tiles:
                gn, un = tile(t + 1)
            east = [pltpu.roll(v, LANES - 1, 1) for v in gs]
            west = [pltpu.roll(v, 1, 1) for v in gs]
            t_west = pltpu.roll(tcol[0, rs, :], back, 1)
            t_east = pltpu.roll(tcol[1, rs, :], LANES - 1 - z, 1)
            for j, at in enumerate(spans):
                v = gs[j]
                if t + 1 < tiles:
                    fx = cn[z, rs, at] * (jnp.where(r_last, un[j], ups[j]) - v)
                else:
                    fx = jnp.where(r_last, high[j], cn[z, rs, at] * (ups[j] - v))
                turned = pltpu.roll(fx, 1, 0)
                fxm = jnp.where(r_first, prev[j], turned)
                prev[j] = turned
                yp = jnp.where(l_last, east[j + 1], east[j]) if j + 1 < wide else east[j]
                ym = jnp.where(l_first, west[j - 1], west[j]) if j > 0 else west[j]
                side = ce[z, rs, at] * (yp - v) + cw[z, rs, at] * (ym - v)
                if j == 0:
                    side = side + jnp.where(l_first, t_west, 0.0)
                if j + 1 == wide:
                    side = side + jnp.where(l_last, t_east, 0.0)
                nxt = g[above, rs, at]
                if offset == step - 1:
                    nxt = scale * nxt
                fz = cz[z, rs, at] * (nxt - v)
                total = v + ((fx - fxm) + side + (fz - fzv[rs, at]))
                fzv[rs, at] = fz
                ov[z, rs, at] = total
            if t + 1 < tiles:
                gs, ups = gn, un

    def store(c):
        at = pl.ds(c * step, step)
        return pltpu.make_async_copy(ov.at[at], out.at[at], sem.at[c])

    def chunk(c, _):
        start = pl.multiple_of(c * step, SUBL)
        for offset in range(step):
            layer(start, offset)

        @pl.when(c == 0)
        def _():
            ov[0, :, :] = ov[0] + HR * (bv[...] - g[0])

        store(c).start()
        return 0

    lax.fori_loop(0, chunks, chunk, 0)
    return [store(c) for c in range(chunks)]


def floor_scratch(dims):
    nr, cx, width = dims
    return [
        pltpu.VMEM((cx, width), F32),
        pltpu.VMEM((2, cx, LANES), F32),
        pltpu.VMEM((2, nr, width), F32),
        pltpu.VMEM((cx, width), F32),
        pltpu.SemaphoreType.DMA((3 * nr // SUBL,)),
    ]


def floor_finish(part, g, tcol, trow, bv, out, own, o1, o2, sem):
    nr, cx, width = g.shape
    godd = place()[3]
    rows, lanes = iotas()
    r_first, r_last = rows == 0, rows == SUBL - 1
    l_first, l_last = lanes == 0, lanes == LANES - 1
    tiles, wide = cx // SUBL, width // LANES
    spans = [slice(j * LANES, (j + 1) * LANES) for j in range(wide)]
    step = SUBL
    chunks = nr // step
    own[...] = jnp.zeros_like(own)

    def rows_of(c):
        at = pl.ds(pl.multiple_of(c * step, SUBL), step)
        low, high = out.at[at, 0, :], out.at[at, cx - 1, :]
        return low, high, o1.at[at], o2.at[at]

    def chunk(c, _):
        start = pl.multiple_of(c * step, SUBL)

        for offset in range(step):
            z = start + offset
            back = lax.rem(LANES - z, LANES)
            for t in range(tiles):
                rs = slice(t * SUBL, (t + 1) * SUBL)
                for j, at in enumerate(spans):
                    v = part[z, rs, at]
                    if j == 0:
                        west = pltpu.roll(tcol[0, rs, :], back, 1)
                        v = v + jnp.where(l_first, west, 0.0)
                    if j + 1 == wide:
                        east = pltpu.roll(tcol[1, rs, :], LANES - 1 - z, 1)
                        v = v + jnp.where(l_last, east, 0.0)
                    for s, edge, mask in ((0, 0, r_first), (1, tiles - 1, r_last)):
                        if t == edge:
                            side = trow[s, pl.ds(start, SUBL), at][offset : offset + 1]
                            v = v + jnp.where(mask, jnp.broadcast_to(side, v.shape), 0.0)
                    out[z, rs, at] = v

        @pl.when(c == 0)
        def _():
            out[0, :, :] = out[0] + HR * (bv[...] - g[0])

        low, high, to1, to2 = rows_of(c)
        select_copy(godd, (low, to1), (high, to1), sem.at[c])
        select_copy(godd, (high, to2), (low, to2), sem.at[chunks + c])
        for t in range(tiles):
            rs = slice(t * SUBL, (t + 1) * SUBL)
            edges = lambda offset: (
                out[start + offset, rs, spans[0]],
                out[start + offset, rs, spans[-1]],
            )
            keep_columns(own, 0, start, step, rs, edges)
        return 0

    lax.fori_loop(0, chunks, chunk, 0)
    own[1, :, :] = pltpu.roll(own[1], 1, 1)
    copies = []
    for c in range(chunks):
        low, _, to1, to2 = rows_of(c)
        copies.append(pltpu.make_async_copy(low, to1, sem.at[c]))
        copies.append(pltpu.make_async_copy(low, to2, sem.at[chunks + c]))
    return copies


def fill_halo(halo, e1, e2):
    odd, pos, ny = place()[2], lax.axis_index("len"), halo.shape[2]
    alone = (pos == 0) | (pos == lax.axis_size("len") - 1)
    one, two = e1[:, :ny], jnp.where(alone, 0.0, e2[...])
    halo[0, :, :] = jnp.where(odd, one, two)
    halo[1, :, :] = jnp.where(odd, two, one)


def tin_layer(u, f, halo, rates, start, offset, out):
    zt, nx, ny = u.shape
    rows, lanes = iotas()
    r_first, r_last = rows == 0, rows == SUBL - 1
    l_first, l_last = lanes == 0, lanes == LANES - 1
    tiles, wide = nx // SUBL, ny // LANES
    zero = jnp.zeros((SUBL, LANES), F32)
    z = start + offset
    sx, sy = (
        jnp.broadcast_to(rates[s, pl.ds(start, SUBL), :][offset : offset + 1], (SUBL, LANES))
        for s in range(2)
    )
    centre = 1.0 - 6.0 * KT - sx - sy
    if offset == 0:
        centre = centre - jnp.where(z == 0, HT, 0.0)
    above, below = jnp.minimum(z + 1, zt - 1), jnp.maximum(z - 1, 0)

    def get(ref, z_, t, j):
        return ref[z_, t * SUBL : (t + 1) * SUBL, j * LANES : (j + 1) * LANES]

    left = [zero] * tiles
    now = [get(u, z, t, 0) for t in range(tiles)]
    turned = [pltpu.roll(v, LANES - 1, 1) for v in now]
    for j in range(wide):
        at = slice(j * LANES, (j + 1) * LANES)
        if j + 1 < wide:
            nxt = [get(u, z, t, j + 1) for t in range(tiles)]
            nxt_turned = [pltpu.roll(v, LANES - 1, 1) for v in nxt]
        else:
            nxt, nxt_turned = None, [zero] * tiles
        low, high = (
            jnp.broadcast_to(halo[s, pl.ds(start, SUBL), at][offset : offset + 1], (SUBL, LANES))
            for s in range(2)
        )
        downs = [low] + [pltpu.roll(v, 1, 0) for v in now]
        ups = [pltpu.roll(v, SUBL - 1, 0) for v in now] + [high]
        for t in range(tiles):
            v = now[t]
            xm = jnp.where(r_first, downs[t], downs[t + 1])
            xp = jnp.where(r_last, ups[t + 1], ups[t])
            turn = pltpu.roll(v, 1, 1)
            ym = jnp.where(l_first, left[t], turn)
            yp = jnp.where(l_last, nxt_turned[t], turned[t])
            left[t] = turn
            code = get(f, z, t, j)
            xs = jnp.where((code & 1) == 0, xm, xp)
            ys = jnp.where(code < 2, ym, yp)
            spread = (xm + xp) + (ym + yp) + (get(u, above, t, j) + get(u, below, t, j))
            out[t * SUBL : (t + 1) * SUBL, at] = (centre * v + KT * spread) + (sx * xs + sy * ys)
        now, turned = nxt, nxt_turned


def gather_floor_top(pv, e1, x2, x3, g):
    nx, ny = pv.shape
    width = x2.shape[1]
    column = place()[1]
    lanes_at = lambda other: pl.ds(pl.multiple_of(other * width, LANES), width)
    pv[:, lanes_at(column)] = g[0, pl.ds(pl.multiple_of(column * nx, SUBL), nx), :]
    for k, ref in ((1, e1.at[:, ny:]), (2, x2), (3, x3)):
        pv[:, lanes_at(column ^ k)] = ref[nx : 2 * nx, :]


def edge_kernel(
    u, f, mine1, mine2, urows, frows, x2, x3, e1, e2, g, part, z1, z2, y1, y2, own, halves, rates,
    ox2, ox3, o1, o2, g_new, own_new, oz1, oz2, kc, kr,
    pv, plane, halo, tcol, trow, bv, sem
):
    floor_sides(halves, u, e1, x2, x3, z1, z2, y1, y2, own, kc, kr, tcol, trow, bv)
    copies = floor_finish(part, g, tcol, trow, bv, g_new, own_new, oz1, oz2, sem)
    zt, nx, ny = u.shape
    group, column, odd, _ = place()
    gather_floor_top(pv, e1, x2, x3, g)
    fill_halo(halo, e1, e2)
    tin_layer(u, f, halo, rates, 0, 0, plane)
    plane[...] = plane[...] + HT * pv[...]
    put_parts(o1.at[:, ny:], ox2, ox3, own_new, plane, g_new.at[0], column, odd)
    rows, lanes = iotas()
    r_first, r_last = rows == 0, rows == SUBL - 1
    l_first, l_last = lanes == 0, lanes == LANES - 1
    wide, blocks = ny // LANES, zt // SUBL
    zero = jnp.zeros((SUBL, LANES), F32)

    def block(b, _):
        start = pl.multiple_of(b * SUBL, SUBL)
        here = pl.ds(start, SUBL)
        before = pl.ds(pl.multiple_of(jnp.maximum(start - SUBL, 0), SUBL), SUBL)
        after = pl.ds(pl.multiple_of(jnp.minimum(start + SUBL, zt - SUBL), SUBL), SUBL)
        bottom, top = b == 0, b == blocks - 1
        sx, sy = rates[0, here, :], rates[1, here, :]
        contact = jnp.where(r_first & bottom, HT, 0.0)
        centre = 1.0 - 6.0 * KT - sx - sy - contact
        outs = []
        def own_row(s, rows_, at):
            one, two = mine1[rows_, at], mine2[rows_, at]
            return jnp.where(odd, two, one) if s else jnp.where(odd, one, two)

        for s, side in ((0, 0), (1, nx - 1)):
            vs = [own_row(s, here, slice(j * LANES, (j + 1) * LANES)) for j in range(wide)]
            east = [pltpu.roll(v, LANES - 1, 1) for v in vs] + [zero]
            west = [zero] + [pltpu.roll(v, 1, 1) for v in vs]
            for j in range(wide):
                at = slice(j * LANES, (j + 1) * LANES)
                v, code, inside, outside = vs[j], frows[s, here, at], urows[s, here, at], halo[s, here, at]
                xm, xp = (inside, outside) if s else (outside, inside)
                ym = jnp.where(l_first, west[j], west[j + 1])
                yp = jnp.where(l_last, east[j + 1], east[j])
                above, below = own_row(s, after, at), own_row(s, before, at)
                above = jnp.where(top, pltpu.roll(v, 1, 0), above)
                below = jnp.where(bottom, pltpu.roll(v, SUBL - 1, 0), below)
                above = jnp.where(r_last, pltpu.roll(above, SUBL - 1, 0), pltpu.roll(v, SUBL - 1, 0))
                below = jnp.where(r_first, pltpu.roll(below, 1, 0), pltpu.roll(v, 1, 0))
                xs = jnp.where((code & 1) == 0, xm, xp)
                ys = jnp.where(code < 2, ym, yp)
                spread = (xm + xp) + (ym + yp) + (above + below)
                new = (centre * v + KT * spread) + (sx * xs + sy * ys)
                new = new + contact * jnp.broadcast_to(pv[side : side + 1, at], (SUBL, LANES))
                outs.append(new)
        for j in range(wide):
            at = slice(j * LANES, (j + 1) * LANES)
            low, high = outs[j], outs[wide + j]
            o1[here, at] = jnp.where(odd, low, high)
            o2[here, at] = jnp.where(odd, high, low)
        return 0

    lax.fori_loop(0, blocks, block, 0)
    for copy in copies:
        copy.wait()


def edge_sweep(
    u, f, mine1, mine2, urows, frows, x2, x3, e1, e2, g, part, z1, z2, y1, y2, own, halves, rates
):
    plane = pltpu.VMEM(u.shape[1:], F32)
    nr, cx, width = g.shape
    return pl.pallas_call(
        edge_kernel,
        out_shape=[shape(v.shape) for v in (x2, x3, e1, e2, g, own)]
        + [shape((nr, width))] * 2
        + [shape(own.shape), shape((2, nr, width))],
        in_specs=[VMEM] * 19,
        out_specs=[VMEM] * 10,
        scratch_shapes=[plane, plane, pltpu.VMEM((2, *e2.shape), F32), *floor_scratch(g.shape)[1:]],
        compiler_params=params(2),
        cost_estimate=cost(0, 10 << 20),
        name="edge",
    )(
        *in_vmem(
            u, f, mine1, mine2, urows, frows, x2, x3, e1, e2, g, part, z1, z2, y1, y2, own, halves, rates
        )
    )


def tin_kernel(final, u, f, x2, x3, e1, e2, g, rates, out, ov, pv, halo, sem):
    zt, nx, ny = u.shape
    step = SUBL
    gather_floor_top(pv, e1, x2, x3, g)
    fill_halo(halo, e1, e2)

    def store(c):
        at = pl.ds(c * step, step)
        return pltpu.make_async_copy(ov.at[at], out.at[at], sem.at[c])

    def chunk(c, _):
        start = pl.multiple_of(c * step, SUBL)
        for offset in range(step):
            tin_layer(u, f, halo, rates, start, offset, ov.at[start + offset])

        @pl.when(c == 0)
        def _():
            ov[0, :, :] = ov[0] + HT * pv[...]

        if final:
            store(c).start()
        return 0

    lax.fori_loop(0, zt // step, chunk, 0)
    return [store(c) for c in range(zt // step)] if final else []


def tin_scratch(dims):
    zt, nx, ny = dims
    return [
        pltpu.VMEM((nx, ny), F32),
        pltpu.VMEM((2, zt, ny), F32),
        pltpu.SemaphoreType.DMA((zt // SUBL,)),
    ]


def tin_first(u, f, x2, x3, e1, e2, g, rates):
    def kernel(u, f, x2, x3, e1, e2, g, rates, out, *scratch):
        tin_kernel(False, u, f, x2, x3, e1, e2, g, rates, out, out, *scratch)

    return pl.pallas_call(
        kernel,
        out_shape=shape(u.shape),
        in_specs=[VMEM] * 8,
        out_specs=VMEM,
        scratch_shapes=tin_scratch(u.shape),
        compiler_params=params(2),
        cost_estimate=cost(0, 20 << 20),
        name="tin_first",
    )(*in_vmem(u, f, x2, x3, e1, e2, g, rates))


def last_sweep(u, f, x2, x3, x1, e2, g, rates, coefs, z1, z2, y1, y2, own, kc, kr):
    def kernel(
        u, f, x2, x3, x1, e2, g, ce, cw, cn, cz, z1, z2, y1, y2, own, kc, kr, rates,
        u_out, g_out, uv, gv, *scratch
    ):
        stores = tin_kernel(
            True, u, f, x2, x3, x1, e2, g, rates, u_out, uv, *scratch[:3]
        )
        stores += floor_kernel(
            g, ce, cw, cn, cz, u, x1, x2, x3, z1, z2, y1, y2, own, kc, kr, g_out, gv,
            *scratch[3:]
        )
        for copy in stores:
            copy.wait()

    return pl.pallas_call(
        kernel,
        out_shape=[far(u.shape), far(g.shape)],
        in_specs=[VMEM] * 19,
        out_specs=[ANY] * 2,
        scratch_shapes=[pltpu.VMEM(u.shape, F32), pltpu.VMEM(g.shape, F32)]
        + tin_scratch(u.shape)
        + floor_scratch(g.shape),
        compiler_params=params(10),
        cost_estimate=cost(0, 36 << 20),
        name="last_sweep",
    )(*in_vmem(u, f, x2, x3, x1, e2, g, *coefs, z1, z2, y1, y2, own, kc, kr, rates))


def local(tin_temp, flow_code, speeds, floor_temp, material, conductivity):
    u, f, g, m = tin_temp, flow_code, floor_temp[0], material[0]
    zt, nx, ny = u.shape
    nr, cx, width = g.shape
    e1, e2, x2, x3, z1, z2, own, gv, mv, rates, halves = pl.pallas_call(
        pack_kernel,
        out_shape=[
            shape((zt, ny + 2 * LANES)),
            shape((zt, ny)),
            shape((2 * nx, width)),
            shape((cx, 2 * LANES)),
            shape((2 * nr, width)),
            shape((2 * nr, width)),
            shape((2, cx, LANES)),
            shape(g.shape),
            shape(g.shape, jnp.int32),
            shape((2, zt, LANES)),
            shape((conductivity.shape[0], SUBL, LANES)),
        ],
        in_specs=[ANY] * 5,
        out_specs=[VMEM] * 11,
        scratch_shapes=[
            pltpu.VMEM((2, cx, LANES), jnp.int32),
            pltpu.VMEM((nx, ny), F32),
            pltpu.VMEM((2, nr, width), jnp.int32),
            pltpu.VMEM(speeds.shape, F32),
            pltpu.VMEM((1, conductivity.shape[0]), F32),
            pltpu.SemaphoreType.DMA((2 * nr // SUBL + 9,)),
        ],
        compiler_params=params(2),
        cost_estimate=cost(0, 12 << 20),
        name="pack",
    )(*in_hbm(u, floor_temp, material, speeds, conductivity[None]))
    mine1, mine2 = e1, e2
    e1, e2 = swap(e1, "e1"), swap(e2, "e2")
    e1, x3 = lax.optimization_barrier((e1, x3))
    x2, x3 = swap(x2, "x2"), swap(x3, "x3")
    y1, y2 = swap(z1, "z1"), swap(z2, "z2")
    part, *coefs, urows, frows = pl.pallas_call(
        inner_kernel,
        out_shape=[shape(g.shape)] * 5
        + [shape((2, zt, ny)), shape((2, zt, ny), jnp.int32)],
        in_specs=[VMEM] * 3 + [ANY] * 2,
        out_specs=[VMEM] * 7,
        scratch_shapes=[
            pltpu.VMEM((2, cx, width), F32),
            pltpu.VMEM((cx, width), F32),
            pltpu.SemaphoreType.DMA((4,)),
        ],
        compiler_params=params(2),
        cost_estimate=cost(0, 24 << 20),
        name="inner",
    )(*in_vmem(mv, gv, halves), *in_hbm(u, f))
    w2, w3, w1, d2, g1, own1, z1, z2, kc, kr = edge_sweep(
        u, f, mine1, mine2, urows, frows, x2, x3, e1, e2, gv, part, z1, z2, y1, y2, own, halves, rates
    )
    w1, d2 = swap(w1, "e1"), swap(d2, "e2")
    w1, w3 = lax.optimization_barrier((w1, w3))
    w2, w3 = swap(w2, "x2"), swap(w3, "x3")
    y1, y2 = swap(z1, "z1"), swap(z2, "z2")
    u1 = tin_first(u, f, x2, x3, e1, e2, gv, rates)
    u2, g2 = last_sweep(
        u1, f, w2, w3, w1, d2, g1, rates, coefs, z1, z2, y1, y2, own1, kc, kr
    )
    return u2, g2[None]


def solution(mesh):
    placed = (
        P(None, ("grp", "len"), None),
        P(None, ("grp", "len"), None),
        P(),
        P(("grp", "len"), None, None, None),
        P(("grp", "len"), None, None, None),
        P(),
    )
    return jax.shard_map(
        local,
        mesh=mesh,
        in_specs=placed,
        out_specs=(P(None, ("grp", "len"), None), P(("grp", "len"), None, None, None)),
        check_vma=False,
    )
```

```python
import functools

import jax
import jax.numpy as jnp
from jax import lax
from jax.experimental import pallas as pl
from jax.experimental.pallas import tpu as pltpu
from jax.sharding import PartitionSpec as P

TILE_Y = 4
KT = 0.1
HT = 0.2
HR = 0.2
LANES = 128
SUBL = 8
F32 = jnp.float32
ANY = pl.BlockSpec(memory_space=pl.ANY)
VMEM = pl.BlockSpec(memory_space=pltpu.VMEM)


def params(mib):
    return pltpu.CompilerParams(vmem_limit_bytes=mib * 1024 * 1024)


def shape(dims, dtype=F32):
    return pltpu.VMEM(dims, dtype)


def far(dims, dtype=F32):
    return pltpu.HBM(dims, dtype)


def in_hbm(*arrays):
    return [pltpu.with_memory_space_constraint(a, pltpu.HBM) for a in arrays]


def in_vmem(*arrays):
    return [pltpu.with_memory_space_constraint(a, pltpu.VMEM) for a in arrays]


def cost(flops, nbytes):
    return pl.CostEstimate(flops=flops, bytes_accessed=nbytes, transcendentals=0)


def place():
    pos = lax.axis_index("len")
    group, column = pos // TILE_Y, pos % TILE_Y
    return group, column, pos % 2 == 1, group % 2 == 1


def alone():
    pos = lax.axis_index("len")
    return (pos == 0) | (pos == lax.axis_size("len") - 1)


def iotas():
    rows = lax.broadcasted_iota(jnp.int32, (SUBL, LANES), 0)
    lanes = lax.broadcasted_iota(jnp.int32, (SUBL, LANES), 1)
    return rows, lanes


def partner(kind, pos):
    return {
        "e1": lambda: pos ^ 1,
        "e2": lambda: pos + 1 if pos % 2 else pos - 1,
        "x2": lambda: pos ^ 2,
        "x3": lambda: pos ^ 3,
        "z1": lambda: pos ^ TILE_Y,
        "z2": lambda: pos + TILE_Y if (pos // TILE_Y) % 2 else pos - TILE_Y,
    }[kind]()


def swap(value, kind):
    count, parts = lax.axis_size("len"), lax.axis_size("grp")
    pairs = []
    for part in range(parts):
        for pos in range(count):
            to, other = part, partner(kind, pos)
            if not 0 <= other < count:
                to, other = (part ^ 1, pos) if kind == "e2" else (part, pos ^ 1)
            if 0 <= to < parts:
                pairs.append((part * count + pos, to * count + other))
    return lax.ppermute(value, ("grp", "len"), pairs)


def select_copy(cond, first, second, sem):
    @pl.when(cond)
    def _():
        pltpu.make_async_copy(*first, sem).start()

    @pl.when(jnp.logical_not(cond))
    def _():
        pltpu.make_async_copy(*second, sem).start()


def half_coded(codes, halves):
    value = jnp.zeros(codes.shape, F32)
    for i in range(halves.shape[0]):
        value = jnp.where(codes == i + 1.0, halves[i, 0:1, 0:1], value)
    return value


def wait_bytes(src, dst, sem):
    pltpu.make_async_copy(src, dst, sem).wait()


def put_columns(aux, cols):
    half = cols.shape[0] // 2
    aux[half:, :LANES] = cols[:half]
    aux[half:, LANES:] = cols[half:]


def get_columns(aux):
    half = aux.shape[0] // 2
    return jnp.concatenate([aux[half:, :LANES], aux[half:, LANES:]], 0)


def put_planes(dst, b_plane, p_plane, other):
    nx, width = b_plane.shape[0], p_plane.shape[1]
    lane = pl.multiple_of(other * width, LANES)
    row = pl.multiple_of(other * nx, SUBL)
    dst[:nx, :] = b_plane[:, pl.ds(lane, width)]
    dst[nx : 2 * nx, :] = p_plane[pl.ds(row, nx), :]


def keep_columns(own, slots, start, step, rs, edges):
    lanes = lax.broadcasted_iota(jnp.int32, (SUBL, LANES), 1)
    left, right = own[0, rs, :], own[1, rs, :]
    for offset in range(step):
        z = start + offset + slots
        first, last = edges(offset)
        both = pltpu.roll(jnp.where(lanes == 0, first, last), z, 1)
        left = jnp.where(lanes == z, both, left)
        right = jnp.where(lanes == lax.rem(z + LANES - 1, LANES), both, right)
    own[0, rs, :] = left
    own[1, rs, :] = right


def put_parts(x1, x2, x3, own, b_plane, p_plane, column, odd):
    nx = b_plane.shape[0]
    left, right = own[0], own[1]
    put_columns(x1, jnp.where(odd, left, right))
    put_planes(x1, b_plane, p_plane, column ^ 1)
    put_planes(x2, b_plane, p_plane, column ^ 2)
    inner = (column > 0) & (column < TILE_Y - 1)
    put_columns(x3, jnp.where(inner, jnp.where(odd, right, left), 0.0))
    put_planes(x3, b_plane, p_plane, column ^ 3)


def pack_rows_kernel(u, floor, ids, e1, e2, z1, z2, mrow, sem):
    g, m = floor.at[0], ids.at[0]
    group, column, odd, godd = place()
    nx = u.shape[1]
    nr, cx, width = g.shape
    low, high = g.at[:, 0, :], g.at[:, cx - 1, :]
    mrows = [
        pltpu.make_async_copy(m.at[:, r, :], mrow.at[s], sem.at[s]) for r, s in ((0, 0), (cx - 1, 1))
    ]
    for copy in mrows:
        copy.start()
    select_copy(odd, (u.at[:, nx - 1, :], e2), (u.at[:, 0, :], e2), sem.at[4])
    select_copy(godd, (low, z1.at[:nr]), (high, z1.at[:nr]), sem.at[2])
    select_copy(godd, (high, z2.at[:nr]), (low, z2.at[:nr]), sem.at[3])
    select_copy(odd, (u.at[:, 0, :], e1), (u.at[:, nx - 1, :], e1), sem.at[5])
    for copy in mrows:
        copy.wait()
    m_low, m_high = mrow[0].astype(F32) + 1.0, mrow[1].astype(F32) + 1.0
    z1[nr:, :] = jnp.where(godd, m_low, m_high)
    z2[nr:, :] = jnp.where(godd, m_high, m_low)
    wait_bytes(low, z1.at[:nr], sem.at[2])
    wait_bytes(low, z2.at[:nr], sem.at[3])
    wait_bytes(u.at[:, 0, :], e2, sem.at[4])

    @pl.when(alone())
    def _():
        e2[...] = jnp.zeros_like(e2)

    wait_bytes(u.at[:, 0, :], e1, sem.at[5])


def pack_columns_kernel(
    g, m, u, speeds, cond, x1, x2, x3, own, rates, halves, b_plane, own_m, speeds_v, cond_v, sem
):
    group, column, odd, godd = place()
    nr, cx, width = g.shape
    step = SUBL
    shift = LANES // 2
    small = (
        pltpu.make_async_copy(u.at[0], b_plane, sem.at[0]),
        pltpu.make_async_copy(speeds, speeds_v, sem.at[1]),
        pltpu.make_async_copy(cond, cond_v, sem.at[2]),
    )
    for copy in small:
        copy.start()
    own[...] = jnp.zeros_like(own)
    own_m[...] = jnp.zeros_like(own_m)

    def chunk(c, _):
        start = c * step
        for t in range(cx // SUBL):
            rs = slice(t * SUBL, (t + 1) * SUBL)

            def edges(ref):
                return lambda offset: (
                    ref[start + offset, rs, :LANES],
                    ref[start + offset, rs, width - LANES :],
                )

            keep_columns(own, 0, start, step, rs, edges(g))
            keep_columns(own_m, shift, start, step, rs, edges(m))
        return 0

    lax.fori_loop(0, nr // step, chunk, 0)
    is_k = lax.broadcasted_iota(jnp.int32, (cx, LANES), 1) >= shift
    for s in range(2):
        codes = pltpu.roll(own_m[s], s, 1)
        own[s, :, :] = jnp.where(is_k, codes.astype(F32) + 1.0, pltpu.roll(own[s], s, 1))
    for copy in small:
        copy.wait()
    put_parts(x1, x2, x3, own, b_plane, g.at[0], column, odd)
    zt = u.shape[0]
    diagonal = lax.broadcasted_iota(jnp.int32, (zt, zt), 0) == lax.broadcasted_iota(
        jnp.int32, (zt, zt), 1
    )
    for s in range(2):
        spread = jnp.where(diagonal, jnp.broadcast_to(speeds_v[s : s + 1, :], (zt, zt)), 0.0)
        along = jnp.sum(spread, axis=1, keepdims=True)
        rates[s, :, :] = jnp.broadcast_to(along, (zt, LANES))
    for i in range(halves.shape[0]):
        halves[i, :, :] = jnp.broadcast_to(0.5 * cond_v[0:1, i : i + 1], (SUBL, LANES))


def inner_kernel(m, g, halves, u, f, out, ce, cw, cn, cz, urows, frows, padded, kv, fzv, sem):
    nr, cx, width = m.shape
    nx = u.shape[1]
    picks = [
        (u.at[:, :, j * LANES : (j + 1) * LANES], padded.at[:, j, SUBL : SUBL + nx, :])
        for j in range(padded.shape[1])
    ]
    picks += [(u.at[:, r, :], urows.at[i]) for i, r in enumerate((0, 1, nx - 2, nx - 1))]
    picks += [(f.at[:, r, :], frows.at[i]) for i, r in enumerate((0, nx - 1))]
    picks = [pltpu.make_async_copy(a, b, sem.at[i]) for i, (a, b) in enumerate(picks)]
    for copy in picks:
        copy.start()
    rows, lanes = iotas()
    r_first, r_last = rows == 0, rows == SUBL - 1
    l_first, l_last = lanes == 0, lanes == LANES - 1
    tiles, wide = cx // SUBL, width // LANES
    spans = [slice(j * LANES, (j + 1) * LANES) for j in range(wide)]
    step = SUBL
    values = [halves[i] for i in range(halves.shape[0])]
    zero = jnp.zeros((SUBL, LANES), F32)

    def lookup(ids):
        value = values[0]
        for i in range(1, len(values)):
            value = jnp.where(ids == i, values[i], value)
        return value

    for t in range(tiles):
        rs = slice(t * SUBL, (t + 1) * SUBL)
        for at in spans:
            kv[0, rs, at] = lookup(m[0, rs, at])
    fzv[...] = jnp.zeros_like(fzv)
    turn = lambda vs, by, axis: [pltpu.roll(v, by, axis) for v in vs]

    def layer(start, offset):
        z = start + offset
        above, here, there = z + 1, offset % 2, (offset + 1) % 2
        last = offset == step - 1
        if last:
            above = jnp.minimum(above, nr - 1)
            scale = jnp.where(z + 1 < nr, 1.0, 0.0)

        def tile(t):
            rs = slice(t * SUBL, (t + 1) * SUBL)
            gs = [g[z, rs, at] for at in spans]
            ks = [kv[here, rs, at] for at in spans]
            return gs, ks, turn(gs, SUBL - 1, 0), turn(ks, SUBL - 1, 0)

        now = tile(0)
        prev = [zero] * wide
        for t in range(tiles):
            rs = slice(t * SUBL, (t + 1) * SUBL)
            gs, ks, g_up, k_up = now
            if t + 1 < tiles:
                now = tile(t + 1)
            ge, gw = turn(gs, LANES - 1, 1), turn(gs, 1, 1)
            ke, kw = turn(ks, LANES - 1, 1), turn(ks, 1, 1)
            for j, at in enumerate(spans):
                v, k = gs[j], ks[j]
                k_next, v_next = lookup(m[above, rs, at]), g[above, rs, at]
                if last:
                    k_next, v_next = scale * k_next, scale * v_next
                kv[there, rs, at] = k_next
                below = k + k_next
                if t + 1 < tiles:
                    north = k + jnp.where(r_last, now[3][j], k_up[j])
                    xp = jnp.where(r_last, now[2][j], g_up[j])
                else:
                    north, xp = jnp.where(r_last, 0.0, k + k_up[j]), g_up[j]
                if j + 1 < wide:
                    east = k + jnp.where(l_last, ke[j + 1], ke[j])
                    yp = jnp.where(l_last, ge[j + 1], ge[j])
                else:
                    east, yp = jnp.where(l_last, 0.0, k + ke[j]), ge[j]
                if j > 0:
                    west = k + jnp.where(l_first, kw[j - 1], kw[j])
                    ym = jnp.where(l_first, gw[j - 1], gw[j])
                else:
                    west, ym = jnp.where(l_first, 0.0, k + kw[j]), gw[j]
                ce[z, rs, at], cw[z, rs, at] = east, west
                cn[z, rs, at], cz[z, rs, at] = north, below
                fx = north * (xp - v)
                turned = pltpu.roll(fx, 1, 0)
                fxm = jnp.where(r_first, prev[j], turned)
                prev[j] = turned
                fz = below * (v_next - v)
                side = east * (yp - v) + west * (ym - v)
                out[z, rs, at] = v + ((fx - fxm) + side + (fz - fzv[rs, at]))
                fzv[rs, at] = fz

    def chunk(c, _):
        start = pl.multiple_of(c * step, SUBL)
        for offset in range(step):
            layer(start, offset)
        return 0

    lax.fori_loop(0, nr // step, chunk, 0)
    for copy in picks:
        copy.wait()


def floor_sides(halves, plane, x1, x2, x3, z1, z2, y1, y2, own, kc, kr, tcol, trow, bv):
    nr = kr.shape[1]
    nx, ny = plane.shape
    width = bv.shape[1]
    group, column, odd, godd = place()
    shift = LANES // 2
    groups = lax.axis_size("len") // TILE_Y
    known = (group ^ 1) < groups, jnp.where(godd, group + 1 < groups, group > 0)
    sides = []
    one, three = get_columns(x1), get_columns(x3)
    for s, halo in ((0, jnp.where(odd, one, three)), (1, jnp.where(odd, three, one))):
        if halves is not None:
            both = half_coded(own[s], halves) + half_coded(halo, halves)
            kc[s, :, :] = pltpu.roll(both, shift, 1)
        sides.append(kc[s] * (halo - own[s]))
    west, east = sides[0], pltpu.roll(sides[1], LANES - 1, 1)
    even = lax.broadcasted_iota(jnp.int32, west.shape, 1) % 2 == 0
    tcol[0, :, :], tcol[1, :, :] = jnp.where(even, west, east), jnp.where(even, east, west)
    for s, (mine, halo) in enumerate(((z1, y1), (z2, y2))):
        halo = jnp.where(known[s], halo[...], 0.0)
        if halves is not None:
            kr[s, :, :] = half_coded(mine[nr:, :], halves) + half_coded(halo[nr:, :], halves)
        side = kr[s] * (halo[:nr, :] - mine[:nr, :])
        trow[jnp.where(godd, s, 1 - s), :, :] = side
    row = lambda other: pl.ds(pl.multiple_of(other * nx, SUBL), nx)
    bv[row(column), :] = plane[:, pl.ds(pl.multiple_of(column * width, LANES), width)]
    for k, ref in ((1, x1), (2, x2), (3, x3)):
        bv[row(column ^ k), :] = ref[:nx, :]


def floor_kernel(
    g, ce, cw, cn, cz, plane, x1, x2, x3, z1, z2, y1, y2, own, kc, kr, out, ov, fzv, tcol, trow, bv, sem
):
    nr, cx, width = g.shape
    tiles, wide = cx // SUBL, width // LANES
    step = SUBL
    chunks = nr // step
    floor_sides(None, plane, x1, x2, x3, z1, z2, y1, y2, own, kc, kr, tcol, trow, bv)
    rows, lanes = iotas()
    r_first, r_last = rows == 0, rows == SUBL - 1
    l_first, l_last = lanes == 0, lanes == LANES - 1
    fzv[...] = jnp.zeros_like(fzv)
    spans = [slice(j * LANES, (j + 1) * LANES) for j in range(wide)]

    def layer(start, offset):
        z = start + offset
        back = lax.rem(LANES - z, LANES)
        above = z + 1
        if offset == step - 1:
            above = jnp.minimum(above, nr - 1)
            scale = jnp.where(z + 1 < nr, 1.0, 0.0)

        def tile(t):
            rs = slice(t * SUBL, (t + 1) * SUBL)
            gs = [g[z, rs, at] for at in spans]
            return gs, [pltpu.roll(v, SUBL - 1, 0) for v in gs]

        def row_of(s):
            block = trow[s, pl.ds(start, SUBL), :][offset : offset + 1]
            return [jnp.broadcast_to(block[:, at], (SUBL, LANES)) for at in spans]

        low, high = row_of(0), row_of(1)
        gs, ups = tile(0)
        prev = [-v for v in low]
        for t in range(tiles):
            rs = slice(t * SUBL, (t + 1) * SUBL)
            if t + 1 < tiles:
                gn, un = tile(t + 1)
            east = [pltpu.roll(v, LANES - 1, 1) for v in gs]
            west = [pltpu.roll(v, 1, 1) for v in gs]
            sides = pltpu.roll(tcol[offset % 2, rs, :], back, 1)
            for j, at in enumerate(spans):
                v = gs[j]
                if t + 1 < tiles:
                    fx = cn[z, rs, at] * (jnp.where(r_last, un[j], ups[j]) - v)
                else:
                    fx = jnp.where(r_last, high[j], cn[z, rs, at] * (ups[j] - v))
                turned = pltpu.roll(fx, 1, 0)
                fxm = jnp.where(r_first, prev[j], turned)
                prev[j] = turned
                yp = jnp.where(l_last, east[j + 1], east[j]) if j + 1 < wide else east[j]
                ym = jnp.where(l_first, west[j - 1], west[j]) if j > 0 else west[j]
                side = ce[z, rs, at] * (yp - v) + cw[z, rs, at] * (ym - v)
                if j == 0:
                    side = side + jnp.where(l_first, sides, 0.0)
                if j + 1 == wide:
                    side = side + jnp.where(l_last, sides, 0.0)
                nxt = g[above, rs, at]
                if offset == step - 1:
                    nxt = scale * nxt
                fz = cz[z, rs, at] * (nxt - v)
                total = v + ((fx - fxm) + side + (fz - fzv[rs, at]))
                fzv[rs, at] = fz
                ov[z, rs, at] = total
            if t + 1 < tiles:
                gs, ups = gn, un

    def store(c):
        at = pl.ds(c * step, step)
        return pltpu.make_async_copy(ov.at[at], out.at[at], sem.at[c])

    def chunk(c, _):
        start = pl.multiple_of(c * step, SUBL)
        for offset in range(step):
            layer(start, offset)

        @pl.when(c == 0)
        def _():
            ov[0, :, :] = ov[0] + HR * (bv[...] - g[0])

        store(c).start()
        return 0

    lax.fori_loop(0, chunks, chunk, 0)
    return [store(c) for c in range(chunks)]


def floor_scratch(dims):
    nr, cx, width = dims
    return [
        pltpu.VMEM((cx, width), F32),
        pltpu.VMEM((2, cx, LANES), F32),
        pltpu.VMEM((2, nr, width), F32),
        pltpu.VMEM((cx, width), F32),
        pltpu.SemaphoreType.DMA((3 * nr // SUBL,)),
    ]


def floor_finish(part, g, tcol, trow, bv, out, own, o1, o2, sem):
    nr, cx, width = g.shape
    godd = place()[3]
    rows, lanes = iotas()
    r_first, r_last = rows == 0, rows == SUBL - 1
    l_first, l_last = lanes == 0, lanes == LANES - 1
    tiles, wide = cx // SUBL, width // LANES
    spans = [slice(j * LANES, (j + 1) * LANES) for j in range(wide)]
    step = SUBL
    chunks = nr // step
    own[...] = jnp.zeros_like(own)

    def rows_of(c):
        at = pl.ds(pl.multiple_of(c * step, SUBL), step)
        low, high = out.at[at, 0, :], out.at[at, cx - 1, :]
        return low, high, o1.at[at], o2.at[at]

    def chunk(c, _):
        start = pl.multiple_of(c * step, SUBL)

        for offset in range(step):
            z = start + offset
            back = lax.rem(LANES - z, LANES)
            for t in range(tiles):
                rs = slice(t * SUBL, (t + 1) * SUBL)
                sides = pltpu.roll(tcol[offset % 2, rs, :], back, 1)
                for j, at in enumerate(spans):
                    v = part[z, rs, at]
                    if j == 0:
                        v = v + jnp.where(l_first, sides, 0.0)
                    if j + 1 == wide:
                        v = v + jnp.where(l_last, sides, 0.0)
                    for s, edge, mask in ((0, 0, r_first), (1, tiles - 1, r_last)):
                        if t == edge:
                            side = trow[s, pl.ds(start, SUBL), at][offset : offset + 1]
                            v = v + jnp.where(mask, jnp.broadcast_to(side, v.shape), 0.0)
                    out[z, rs, at] = v

        @pl.when(c == 0)
        def _():
            out[0, :, :] = out[0] + HR * (bv[...] - g[0])

        low, high, to1, to2 = rows_of(c)
        select_copy(godd, (low, to1), (high, to1), sem.at[c])
        select_copy(godd, (high, to2), (low, to2), sem.at[chunks + c])
        for t in range(tiles):
            rs = slice(t * SUBL, (t + 1) * SUBL)
            edges = lambda offset: (
                out[start + offset, rs, spans[0]],
                out[start + offset, rs, spans[-1]],
            )
            keep_columns(own, 0, start, step, rs, edges)
        return 0

    lax.fori_loop(0, chunks, chunk, 0)
    own[1, :, :] = pltpu.roll(own[1], 1, 1)
    copies = []
    for c in range(chunks):
        low, _, to1, to2 = rows_of(c)
        copies.append(pltpu.make_async_copy(low, to1, sem.at[c]))
        copies.append(pltpu.make_async_copy(low, to2, sem.at[chunks + c]))
    return copies


def fill_rows(padded, e1, e2, start):
    odd = place()[2]
    here = pl.ds(start, SUBL)
    for j in range(padded.shape[1]):
        at = slice(j * LANES, (j + 1) * LANES)
        one, two = e1[here, at], e2[here, at]
        for row, v in (
            (SUBL - 1, jnp.where(odd, one, two)),
            (padded.shape[2] - SUBL, jnp.where(odd, two, one)),
        ):
            for i in range(SUBL):
                padded[start + i, j, row : row + 1, :] = v[i : i + 1, :]


def tin_layer(padded, f, rates, start, offset, store):
    zt, wide, _, _ = padded.shape
    lanes = lax.broadcasted_iota(jnp.int32, (SUBL, LANES), 1)
    l_first, l_last = lanes == 0, lanes == LANES - 1
    tiles = f.shape[1] // SUBL
    zero = jnp.zeros((SUBL, LANES), F32)
    z = start + offset
    sx, sy = (
        jnp.broadcast_to(rates[s, pl.ds(start, SUBL), :][offset : offset + 1], (SUBL, LANES))
        for s in range(2)
    )
    centre = 1.0 - 6.0 * KT - sx - sy
    if offset == 0:
        centre = centre - jnp.where(z == 0, HT, 0.0)
    above, below = jnp.minimum(z + 1, zt - 1), jnp.maximum(z - 1, 0)

    def get(layer, t, j, by=0):
        return padded[layer, j, (t + 1) * SUBL + by : (t + 2) * SUBL + by, :]

    left = [zero] * tiles
    now = [get(z, t, 0) for t in range(tiles)]
    turned = [pltpu.roll(v, LANES - 1, 1) for v in now]
    for j in range(wide):
        at = slice(j * LANES, (j + 1) * LANES)
        if j + 1 < wide:
            nxt = [get(z, t, j + 1) for t in range(tiles)]
            nxt_turned = [pltpu.roll(v, LANES - 1, 1) for v in nxt]
        else:
            nxt, nxt_turned = None, [zero] * tiles
        for t in range(tiles):
            v, xm, xp = now[t], get(z, t, j, -1), get(z, t, j, 1)
            turn = pltpu.roll(v, 1, 1)
            ym = jnp.where(l_first, left[t], turn)
            yp = jnp.where(l_last, nxt_turned[t], turned[t])
            left[t] = turn
            code = f[z, t * SUBL : (t + 1) * SUBL, at]
            xs = jnp.where((code & 1) == 0, xm, xp)
            ys = jnp.where(code < 2, ym, yp)
            spread = (xm + xp) + (ym + yp) + (get(above, t, j) + get(below, t, j))
            store(t, j, (centre * v + KT * spread) + (sx * xs + sy * ys))
        now, turned = nxt, nxt_turned


def flat_store(ref):
    def store(t, j, value):
        ref[t * SUBL : (t + 1) * SUBL, j * LANES : (j + 1) * LANES] = value

    return store


def gather_floor_top(pv, x1, x2, x3, g):
    nx, ny = pv.shape
    width = x2.shape[1]
    column = place()[1]
    lanes_at = lambda other: pl.ds(pl.multiple_of(other * width, LANES), width)
    pv[:, lanes_at(column)] = g[0, pl.ds(pl.multiple_of(column * nx, SUBL), nx), :]
    for k, ref in ((1, x1), (2, x2), (3, x3)):
        pv[:, lanes_at(column ^ k)] = ref[nx : 2 * nx, :]


def tin_edge_kernel(
    padded_in, f, urows, frows, x1, x2, x3, e1, e2, g, rates, padded, o1, o2, plane, pv
):
    zt, nx, ny = f.shape
    odd, lonely = place()[2], alone()
    gather_floor_top(pv, x1, x2, x3, g)
    fill_rows(padded, e1, e2, 0)
    tin_layer(padded, f, rates, 0, 0, flat_store(plane))
    plane[...] = plane[...] + HT * pv[...]
    rows, lanes = iotas()
    r_first, r_last = rows == 0, rows == SUBL - 1
    l_first, l_last = lanes == 0, lanes == LANES - 1
    wide, blocks = ny // LANES, zt // SUBL
    zero = jnp.zeros((SUBL, LANES), F32)

    def block(b, _):
        start = pl.multiple_of(b * SUBL, SUBL)
        here = pl.ds(start, SUBL)
        before = pl.ds(pl.multiple_of(jnp.maximum(start - SUBL, 0), SUBL), SUBL)
        after = pl.ds(pl.multiple_of(jnp.minimum(start + SUBL, zt - SUBL), SUBL), SUBL)
        bottom, top = b == 0, b == blocks - 1
        sx, sy = rates[0, here, :], rates[1, here, :]
        contact = jnp.where(r_first & bottom, HT, 0.0)
        centre = 1.0 - 6.0 * KT - sx - sy - contact
        outs = []
        for s, side in ((0, 0), (1, nx - 1)):
            edge, inner = (3, 2) if s else (0, 1)
            vs = [urows[edge, here, j * LANES : (j + 1) * LANES] for j in range(wide)]
            east = [pltpu.roll(v, LANES - 1, 1) for v in vs] + [zero]
            west = [zero] + [pltpu.roll(v, 1, 1) for v in vs]
            for j in range(wide):
                at = slice(j * LANES, (j + 1) * LANES)
                v, code, inside = vs[j], frows[s, here, at], urows[inner, here, at]
                one, two = e1[here, at], e2[here, at]
                outside = jnp.where(odd, two, one) if s else jnp.where(odd, one, two)
                xm, xp = (inside, outside) if s else (outside, inside)
                ym = jnp.where(l_first, west[j], west[j + 1])
                yp = jnp.where(l_last, east[j + 1], east[j])
                above, below = urows[edge, after, at], urows[edge, before, at]
                above = jnp.where(top, pltpu.roll(v, 1, 0), above)
                below = jnp.where(bottom, pltpu.roll(v, SUBL - 1, 0), below)
                above = jnp.where(r_last, pltpu.roll(above, SUBL - 1, 0), pltpu.roll(v, SUBL - 1, 0))
                below = jnp.where(r_first, pltpu.roll(below, 1, 0), pltpu.roll(v, 1, 0))
                xs = jnp.where((code & 1) == 0, xm, xp)
                ys = jnp.where(code < 2, ym, yp)
                spread = (xm + xp) + (ym + yp) + (above + below)
                new = (centre * v + KT * spread) + (sx * xs + sy * ys)
                new = new + contact * jnp.broadcast_to(pv[side : side + 1, at], (SUBL, LANES))
                outs.append(new)
        for j in range(wide):
            at = slice(j * LANES, (j + 1) * LANES)
            low, high = outs[j], outs[wide + j]
            o1[here, at] = jnp.where(odd, low, high)
            o2[here, at] = jnp.where(lonely, 0.0, jnp.where(odd, high, low))
        return 0

    lax.fori_loop(0, blocks, block, 0)


def tin_edges(*arrays):
    padded, f, _, _, _, _, _, e1, e2, _, _ = arrays
    plane = f.shape[1:]
    return pl.pallas_call(
        tin_edge_kernel,
        out_shape=[shape(padded.shape), shape(e1.shape), shape(e2.shape), shape(plane)],
        in_specs=[VMEM] * 11,
        out_specs=[VMEM] * 4,
        input_output_aliases={0: 0},
        scratch_shapes=[pltpu.VMEM(plane, F32)],
        compiler_params=params(2),
        cost_estimate=cost(0, 4 << 20),
        name="tin_edges",
    )(*in_vmem(*arrays))


def floor_edge_kernel(
    b_plane, plane, x1, x2, x3, g, part, z1, z2, y1, y2, own, halves,
    ox1, ox2, ox3, g_new, own_new, oz1, oz2, kc, kr, tcol, trow, bv, sem
):
    group, column, odd, _ = place()
    floor_sides(halves, b_plane, x1, x2, x3, z1, z2, y1, y2, own, kc, kr, tcol, trow, bv)
    copies = floor_finish(part, g, tcol, trow, bv, g_new, own_new, oz1, oz2, sem)
    put_parts(ox1, ox2, ox3, own_new, plane, g_new.at[0], column, odd)
    for copy in copies:
        copy.wait()


def floor_edges(*arrays):
    _, _, x1, x2, x3, g, _, _, _, _, _, own, _ = arrays
    nr, cx, width = g.shape
    return pl.pallas_call(
        floor_edge_kernel,
        out_shape=[shape(v.shape) for v in (x1, x2, x3, g, own)]
        + [shape((nr, width))] * 2
        + [shape(own.shape), shape((2, nr, width))],
        in_specs=[VMEM] * 13,
        out_specs=[VMEM] * 9,
        scratch_shapes=floor_scratch(g.shape)[1:],
        compiler_params=params(2),
        cost_estimate=cost(0, 10 << 20),
        name="floor_edges",
    )(*in_vmem(*arrays))


def tin_first(padded, f, x1, x2, x3, e1, e2, g, rates):
    zt, wide, _, _ = padded.shape
    nx, step = f.shape[1], SUBL
    tiles = nx // SUBL

    def kernel(padded_in, f, x1, x2, x3, e1, e2, g, rates, padded, out, pv):
        gather_floor_top(pv, x1, x2, x3, g)

        def chunk(c, _):
            start = pl.multiple_of(c * step, SUBL)
            fill_rows(padded, e1, e2, start)
            for offset in range(step):

                def store(t, j, value):
                    out[start + offset, j, (t + 1) * SUBL : (t + 2) * SUBL, :] = value

                tin_layer(padded, f, rates, start, offset, store)
            return 0

        lax.fori_loop(0, zt // step, chunk, 0)
        for t in range(tiles):
            rs = slice((t + 1) * SUBL, (t + 2) * SUBL)
            for j in range(wide):
                top = pv[t * SUBL : (t + 1) * SUBL, j * LANES : (j + 1) * LANES]
                out[0, j, rs, :] = out[0, j, rs, :] + HT * top

    return pl.pallas_call(
        kernel,
        out_shape=[shape(padded.shape)] * 2,
        in_specs=[VMEM] * 9,
        out_specs=[VMEM] * 2,
        input_output_aliases={0: 0},
        scratch_shapes=[pltpu.VMEM((nx, wide * LANES), F32)],
        compiler_params=params(2),
        cost_estimate=cost(0, 20 << 20),
        name="tin_first",
    )(*in_vmem(padded, f, x1, x2, x3, e1, e2, g, rates))[1]


def tin_last(padded, f, e1, e2, pv, rates, out, ov, sem):
    zt, step = padded.shape[0], SUBL

    def store(c):
        at = pl.ds(c * step, step)
        return pltpu.make_async_copy(ov.at[at], out.at[at], sem.at[c])

    def chunk(c, _):
        start = pl.multiple_of(c * step, SUBL)
        fill_rows(padded, e1, e2, start)
        for offset in range(step):
            tin_layer(padded, f, rates, start, offset, flat_store(ov.at[start + offset]))

        @pl.when(c == 0)
        def _():
            ov[0, :, :] = ov[0] + HT * pv[...]

        store(c).start()
        return 0

    lax.fori_loop(0, zt // step, chunk, 0)
    return [store(c) for c in range(zt // step)]


def last_sweep(padded, f, plane, x1, x2, x3, e1, e2, g, rates, coefs, z1, z2, y1, y2, own, kc, kr):
    zt, wide, _, _ = padded.shape

    def kernel(
        padded_in, f, plane, x1, x2, x3, e1, e2, g, ce, cw, cn, cz, z1, z2, y1, y2, own, kc, kr, rates,
        padded, u_out, g_out, uv, gv, pv, sem, *scratch
    ):
        stores = floor_kernel(
            g, ce, cw, cn, cz, plane, x1, x2, x3, z1, z2, y1, y2, own, kc, kr, g_out, gv, *scratch
        )
        gather_floor_top(pv, x1, x2, x3, g)
        stores += tin_last(padded, f, e1, e2, pv, rates, u_out, uv, sem)
        for copy in stores:
            copy.wait()

    return pl.pallas_call(
        kernel,
        out_shape=[shape(padded.shape), far(f.shape), far(g.shape)],
        in_specs=[VMEM] * 21,
        out_specs=[VMEM, ANY, ANY],
        input_output_aliases={0: 0},
        scratch_shapes=[
            pltpu.VMEM(f.shape, F32),
            pltpu.VMEM(g.shape, F32),
            pltpu.VMEM(plane.shape, F32),
            pltpu.SemaphoreType.DMA((zt // SUBL,)),
        ]
        + floor_scratch(g.shape),
        compiler_params=params(10),
        cost_estimate=cost(0, 36 << 20),
        name="last_sweep",
    )(*in_vmem(padded, f, plane, x1, x2, x3, e1, e2, g, *coefs, z1, z2, y1, y2, own, kc, kr, rates))[1:]


def local(tin_temp, flow_code, speeds, floor_temp, material, conductivity):
    u, f, g, m = tin_temp, flow_code, floor_temp[0], material[0]
    zt, nx, ny = u.shape
    nr, cx, width = g.shape
    e1, e2, z1, z2 = pl.pallas_call(
        pack_rows_kernel,
        out_shape=[shape((zt, ny))] * 2 + [shape((2 * nr, width))] * 2,
        in_specs=[ANY] * 3,
        out_specs=[VMEM] * 4,
        scratch_shapes=[pltpu.VMEM((2, nr, width), jnp.int32), pltpu.SemaphoreType.DMA((6,))],
        compiler_params=params(2),
        cost_estimate=cost(0, 6 << 20),
        name="pack_rows",
    )(*in_hbm(u, floor_temp, material))
    e2, e1 = swap(e2, "e2"), swap(e1, "e1")
    y1, y2 = swap(z1, "z1"), swap(z2, "z2")
    x1, x2, x3, own, rates, halves, b_plane = pl.pallas_call(
        pack_columns_kernel,
        out_shape=[
            shape((cx, 2 * LANES)),
            shape((2 * nx, width)),
            shape((cx, 2 * LANES)),
            shape((2, cx, LANES)),
            shape((2, zt, LANES)),
            shape((conductivity.shape[0], SUBL, LANES)),
            shape((nx, ny)),
        ],
        in_specs=[VMEM] * 2 + [ANY] * 3,
        out_specs=[VMEM] * 7,
        scratch_shapes=[
            pltpu.VMEM((2, cx, LANES), jnp.int32),
            pltpu.VMEM(speeds.shape, F32),
            pltpu.VMEM((1, conductivity.shape[0]), F32),
            pltpu.SemaphoreType.DMA((3,)),
        ],
        compiler_params=params(2),
        cost_estimate=cost(0, 12 << 20),
        name="pack_columns",
    )(*in_vmem(g, m), *in_hbm(u, speeds, conductivity[None]))
    x1 = swap(x1, "e1")
    e1, x3 = lax.optimization_barrier((e1, x3))
    x1, x2 = lax.optimization_barrier((x1, x2))
    x2, x3 = swap(x2, "x2"), swap(x3, "x3")
    part, *coefs, urows, frows, padded = pl.pallas_call(
        inner_kernel,
        out_shape=[shape(g.shape)] * 5
        + [
            shape((4, zt, ny)),
            shape((2, zt, ny), jnp.int32),
            shape((zt, ny // LANES, nx + 2 * SUBL, LANES)),
        ],
        in_specs=[VMEM] * 3 + [ANY] * 2,
        out_specs=[VMEM] * 8,
        scratch_shapes=[
            pltpu.VMEM((2, cx, width), F32),
            pltpu.VMEM((cx, width), F32),
            pltpu.SemaphoreType.DMA((6 + ny // LANES,)),
        ],
        compiler_params=params(2),
        cost_estimate=cost(0, 24 << 20),
        name="inner",
    )(*in_vmem(m, g, halves), *in_hbm(u, f))
    rates, y1, y2 = lax.optimization_barrier((rates, y1, y2))
    padded, d1, d2, plane = tin_edges(
        padded, f, urows, frows, x1, x2, x3, e1, e2, g, rates
    )
    d1, d2 = swap(d1, "e1"), swap(d2, "e2")
    w1, w2, w3, g1, own1, z1, z2, kc, kr = floor_edges(
        b_plane, plane, x1, x2, x3, g, part, z1, z2, y1, y2, own, halves
    )
    w1 = swap(w1, "e1")
    d1, w3 = lax.optimization_barrier((d1, w3))
    w1, w2 = lax.optimization_barrier((w1, w2))
    w2, w3 = swap(w2, "x2"), swap(w3, "x3")
    y1, y2 = swap(z1, "z1"), swap(z2, "z2")
    u1 = tin_first(padded, f, x1, x2, x3, e1, e2, g, rates)
    u2, g2 = last_sweep(
        u1, f, plane, w1, w2, w3, d1, d2, g1, rates, coefs, z1, z2, y1, y2, own1, kc, kr
    )
    return u2, g2[None]


def solution(mesh):
    placed = (
        P(None, ("grp", "len"), None),
        P(None, ("grp", "len"), None),
        P(),
        P(("grp", "len"), None, None, None),
        P(("grp", "len"), None, None, None),
        P(),
    )
    return jax.shard_map(
        local,
        mesh=mesh,
        in_specs=placed,
        out_specs=(P(None, ("grp", "len"), None), P(("grp", "len"), None, None, None)),
        check_vma=False,
    )
```

```python
import functools

import jax
import jax.numpy as jnp
from jax import lax
from jax.experimental import pallas as pl
from jax.experimental.pallas import tpu as pltpu
from jax.sharding import PartitionSpec as P

TILE_Y = 4
KT = 0.1
HT = 0.2
HR = 0.2
LANES = 128
SUBL = 8
BODY = 16
F32 = jnp.float32
ANY = pl.BlockSpec(memory_space=pl.ANY)
VMEM = pl.BlockSpec(memory_space=pltpu.VMEM)


def params(mib):
    return pltpu.CompilerParams(vmem_limit_bytes=mib * 1024 * 1024)


def shape(dims, dtype=F32):
    return pltpu.VMEM(dims, dtype)


def far(dims, dtype=F32):
    return pltpu.HBM(dims, dtype)


def in_hbm(*arrays):
    return [pltpu.with_memory_space_constraint(a, pltpu.HBM) for a in arrays]


def in_vmem(*arrays):
    return [pltpu.with_memory_space_constraint(a, pltpu.VMEM) for a in arrays]


def cost(flops, nbytes):
    return pl.CostEstimate(flops=flops, bytes_accessed=nbytes, transcendentals=0)


def place():
    pos = lax.axis_index("len")
    group, column = pos // TILE_Y, pos % TILE_Y
    return group, column, pos % 2 == 1, group % 2 == 1


def alone():
    pos = lax.axis_index("len")
    return (pos == 0) | (pos == lax.axis_size("len") - 1)


def iotas():
    rows = lax.broadcasted_iota(jnp.int32, (SUBL, LANES), 0)
    lanes = lax.broadcasted_iota(jnp.int32, (SUBL, LANES), 1)
    return rows, lanes


def partner(kind, pos):
    return {
        "e1": lambda: pos ^ 1,
        "e2": lambda: pos + 1 if pos % 2 else pos - 1,
        "x2": lambda: pos ^ 2,
        "x3": lambda: pos ^ 3,
        "z1": lambda: pos ^ TILE_Y,
        "z2": lambda: pos + TILE_Y if (pos // TILE_Y) % 2 else pos - TILE_Y,
    }[kind]()


def swap(value, kind):
    count, parts = lax.axis_size("len"), lax.axis_size("grp")
    pairs = []
    for part in range(parts):
        for pos in range(count):
            to, other = part, partner(kind, pos)
            if not 0 <= other < count:
                to, other = (part ^ 1, pos) if kind == "e2" else (part, pos ^ 1)
            if 0 <= to < parts:
                pairs.append((part * count + pos, to * count + other))
    return lax.ppermute(value, ("grp", "len"), pairs)


def select_copy(cond, first, second, sem):
    @pl.when(cond)
    def _():
        pltpu.make_async_copy(*first, sem).start()

    @pl.when(jnp.logical_not(cond))
    def _():
        pltpu.make_async_copy(*second, sem).start()


def half_coded(codes, halves):
    value = jnp.zeros(codes.shape, F32)
    for i in range(halves.shape[0]):
        value = jnp.where(codes == i + 1.0, halves[i, 0:1, 0:1], value)
    return value


def wait_bytes(src, dst, sem):
    pltpu.make_async_copy(src, dst, sem).wait()


def put_columns(aux, cols):
    half = cols.shape[0] // 2
    aux[half:, :LANES] = cols[:half]
    aux[half:, LANES:] = cols[half:]


def get_columns(aux):
    half = aux.shape[0] // 2
    return jnp.concatenate([aux[half:, :LANES], aux[half:, LANES:]], 0)


def put_planes(dst, b_plane, p_plane, other):
    nx, width = b_plane.shape[0], p_plane.shape[1]
    lane = pl.multiple_of(other * width, LANES)
    row = pl.multiple_of(other * nx, SUBL)
    dst[:nx, :] = b_plane[:, pl.ds(lane, width)]
    dst[nx : 2 * nx, :] = p_plane[pl.ds(row, nx), :]


def keep_columns(own, slots, start, step, rs, edges):
    lanes = lax.broadcasted_iota(jnp.int32, (SUBL, LANES), 1)
    left, right = own[0, rs, :], own[1, rs, :]
    for offset in range(step):
        z = start + offset + slots
        first, last = edges(offset)
        both = pltpu.roll(jnp.where(lanes == 0, first, last), z, 1)
        left = jnp.where(lanes == z, both, left)
        right = jnp.where(lanes == lax.rem(z + LANES - 1, LANES), both, right)
    own[0, rs, :] = left
    own[1, rs, :] = right


def put_parts(x1, x2, x3, own, b_plane, p_plane, column, odd):
    nx = b_plane.shape[0]
    left, right = own[0], own[1]
    put_columns(x1, jnp.where(odd, left, right))
    put_planes(x1, b_plane, p_plane, column ^ 1)
    put_planes(x2, b_plane, p_plane, column ^ 2)
    inner = (column > 0) & (column < TILE_Y - 1)
    put_columns(x3, jnp.where(inner, jnp.where(odd, right, left), 0.0))
    put_planes(x3, b_plane, p_plane, column ^ 3)


def pack_rows_kernel(u, floor, ids, e1, e2, z1, z2, mrow, sem):
    g, m = floor.at[0], ids.at[0]
    group, column, odd, godd = place()
    nx = u.shape[1]
    nr, cx, width = g.shape
    low, high = g.at[:, 0, :], g.at[:, cx - 1, :]
    mrows = [
        pltpu.make_async_copy(m.at[:, r, :], mrow.at[s], sem.at[s]) for r, s in ((0, 0), (cx - 1, 1))
    ]
    for copy in mrows:
        copy.start()
    select_copy(odd, (u.at[:, nx - 1, :], e2), (u.at[:, 0, :], e2), sem.at[4])
    select_copy(godd, (low, z1.at[:nr]), (high, z1.at[:nr]), sem.at[2])
    select_copy(godd, (high, z2.at[:nr]), (low, z2.at[:nr]), sem.at[3])
    select_copy(odd, (u.at[:, 0, :], e1), (u.at[:, nx - 1, :], e1), sem.at[5])
    for copy in mrows:
        copy.wait()
    m_low, m_high = mrow[0].astype(F32) + 1.0, mrow[1].astype(F32) + 1.0
    z1[nr:, :] = jnp.where(godd, m_low, m_high)
    z2[nr:, :] = jnp.where(godd, m_high, m_low)
    wait_bytes(low, z1.at[:nr], sem.at[2])
    wait_bytes(low, z2.at[:nr], sem.at[3])
    wait_bytes(u.at[:, 0, :], e2, sem.at[4])

    @pl.when(alone())
    def _():
        e2[...] = jnp.zeros_like(e2)

    wait_bytes(u.at[:, 0, :], e1, sem.at[5])


def pack_columns_kernel(
    g, m, u, speeds, cond, x1, x2, x3, own, rates, halves, b_plane, own_m, speeds_v, cond_v, sem
):
    group, column, odd, godd = place()
    nr, cx, width = g.shape
    step = SUBL
    shift = LANES // 2
    small = (
        pltpu.make_async_copy(u.at[0], b_plane, sem.at[0]),
        pltpu.make_async_copy(speeds, speeds_v, sem.at[1]),
        pltpu.make_async_copy(cond, cond_v, sem.at[2]),
    )
    for copy in small:
        copy.start()
    own[...] = jnp.zeros_like(own)
    own_m[...] = jnp.zeros_like(own_m)

    def chunk(c, _):
        start = c * step
        for t in range(cx // SUBL):
            rs = slice(t * SUBL, (t + 1) * SUBL)

            def edges(ref):
                return lambda offset: (
                    ref[start + offset, rs, :LANES],
                    ref[start + offset, rs, width - LANES :],
                )

            keep_columns(own, 0, start, step, rs, edges(g))
            keep_columns(own_m, shift, start, step, rs, edges(m))
        return 0

    lax.fori_loop(0, nr // step, chunk, 0)
    is_k = lax.broadcasted_iota(jnp.int32, (cx, LANES), 1) >= shift
    for s in range(2):
        codes = pltpu.roll(own_m[s], s, 1)
        own[s, :, :] = jnp.where(is_k, codes.astype(F32) + 1.0, pltpu.roll(own[s], s, 1))
    for copy in small:
        copy.wait()
    put_parts(x1, x2, x3, own, b_plane, g.at[0], column, odd)
    zt = u.shape[0]
    diagonal = lax.broadcasted_iota(jnp.int32, (zt, zt), 0) == lax.broadcasted_iota(
        jnp.int32, (zt, zt), 1
    )
    for s in range(2):
        spread = jnp.where(diagonal, jnp.broadcast_to(speeds_v[s : s + 1, :], (zt, zt)), 0.0)
        along = jnp.sum(spread, axis=1, keepdims=True)
        rates[s, :, :] = jnp.broadcast_to(along, (zt, LANES))
    for i in range(halves.shape[0]):
        halves[i, :, :] = jnp.broadcast_to(0.5 * cond_v[0:1, i : i + 1], (SUBL, LANES))


def inner_kernel(m, g, halves, u, f, out, ce, cw, cn, cz, urows, frows, padded, kv, fzv, sem):
    nr, cx, width = m.shape
    nx = u.shape[1]
    picks = [
        (u.at[:, :, j * LANES : (j + 1) * LANES], padded.at[:, j, SUBL : SUBL + nx, :])
        for j in range(padded.shape[1])
    ]
    picks += [(u.at[:, r, :], urows.at[i]) for i, r in enumerate((0, 1, nx - 2, nx - 1))]
    picks += [(f.at[:, r, :], frows.at[i]) for i, r in enumerate((0, nx - 1))]
    picks = [pltpu.make_async_copy(a, b, sem.at[i]) for i, (a, b) in enumerate(picks)]
    for copy in picks:
        copy.start()
    rows, lanes = iotas()
    r_first, r_last = rows == 0, rows == SUBL - 1
    l_first, l_last = lanes == 0, lanes == LANES - 1
    tiles, wide = cx // SUBL, width // LANES
    spans = [slice(j * LANES, (j + 1) * LANES) for j in range(wide)]
    step = SUBL
    values = [halves[i] for i in range(halves.shape[0])]
    zero = jnp.zeros((SUBL, LANES), F32)

    def lookup(ids):
        value = values[0]
        for i in range(1, len(values)):
            value = jnp.where(ids == i, values[i], value)
        return value

    for t in range(tiles):
        rs = slice(t * SUBL, (t + 1) * SUBL)
        for at in spans:
            kv[0, rs, at] = lookup(m[0, rs, at])
    fzv[...] = jnp.zeros_like(fzv)
    turn = lambda vs, by, axis: [pltpu.roll(v, by, axis) for v in vs]

    def layer(start, offset):
        z = start + offset
        above, here, there = z + 1, offset % 2, (offset + 1) % 2
        last = offset == step - 1
        if last:
            above = jnp.minimum(above, nr - 1)
            scale = jnp.where(z + 1 < nr, 1.0, 0.0)

        def tile(t):
            rs = slice(t * SUBL, (t + 1) * SUBL)
            gs = [g[z, rs, at] for at in spans]
            ks = [kv[here, rs, at] for at in spans]
            return gs, ks, turn(gs, SUBL - 1, 0), turn(ks, SUBL - 1, 0)

        now = tile(0)
        prev = [zero] * wide
        for t in range(tiles):
            rs = slice(t * SUBL, (t + 1) * SUBL)
            gs, ks, g_up, k_up = now
            if t + 1 < tiles:
                now = tile(t + 1)
            ge, gw = turn(gs, LANES - 1, 1), turn(gs, 1, 1)
            ke, kw = turn(ks, LANES - 1, 1), turn(ks, 1, 1)
            for j, at in enumerate(spans):
                v, k = gs[j], ks[j]
                k_next, v_next = lookup(m[above, rs, at]), g[above, rs, at]
                if last:
                    k_next, v_next = scale * k_next, scale * v_next
                kv[there, rs, at] = k_next
                below = k + k_next
                if t + 1 < tiles:
                    north = k + jnp.where(r_last, now[3][j], k_up[j])
                    xp = jnp.where(r_last, now[2][j], g_up[j])
                else:
                    north, xp = jnp.where(r_last, 0.0, k + k_up[j]), g_up[j]
                if j + 1 < wide:
                    east = k + jnp.where(l_last, ke[j + 1], ke[j])
                    yp = jnp.where(l_last, ge[j + 1], ge[j])
                else:
                    east, yp = jnp.where(l_last, 0.0, k + ke[j]), ge[j]
                if j > 0:
                    west = k + jnp.where(l_first, kw[j - 1], kw[j])
                    ym = jnp.where(l_first, gw[j - 1], gw[j])
                else:
                    west, ym = jnp.where(l_first, 0.0, k + kw[j]), gw[j]
                ce[z, rs, at], cw[z, rs, at] = east, west
                cn[z, rs, at], cz[z, rs, at] = north, below
                fx = north * (xp - v)
                turned = pltpu.roll(fx, 1, 0)
                fxm = jnp.where(r_first, prev[j], turned)
                prev[j] = turned
                fz = below * (v_next - v)
                side = east * (yp - v) + west * (ym - v)
                out[z, rs, at] = v + ((fx - fxm) + side + (fz - fzv[rs, at]))
                fzv[rs, at] = fz

    def chunk(c, _):
        for block in range(BODY // step):
            start = pl.multiple_of(c * BODY + block * step, SUBL)
            for offset in range(step):
                layer(start, offset)
        return 0

    lax.fori_loop(0, nr // BODY, chunk, 0)
    for copy in picks:
        copy.wait()


def floor_sides(halves, plane, x1, x2, x3, z1, z2, y1, y2, own, kc, kr, tcol, trow, bv):
    nr = kr.shape[1]
    nx, ny = plane.shape
    width = bv.shape[1]
    group, column, odd, godd = place()
    shift = LANES // 2
    groups = lax.axis_size("len") // TILE_Y
    known = (group ^ 1) < groups, jnp.where(godd, group + 1 < groups, group > 0)
    sides = []
    one, three = get_columns(x1), get_columns(x3)
    for s, halo in ((0, jnp.where(odd, one, three)), (1, jnp.where(odd, three, one))):
        if halves is not None:
            both = half_coded(own[s], halves) + half_coded(halo, halves)
            kc[s, :, :] = pltpu.roll(both, shift, 1)
        sides.append(kc[s] * (halo - own[s]))
    west, east = sides[0], pltpu.roll(sides[1], LANES - 1, 1)
    even = lax.broadcasted_iota(jnp.int32, west.shape, 1) % 2 == 0
    tcol[0, :, :], tcol[1, :, :] = jnp.where(even, west, east), jnp.where(even, east, west)
    for s, (mine, halo) in enumerate(((z1, y1), (z2, y2))):
        halo = jnp.where(known[s], halo[...], 0.0)
        if halves is not None:
            kr[s, :, :] = half_coded(mine[nr:, :], halves) + half_coded(halo[nr:, :], halves)
        side = kr[s] * (halo[:nr, :] - mine[:nr, :])
        trow[jnp.where(godd, s, 1 - s), :, :] = side
    row = lambda other: pl.ds(pl.multiple_of(other * nx, SUBL), nx)
    bv[row(column), :] = plane[:, pl.ds(pl.multiple_of(column * width, LANES), width)]
    for k, ref in ((1, x1), (2, x2), (3, x3)):
        bv[row(column ^ k), :] = ref[:nx, :]


def floor_kernel(
    g, ce, cw, cn, cz, plane, x1, x2, x3, z1, z2, y1, y2, own, kc, kr, out, ov, fzv, tcol, trow, bv, sem
):
    nr, cx, width = g.shape
    tiles, wide = cx // SUBL, width // LANES
    step = SUBL
    chunks = nr // BODY
    floor_sides(None, plane, x1, x2, x3, z1, z2, y1, y2, own, kc, kr, tcol, trow, bv)
    rows, lanes = iotas()
    r_first, r_last = rows == 0, rows == SUBL - 1
    l_first, l_last = lanes == 0, lanes == LANES - 1
    fzv[...] = jnp.zeros_like(fzv)
    spans = [slice(j * LANES, (j + 1) * LANES) for j in range(wide)]

    def layer(start, offset):
        z = start + offset
        back = lax.rem(LANES - z, LANES)
        above = z + 1
        if offset == step - 1:
            above = jnp.minimum(above, nr - 1)
            scale = jnp.where(z + 1 < nr, 1.0, 0.0)

        def tile(t):
            rs = slice(t * SUBL, (t + 1) * SUBL)
            gs = [g[z, rs, at] for at in spans]
            return gs, [pltpu.roll(v, SUBL - 1, 0) for v in gs]

        def row_of(s):
            block = trow[s, pl.ds(start, SUBL), :][offset : offset + 1]
            return [jnp.broadcast_to(block[:, at], (SUBL, LANES)) for at in spans]

        low, high = row_of(0), row_of(1)
        gs, ups = tile(0)
        prev = [-v for v in low]
        for t in range(tiles):
            rs = slice(t * SUBL, (t + 1) * SUBL)
            if t + 1 < tiles:
                gn, un = tile(t + 1)
            east = [pltpu.roll(v, LANES - 1, 1) for v in gs]
            west = [pltpu.roll(v, 1, 1) for v in gs]
            sides = pltpu.roll(tcol[offset % 2, rs, :], back, 1)
            for j, at in enumerate(spans):
                v = gs[j]
                if t + 1 < tiles:
                    fx = cn[z, rs, at] * (jnp.where(r_last, un[j], ups[j]) - v)
                else:
                    fx = jnp.where(r_last, high[j], cn[z, rs, at] * (ups[j] - v))
                turned = pltpu.roll(fx, 1, 0)
                fxm = jnp.where(r_first, prev[j], turned)
                prev[j] = turned
                yp = jnp.where(l_last, east[j + 1], east[j]) if j + 1 < wide else east[j]
                ym = jnp.where(l_first, west[j - 1], west[j]) if j > 0 else west[j]
                side = ce[z, rs, at] * (yp - v) + cw[z, rs, at] * (ym - v)
                if j == 0:
                    side = side + jnp.where(l_first, sides, 0.0)
                if j + 1 == wide:
                    side = side + jnp.where(l_last, sides, 0.0)
                nxt = g[above, rs, at]
                if offset == step - 1:
                    nxt = scale * nxt
                fz = cz[z, rs, at] * (nxt - v)
                total = v + ((fx - fxm) + side + (fz - fzv[rs, at]))
                fzv[rs, at] = fz
                ov[z, rs, at] = total
            if t + 1 < tiles:
                gs, ups = gn, un

    def store(c):
        at = pl.ds(c * BODY, BODY)
        return pltpu.make_async_copy(ov.at[at], out.at[at], sem.at[c])

    def chunk(c, _):
        for block in range(BODY // step):
            start = pl.multiple_of(c * BODY + block * step, SUBL)
            for offset in range(step):
                layer(start, offset)

        @pl.when(c == 0)
        def _():
            ov[0, :, :] = ov[0] + HR * (bv[...] - g[0])

        store(c).start()
        return 0

    lax.fori_loop(0, chunks, chunk, 0)
    return [store(c) for c in range(chunks)]


def floor_scratch(dims):
    nr, cx, width = dims
    return [
        pltpu.VMEM((cx, width), F32),
        pltpu.VMEM((2, cx, LANES), F32),
        pltpu.VMEM((2, nr, width), F32),
        pltpu.VMEM((cx, width), F32),
        pltpu.SemaphoreType.DMA((3 * nr // SUBL,)),
    ]


def floor_finish(part, g, tcol, trow, bv, out, own, o1, o2):
    nr, cx, width = g.shape
    godd = place()[3]
    rows, lanes = iotas()
    r_first, r_last = rows == 0, rows == SUBL - 1
    l_first, l_last = lanes == 0, lanes == LANES - 1
    tiles, wide = cx // SUBL, width // LANES
    spans = [slice(j * LANES, (j + 1) * LANES) for j in range(wide)]
    step = SUBL
    chunks = nr // step
    own[...] = jnp.zeros_like(own)

    zero = jnp.zeros((SUBL, LANES), F32)

    def chunk(c, _):
        start = pl.multiple_of(c * step, SUBL)

        touch = jnp.where(c == 0, HR, 0.0)
        ends = [[zero] * wide, [zero] * wide]
        for offset in range(step):
            z = start + offset
            back = lax.rem(LANES - z, LANES)
            for t in range(tiles):
                rs = slice(t * SUBL, (t + 1) * SUBL)
                sides = pltpu.roll(tcol[offset % 2, rs, :], back, 1)
                for j, at in enumerate(spans):
                    v = part[z, rs, at]
                    if offset == 0:
                        v = v + touch * (bv[rs, at] - g[z, rs, at])
                    if j == 0:
                        v = v + jnp.where(l_first, sides, 0.0)
                    if j + 1 == wide:
                        v = v + jnp.where(l_last, sides, 0.0)
                    for s, edge, mask in ((0, 0, r_first), (1, tiles - 1, r_last)):
                        if t == edge:
                            side = trow[s, pl.ds(start, SUBL), at][offset : offset + 1]
                            v = v + jnp.where(mask, jnp.broadcast_to(side, v.shape), 0.0)
                            turned = pltpu.roll(v, offset + s, 0) if (offset + s) % SUBL else v
                            ends[s][j] = jnp.where(rows == offset, turned, ends[s][j])
                    out[z, rs, at] = v
        for t in range(tiles):
            rs = slice(t * SUBL, (t + 1) * SUBL)
            edges = lambda offset: (
                out[start + offset, rs, spans[0]],
                out[start + offset, rs, spans[-1]],
            )
            keep_columns(own, 0, start, step, rs, edges)
        for at, low, high in zip(spans, *ends):
            o1[pl.ds(start, step), at] = jnp.where(godd, low, high)
            o2[pl.ds(start, step), at] = jnp.where(godd, high, low)
        return 0

    lax.fori_loop(0, chunks, chunk, 0)
    own[1, :, :] = pltpu.roll(own[1], 1, 1)


def fill_rows(padded, e1, e2, start):
    odd = place()[2]
    here = pl.ds(start, SUBL)
    for j in range(padded.shape[1]):
        at = slice(j * LANES, (j + 1) * LANES)
        one, two = e1[here, at], e2[here, at]
        for row, v in (
            (SUBL - 1, jnp.where(odd, one, two)),
            (padded.shape[2] - SUBL, jnp.where(odd, two, one)),
        ):
            for i in range(SUBL):
                padded[start + i, j, row : row + 1, :] = v[i : i + 1, :]


def tin_layer(padded, f, rates, start, offset, store):
    zt, wide, _, _ = padded.shape
    lanes = lax.broadcasted_iota(jnp.int32, (SUBL, LANES), 1)
    l_first, l_last = lanes == 0, lanes == LANES - 1
    tiles = f.shape[1] // SUBL
    zero = jnp.zeros((SUBL, LANES), F32)
    z = start + offset
    sx, sy = (
        jnp.broadcast_to(rates[s, pl.ds(start, SUBL), :][offset : offset + 1], (SUBL, LANES))
        for s in range(2)
    )
    centre = 1.0 - 6.0 * KT - sx - sy
    if offset == 0:
        centre = centre - jnp.where(z == 0, HT, 0.0)
    above, below = jnp.minimum(z + 1, zt - 1), jnp.maximum(z - 1, 0)

    def get(layer, t, j, by=0):
        return padded[layer, j, (t + 1) * SUBL + by : (t + 2) * SUBL + by, :]

    left = [zero] * tiles
    now = [get(z, t, 0) for t in range(tiles)]
    turned = [pltpu.roll(v, LANES - 1, 1) for v in now]
    for j in range(wide):
        at = slice(j * LANES, (j + 1) * LANES)
        if j + 1 < wide:
            nxt = [get(z, t, j + 1) for t in range(tiles)]
            nxt_turned = [pltpu.roll(v, LANES - 1, 1) for v in nxt]
        else:
            nxt, nxt_turned = None, [zero] * tiles
        for t in range(tiles):
            v, xm, xp = now[t], get(z, t, j, -1), get(z, t, j, 1)
            turn = pltpu.roll(v, 1, 1)
            ym = jnp.where(l_first, left[t], turn)
            yp = jnp.where(l_last, nxt_turned[t], turned[t])
            left[t] = turn
            code = f[z, t * SUBL : (t + 1) * SUBL, at]
            xs = jnp.where((code & 1) == 0, xm, xp)
            ys = jnp.where(code < 2, ym, yp)
            spread = (xm + xp) + (ym + yp) + (get(above, t, j) + get(below, t, j))
            store(t, j, (centre * v + KT * spread) + (sx * xs + sy * ys))
        now, turned = nxt, nxt_turned


def flat_store(ref):
    def store(t, j, value):
        ref[t * SUBL : (t + 1) * SUBL, j * LANES : (j + 1) * LANES] = value

    return store


def gather_floor_top(pv, x1, x2, x3, g):
    nx, ny = pv.shape
    width = x2.shape[1]
    column = place()[1]
    lanes_at = lambda other: pl.ds(pl.multiple_of(other * width, LANES), width)
    pv[:, lanes_at(column)] = g[0, pl.ds(pl.multiple_of(column * nx, SUBL), nx), :]
    for k, ref in ((1, x1), (2, x2), (3, x3)):
        pv[:, lanes_at(column ^ k)] = ref[nx : 2 * nx, :]


def tin_edge_kernel(
    padded_in, f, urows, frows, x1, x2, x3, e1, e2, g, rates, padded, o1, o2, plane, pv
):
    zt, nx, ny = f.shape
    odd, lonely = place()[2], alone()
    gather_floor_top(pv, x1, x2, x3, g)
    fill_rows(padded, e1, e2, 0)
    tin_layer(padded, f, rates, 0, 0, flat_store(plane))
    plane[...] = plane[...] + HT * pv[...]
    rows, lanes = iotas()
    r_first, r_last = rows == 0, rows == SUBL - 1
    l_first, l_last = lanes == 0, lanes == LANES - 1
    wide, blocks = ny // LANES, zt // SUBL
    zero = jnp.zeros((SUBL, LANES), F32)

    def block(b, _):
        start = pl.multiple_of(b * SUBL, SUBL)
        here = pl.ds(start, SUBL)
        before = pl.ds(pl.multiple_of(jnp.maximum(start - SUBL, 0), SUBL), SUBL)
        after = pl.ds(pl.multiple_of(jnp.minimum(start + SUBL, zt - SUBL), SUBL), SUBL)
        bottom, top = b == 0, b == blocks - 1
        sx, sy = rates[0, here, :], rates[1, here, :]
        contact = jnp.where(r_first & bottom, HT, 0.0)
        centre = 1.0 - 6.0 * KT - sx - sy - contact
        outs = []
        for s, side in ((0, 0), (1, nx - 1)):
            edge, inner = (3, 2) if s else (0, 1)
            vs = [urows[edge, here, j * LANES : (j + 1) * LANES] for j in range(wide)]
            east = [pltpu.roll(v, LANES - 1, 1) for v in vs] + [zero]
            west = [zero] + [pltpu.roll(v, 1, 1) for v in vs]
            for j in range(wide):
                at = slice(j * LANES, (j + 1) * LANES)
                v, code, inside = vs[j], frows[s, here, at], urows[inner, here, at]
                one, two = e1[here, at], e2[here, at]
                outside = jnp.where(odd, two, one) if s else jnp.where(odd, one, two)
                xm, xp = (inside, outside) if s else (outside, inside)
                ym = jnp.where(l_first, west[j], west[j + 1])
                yp = jnp.where(l_last, east[j + 1], east[j])
                above, below = urows[edge, after, at], urows[edge, before, at]
                above = jnp.where(top, pltpu.roll(v, 1, 0), above)
                below = jnp.where(bottom, pltpu.roll(v, SUBL - 1, 0), below)
                above = jnp.where(r_last, pltpu.roll(above, SUBL - 1, 0), pltpu.roll(v, SUBL - 1, 0))
                below = jnp.where(r_first, pltpu.roll(below, 1, 0), pltpu.roll(v, 1, 0))
                xs = jnp.where((code & 1) == 0, xm, xp)
                ys = jnp.where(code < 2, ym, yp)
                spread = (xm + xp) + (ym + yp) + (above + below)
                new = (centre * v + KT * spread) + (sx * xs + sy * ys)
                new = new + contact * jnp.broadcast_to(pv[side : side + 1, at], (SUBL, LANES))
                outs.append(new)
        for j in range(wide):
            at = slice(j * LANES, (j + 1) * LANES)
            low, high = outs[j], outs[wide + j]
            o1[here, at] = jnp.where(odd, low, high)
            o2[here, at] = jnp.where(lonely, 0.0, jnp.where(odd, high, low))
        return 0

    lax.fori_loop(0, blocks, block, 0)


def tin_edges(*arrays):
    padded, f, _, _, _, _, _, e1, e2, _, _ = arrays
    plane = f.shape[1:]
    return pl.pallas_call(
        tin_edge_kernel,
        out_shape=[shape(padded.shape), shape(e1.shape), shape(e2.shape), shape(plane)],
        in_specs=[VMEM] * 11,
        out_specs=[VMEM] * 4,
        input_output_aliases={0: 0},
        scratch_shapes=[pltpu.VMEM(plane, F32)],
        compiler_params=params(2),
        cost_estimate=cost(0, 4 << 20),
        name="tin_edges",
    )(*in_vmem(*arrays))


def floor_edge_kernel(
    b_plane, plane, x1, x2, x3, g, part, z1, z2, y1, y2, own, halves,
    ox1, ox2, ox3, g_new, own_new, oz1, oz2, kc, kr, tcol, trow, bv
):
    group, column, odd, _ = place()
    floor_sides(halves, b_plane, x1, x2, x3, z1, z2, y1, y2, own, kc, kr, tcol, trow, bv)
    floor_finish(part, g, tcol, trow, bv, g_new, own_new, oz1, oz2)
    put_parts(ox1, ox2, ox3, own_new, plane, g_new.at[0], column, odd)


def floor_edges(*arrays):
    _, _, x1, x2, x3, g, _, _, _, _, _, own, _ = arrays
    nr, cx, width = g.shape
    return pl.pallas_call(
        floor_edge_kernel,
        out_shape=[shape(v.shape) for v in (x1, x2, x3, g, own)]
        + [shape((nr, width))] * 2
        + [shape(own.shape), shape((2, nr, width))],
        in_specs=[VMEM] * 13,
        out_specs=[VMEM] * 9,
        scratch_shapes=floor_scratch(g.shape)[1:-1],
        compiler_params=params(2),
        cost_estimate=cost(0, 10 << 20),
        name="floor_edges",
    )(*in_vmem(*arrays))


def tin_first(padded, f, x1, x2, x3, e1, e2, g, rates):
    zt, wide, _, _ = padded.shape
    nx, step = f.shape[1], SUBL
    tiles = nx // SUBL

    def kernel(padded_in, f, x1, x2, x3, e1, e2, g, rates, padded, out, pv):
        gather_floor_top(pv, x1, x2, x3, g)

        def chunk(c, _):
            for block in range(BODY // step):
                start = pl.multiple_of(c * BODY + block * step, SUBL)
                fill_rows(padded, e1, e2, start)
                for offset in range(step):

                    def store(t, j, value):
                        out[start + offset, j, (t + 1) * SUBL : (t + 2) * SUBL, :] = value

                    tin_layer(padded, f, rates, start, offset, store)
            return 0

        lax.fori_loop(0, zt // BODY, chunk, 0)
        for t in range(tiles):
            rs = slice((t + 1) * SUBL, (t + 2) * SUBL)
            for j in range(wide):
                top = pv[t * SUBL : (t + 1) * SUBL, j * LANES : (j + 1) * LANES]
                out[0, j, rs, :] = out[0, j, rs, :] + HT * top

    return pl.pallas_call(
        kernel,
        out_shape=[shape(padded.shape)] * 2,
        in_specs=[VMEM] * 9,
        out_specs=[VMEM] * 2,
        input_output_aliases={0: 0},
        scratch_shapes=[pltpu.VMEM((nx, wide * LANES), F32)],
        compiler_params=params(2),
        cost_estimate=cost(0, 20 << 20),
        name="tin_first",
    )(*in_vmem(padded, f, x1, x2, x3, e1, e2, g, rates))[1]


def tin_last(padded, f, e1, e2, pv, rates, out, ov, sem):
    zt, step = padded.shape[0], SUBL

    def store(c):
        at = pl.ds(c * BODY, BODY)
        return pltpu.make_async_copy(ov.at[at], out.at[at], sem.at[c])

    def chunk(c, _):
        for block in range(BODY // step):
            start = pl.multiple_of(c * BODY + block * step, SUBL)
            fill_rows(padded, e1, e2, start)
            for offset in range(step):
                tin_layer(padded, f, rates, start, offset, flat_store(ov.at[start + offset]))

        @pl.when(c == 0)
        def _():
            ov[0, :, :] = ov[0] + HT * pv[...]

        store(c).start()
        return 0

    lax.fori_loop(0, zt // BODY, chunk, 0)
    return [store(c) for c in range(zt // BODY)]


def last_sweep(padded, f, plane, x1, x2, x3, e1, e2, g, rates, coefs, z1, z2, y1, y2, own, kc, kr):
    zt, wide, _, _ = padded.shape

    def kernel(
        padded_in, f, plane, x1, x2, x3, e1, e2, g, ce, cw, cn, cz, z1, z2, y1, y2, own, kc, kr, rates,
        padded, u_out, g_out, uv, gv, pv, sem, *scratch
    ):
        stores = floor_kernel(
            g, ce, cw, cn, cz, plane, x1, x2, x3, z1, z2, y1, y2, own, kc, kr, g_out, gv, *scratch
        )
        gather_floor_top(pv, x1, x2, x3, g)
        stores += tin_last(padded, f, e1, e2, pv, rates, u_out, uv, sem)
        for copy in stores:
            copy.wait()

    return pl.pallas_call(
        kernel,
        out_shape=[shape(padded.shape), far(f.shape), far(g.shape)],
        in_specs=[VMEM] * 21,
        out_specs=[VMEM, ANY, ANY],
        input_output_aliases={0: 0},
        scratch_shapes=[
            pltpu.VMEM(f.shape, F32),
            pltpu.VMEM(g.shape, F32),
            pltpu.VMEM(plane.shape, F32),
            pltpu.SemaphoreType.DMA((zt // SUBL,)),
        ]
        + floor_scratch(g.shape),
        compiler_params=params(10),
        cost_estimate=cost(0, 36 << 20),
        name="last_sweep",
    )(*in_vmem(padded, f, plane, x1, x2, x3, e1, e2, g, *coefs, z1, z2, y1, y2, own, kc, kr, rates))[1:]


def local(tin_temp, flow_code, speeds, floor_temp, material, conductivity):
    u, f, g, m = tin_temp, flow_code, floor_temp[0], material[0]
    zt, nx, ny = u.shape
    nr, cx, width = g.shape
    e1, e2, z1, z2 = pl.pallas_call(
        pack_rows_kernel,
        out_shape=[shape((zt, ny))] * 2 + [shape((2 * nr, width))] * 2,
        in_specs=[ANY] * 3,
        out_specs=[VMEM] * 4,
        scratch_shapes=[pltpu.VMEM((2, nr, width), jnp.int32), pltpu.SemaphoreType.DMA((6,))],
        compiler_params=params(2),
        cost_estimate=cost(0, 6 << 20),
        name="pack_rows",
    )(*in_hbm(u, floor_temp, material))
    e2, e1 = swap(e2, "e2"), swap(e1, "e1")
    y1, y2 = swap(z1, "z1"), swap(z2, "z2")
    x1, x2, x3, own, rates, halves, b_plane = pl.pallas_call(
        pack_columns_kernel,
        out_shape=[
            shape((cx, 2 * LANES)),
            shape((2 * nx, width)),
            shape((cx, 2 * LANES)),
            shape((2, cx, LANES)),
            shape((2, zt, LANES)),
            shape((conductivity.shape[0], SUBL, LANES)),
            shape((nx, ny)),
        ],
        in_specs=[VMEM] * 2 + [ANY] * 3,
        out_specs=[VMEM] * 7,
        scratch_shapes=[
            pltpu.VMEM((2, cx, LANES), jnp.int32),
            pltpu.VMEM(speeds.shape, F32),
            pltpu.VMEM((1, conductivity.shape[0]), F32),
            pltpu.SemaphoreType.DMA((3,)),
        ],
        compiler_params=params(2),
        cost_estimate=cost(0, 12 << 20),
        name="pack_columns",
    )(*in_vmem(g, m), *in_hbm(u, speeds, conductivity[None]))
    x1 = swap(x1, "e1")
    e1, x3 = lax.optimization_barrier((e1, x3))
    x1, x2 = lax.optimization_barrier((x1, x2))
    x2, x3 = swap(x2, "x2"), swap(x3, "x3")
    part, *coefs, urows, frows, padded = pl.pallas_call(
        inner_kernel,
        out_shape=[shape(g.shape)] * 5
        + [
            shape((4, zt, ny)),
            shape((2, zt, ny), jnp.int32),
            shape((zt, ny // LANES, nx + 2 * SUBL, LANES)),
        ],
        in_specs=[VMEM] * 3 + [ANY] * 2,
        out_specs=[VMEM] * 8,
        scratch_shapes=[
            pltpu.VMEM((2, cx, width), F32),
            pltpu.VMEM((cx, width), F32),
            pltpu.SemaphoreType.DMA((6 + ny // LANES,)),
        ],
        compiler_params=params(2),
        cost_estimate=cost(0, 24 << 20),
        name="inner",
    )(*in_vmem(m, g, halves), *in_hbm(u, f))
    rates, y1, y2 = lax.optimization_barrier((rates, y1, y2))
    padded, d1, d2, plane = tin_edges(
        padded, f, urows, frows, x1, x2, x3, e1, e2, g, rates
    )
    d1, d2 = swap(d1, "e1"), swap(d2, "e2")
    w1, w2, w3, g1, own1, z1, z2, kc, kr = floor_edges(
        b_plane, plane, x1, x2, x3, g, part, z1, z2, y1, y2, own, halves
    )
    w1 = swap(w1, "e1")
    d1, w3 = lax.optimization_barrier((d1, w3))
    w1, w2 = lax.optimization_barrier((w1, w2))
    w2, w3 = swap(w2, "x2"), swap(w3, "x3")
    y1, y2 = swap(z1, "z1"), swap(z2, "z2")
    u1 = tin_first(padded, f, x1, x2, x3, e1, e2, g, rates)
    u2, g2 = last_sweep(
        u1, f, plane, w1, w2, w3, d1, d2, g1, rates, coefs, z1, z2, y1, y2, own1, kc, kr
    )
    return u2, g2[None]


def solution(mesh):
    placed = (
        P(None, ("grp", "len"), None),
        P(None, ("grp", "len"), None),
        P(),
        P(("grp", "len"), None, None, None),
        P(("grp", "len"), None, None, None),
        P(),
    )
    return jax.shard_map(
        local,
        mesh=mesh,
        in_specs=placed,
        out_specs=(P(None, ("grp", "len"), None), P(("grp", "len"), None, None, None)),
        check_vma=False,
    )
```

```python
import functools

import jax
import jax.numpy as jnp
from jax import lax
from jax.experimental import pallas as pl
from jax.experimental.pallas import tpu as pltpu
from jax.sharding import PartitionSpec as P

TILE_Y = 4
KT = 0.1
HT = 0.2
HR = 0.2
LANES = 128
SUBL = 8
BODY = 16
F32 = jnp.float32
ANY = pl.BlockSpec(memory_space=pl.ANY)
VMEM = pl.BlockSpec(memory_space=pltpu.VMEM)


def params(mib):
    return pltpu.CompilerParams(vmem_limit_bytes=mib * 1024 * 1024)


def shape(dims, dtype=F32):
    return pltpu.VMEM(dims, dtype)


def far(dims, dtype=F32):
    return pltpu.HBM(dims, dtype)


def in_hbm(*arrays):
    return [pltpu.with_memory_space_constraint(a, pltpu.HBM) for a in arrays]


def in_vmem(*arrays):
    return [pltpu.with_memory_space_constraint(a, pltpu.VMEM) for a in arrays]


def cost(flops, nbytes):
    return pl.CostEstimate(flops=flops, bytes_accessed=nbytes, transcendentals=0)


def place():
    pos = lax.axis_index("len")
    group, column = pos // TILE_Y, pos % TILE_Y
    return group, column, pos % 2 == 1, group % 2 == 1


def alone():
    pos = lax.axis_index("len")
    return (pos == 0) | (pos == lax.axis_size("len") - 1)


def iotas():
    rows = lax.broadcasted_iota(jnp.int32, (SUBL, LANES), 0)
    lanes = lax.broadcasted_iota(jnp.int32, (SUBL, LANES), 1)
    return rows, lanes


def partner(kind, pos):
    return {
        "e1": lambda: pos ^ 1,
        "e2": lambda: pos + 1 if pos % 2 else pos - 1,
        "x2": lambda: pos ^ 2,
        "x3": lambda: pos ^ 3,
        "z1": lambda: pos ^ TILE_Y,
        "z2": lambda: pos + TILE_Y if (pos // TILE_Y) % 2 else pos - TILE_Y,
    }[kind]()


def swap(value, kind):
    count, parts = lax.axis_size("len"), lax.axis_size("grp")
    pairs = []
    for part in range(parts):
        for pos in range(count):
            to, other = part, partner(kind, pos)
            if not 0 <= other < count:
                to, other = (part ^ 1, pos) if kind == "e2" else (part, pos ^ 1)
            if 0 <= to < parts:
                pairs.append((part * count + pos, to * count + other))
    return lax.ppermute(value, ("grp", "len"), pairs)


def select_copy(cond, first, second, sem):
    @pl.when(cond)
    def _():
        pltpu.make_async_copy(*first, sem).start()

    @pl.when(jnp.logical_not(cond))
    def _():
        pltpu.make_async_copy(*second, sem).start()


def half_coded(codes, halves):
    value = jnp.zeros(codes.shape, F32)
    for i in range(halves.shape[0]):
        value = jnp.where(codes == i + 1.0, halves[i, 0:1, 0:1], value)
    return value


def wait_bytes(src, dst, sem):
    pltpu.make_async_copy(src, dst, sem).wait()


def put_columns(aux, cols):
    half = cols.shape[0] // 2
    aux[half:, :LANES] = cols[:half]
    aux[half:, LANES:] = cols[half:]


def get_columns(aux):
    half = aux.shape[0] // 2
    return jnp.concatenate([aux[half:, :LANES], aux[half:, LANES:]], 0)


def put_planes(dst, b_plane, p_plane, other):
    nx, width = b_plane.shape[0], p_plane.shape[1]
    lane = pl.multiple_of(other * width, LANES)
    row = pl.multiple_of(other * nx, SUBL)
    dst[:nx, :] = b_plane[:, pl.ds(lane, width)]
    dst[nx : 2 * nx, :] = p_plane[pl.ds(row, nx), :]


def keep_columns(own, slots, start, step, rs, edges):
    lanes = lax.broadcasted_iota(jnp.int32, (SUBL, LANES), 1)
    left, right = own[0, rs, :], own[1, rs, :]
    for offset in range(step):
        z = start + offset + slots
        first, last = edges(offset)
        both = pltpu.roll(jnp.where(lanes == 0, first, last), z, 1)
        left = jnp.where(lanes == z, both, left)
        right = jnp.where(lanes == lax.rem(z + LANES - 1, LANES), both, right)
    own[0, rs, :] = left
    own[1, rs, :] = right


def put_parts(x1, x2, x3, own, b_plane, p_plane, column, odd):
    nx = b_plane.shape[0]
    left, right = own[0], own[1]
    put_columns(x1, jnp.where(odd, left, right))
    put_planes(x1, b_plane, p_plane, column ^ 1)
    put_planes(x2, b_plane, p_plane, column ^ 2)
    inner = (column > 0) & (column < TILE_Y - 1)
    put_columns(x3, jnp.where(inner, jnp.where(odd, right, left), 0.0))
    put_planes(x3, b_plane, p_plane, column ^ 3)


def pack_rows_kernel(u, floor, ids, e1, e2, z1, z2, mrow, sem):
    g, m = floor.at[0], ids.at[0]
    group, column, odd, godd = place()
    nx = u.shape[1]
    nr, cx, width = g.shape
    low, high = g.at[:, 0, :], g.at[:, cx - 1, :]
    mrows = [
        pltpu.make_async_copy(m.at[:, r, :], mrow.at[s], sem.at[s]) for r, s in ((0, 0), (cx - 1, 1))
    ]
    for copy in mrows:
        copy.start()
    select_copy(odd, (u.at[:, nx - 1, :], e2), (u.at[:, 0, :], e2), sem.at[4])
    select_copy(godd, (low, z1.at[:nr]), (high, z1.at[:nr]), sem.at[2])
    select_copy(godd, (high, z2.at[:nr]), (low, z2.at[:nr]), sem.at[3])
    select_copy(odd, (u.at[:, 0, :], e1), (u.at[:, nx - 1, :], e1), sem.at[5])
    for copy in mrows:
        copy.wait()
    m_low, m_high = mrow[0].astype(F32) + 1.0, mrow[1].astype(F32) + 1.0
    z1[nr:, :] = jnp.where(godd, m_low, m_high)
    z2[nr:, :] = jnp.where(godd, m_high, m_low)
    wait_bytes(low, z1.at[:nr], sem.at[2])
    wait_bytes(low, z2.at[:nr], sem.at[3])
    wait_bytes(u.at[:, 0, :], e2, sem.at[4])

    @pl.when(alone())
    def _():
        e2[...] = jnp.zeros_like(e2)

    wait_bytes(u.at[:, 0, :], e1, sem.at[5])


def pack_columns_kernel(
    g, m, u, speeds, cond, x1, x2, x3, own, rates, halves, b_plane, own_m, speeds_v, cond_v, sem
):
    group, column, odd, godd = place()
    nr, cx, width = g.shape
    step = SUBL
    shift = LANES // 2
    small = (
        pltpu.make_async_copy(u.at[0], b_plane, sem.at[0]),
        pltpu.make_async_copy(speeds, speeds_v, sem.at[1]),
        pltpu.make_async_copy(cond, cond_v, sem.at[2]),
    )
    for copy in small:
        copy.start()
    own[...] = jnp.zeros_like(own)
    own_m[...] = jnp.zeros_like(own_m)

    def chunk(c, _):
        for block in range(BODY // step):
            start = c * BODY + block * step
            for t in range(cx // SUBL):
                rs = slice(t * SUBL, (t + 1) * SUBL)

                def edges(ref):
                    return lambda offset: (
                        ref[start + offset, rs, :LANES],
                        ref[start + offset, rs, width - LANES :],
                    )

                keep_columns(own, 0, start, step, rs, edges(g))
                keep_columns(own_m, shift, start, step, rs, edges(m))
        return 0

    lax.fori_loop(0, nr // BODY, chunk, 0)
    is_k = lax.broadcasted_iota(jnp.int32, (cx, LANES), 1) >= shift
    for s in range(2):
        codes = pltpu.roll(own_m[s], s, 1)
        own[s, :, :] = jnp.where(is_k, codes.astype(F32) + 1.0, pltpu.roll(own[s], s, 1))
    for copy in small:
        copy.wait()
    put_parts(x1, x2, x3, own, b_plane, g.at[0], column, odd)
    zt = u.shape[0]
    diagonal = lax.broadcasted_iota(jnp.int32, (zt, zt), 0) == lax.broadcasted_iota(
        jnp.int32, (zt, zt), 1
    )
    for s in range(2):
        spread = jnp.where(diagonal, jnp.broadcast_to(speeds_v[s : s + 1, :], (zt, zt)), 0.0)
        along = jnp.sum(spread, axis=1, keepdims=True)
        rates[s, :, :] = jnp.broadcast_to(along, (zt, LANES))
    for i in range(halves.shape[0]):
        halves[i, :, :] = jnp.broadcast_to(0.5 * cond_v[0:1, i : i + 1], (SUBL, LANES))


def inner_kernel(m, g, halves, u, f, out, ce, cw, cn, cz, urows, frows, padded, kv, fzv, fxv, sem):
    nr, cx, width = m.shape
    nx = u.shape[1]
    picks = [
        (u.at[:, :, j * LANES : (j + 1) * LANES], padded.at[:, j, SUBL : SUBL + nx, :])
        for j in range(padded.shape[1])
    ]
    picks += [(u.at[:, r, :], urows.at[i]) for i, r in enumerate((0, 1, nx - 2, nx - 1))]
    picks += [(f.at[:, r, :], frows.at[i]) for i, r in enumerate((0, nx - 1))]
    picks = [pltpu.make_async_copy(a, b, sem.at[i]) for i, (a, b) in enumerate(picks)]
    for copy in picks:
        copy.start()
    rows, lanes = iotas()
    r_first, r_last = rows == 0, rows == SUBL - 1
    l_first, l_last = lanes == 0, lanes == LANES - 1
    tiles, wide = cx // SUBL, width // LANES
    spans = [slice(j * LANES, (j + 1) * LANES) for j in range(wide)]
    step = SUBL
    values = [halves[i] for i in range(halves.shape[0])]
    zero = jnp.zeros((SUBL, LANES), F32)

    def lookup(ids):
        value = values[0]
        for i in range(1, len(values)):
            value = jnp.where(ids == i, values[i], value)
        return value

    kv[...] = jnp.zeros_like(kv)
    fxv[...] = jnp.zeros_like(fxv)
    for t in range(tiles):
        rs = slice(t * SUBL, (t + 1) * SUBL)
        for j, at in enumerate(spans):
            kv[0, j, rs, :] = lookup(m[0, rs, at])
    fzv[...] = jnp.zeros_like(fzv)
    turn = lambda vs, by, axis: [pltpu.roll(v, by, axis) for v in vs]

    def layer(start, offset):
        z = start + offset
        above, here, there = z + 1, offset % 2, (offset + 1) % 2
        last = offset == step - 1
        if last:
            above = jnp.minimum(above, nr - 1)
            scale = jnp.where(z + 1 < nr, 1.0, 0.0)

        def tile(t):
            rs = slice(t * SUBL, (t + 1) * SUBL)
            gs = [g[z, rs, at] for at in spans]
            ks = [kv[here, j, rs, :] for j in range(wide)]
            return gs, ks, turn(gs, SUBL - 1, 0)

        now = tile(0)
        for t in range(tiles):
            rs = slice(t * SUBL, (t + 1) * SUBL)
            gs, ks, g_up = now
            if t + 1 < tiles:
                now = tile(t + 1)
            ge, gw = turn(gs, LANES - 1, 1), turn(gs, 1, 1)
            ke, kw = turn(ks, LANES - 1, 1), turn(ks, 1, 1)
            for j, at in enumerate(spans):
                v, k = gs[j], ks[j]
                k_next, v_next = lookup(m[above, rs, at]), g[above, rs, at]
                if last:
                    k_next, v_next = scale * k_next, scale * v_next
                kv[there, j, rs, :] = k_next
                below = k + k_next
                north = k + kv[here, j, t * SUBL + 1 : (t + 1) * SUBL + 1, :]
                if t + 1 < tiles:
                    xp = jnp.where(r_last, now[2][j], g_up[j])
                else:
                    north, xp = jnp.where(r_last, 0.0, north), g_up[j]
                if j + 1 < wide:
                    east = k + jnp.where(l_last, ke[j + 1], ke[j])
                    yp = jnp.where(l_last, ge[j + 1], ge[j])
                else:
                    east, yp = jnp.where(l_last, 0.0, k + ke[j]), ge[j]
                if j > 0:
                    west = k + jnp.where(l_first, kw[j - 1], kw[j])
                    ym = jnp.where(l_first, gw[j - 1], gw[j])
                else:
                    west, ym = jnp.where(l_first, 0.0, k + kw[j]), gw[j]
                ce[z, rs, at], cw[z, rs, at] = east, west
                cn[z, rs, at], cz[z, rs, at] = north, below
                fx = north * (xp - v)
                fxv[offset % 4, j, (t + 1) * SUBL : (t + 2) * SUBL, :] = fx
                fxm = fxv[offset % 4, j, (t + 1) * SUBL - 1 : (t + 2) * SUBL - 1, :]
                fz = below * (v_next - v)
                side = east * (yp - v) + west * (ym - v)
                out[z, rs, at] = v + ((fx - fxm) + side + (fz - fzv[rs, at]))
                fzv[rs, at] = fz

    def chunk(c, _):
        for block in range(BODY // step):
            start = pl.multiple_of(c * BODY + block * step, SUBL)
            for offset in range(step):
                layer(start, offset)
        return 0

    lax.fori_loop(0, nr // BODY, chunk, 0)
    for copy in picks:
        copy.wait()


def floor_sides(halves, plane, x1, x2, x3, z1, z2, y1, y2, own, kc, kr, tcol, trow, bv):
    nr = kr.shape[1]
    nx, ny = plane.shape
    width = bv.shape[1]
    group, column, odd, godd = place()
    shift = LANES // 2
    groups = lax.axis_size("len") // TILE_Y
    known = (group ^ 1) < groups, jnp.where(godd, group + 1 < groups, group > 0)
    sides = []
    one, three = get_columns(x1), get_columns(x3)
    for s, halo in ((0, jnp.where(odd, one, three)), (1, jnp.where(odd, three, one))):
        if halves is not None:
            both = half_coded(own[s], halves) + half_coded(halo, halves)
            kc[s, :, :] = pltpu.roll(both, shift, 1)
        sides.append(kc[s] * (halo - own[s]))
    west, east = sides[0], pltpu.roll(sides[1], LANES - 1, 1)
    even = lax.broadcasted_iota(jnp.int32, west.shape, 1) % 2 == 0
    tcol[0, :, :], tcol[1, :, :] = jnp.where(even, west, east), jnp.where(even, east, west)
    for s, (mine, halo) in enumerate(((z1, y1), (z2, y2))):
        halo = jnp.where(known[s], halo[...], 0.0)
        if halves is not None:
            kr[s, :, :] = half_coded(mine[nr:, :], halves) + half_coded(halo[nr:, :], halves)
        side = kr[s] * (halo[:nr, :] - mine[:nr, :])
        trow[jnp.where(godd, s, 1 - s), :, :] = side
    row = lambda other: pl.ds(pl.multiple_of(other * nx, SUBL), nx)
    bv[row(column), :] = plane[:, pl.ds(pl.multiple_of(column * width, LANES), width)]
    for k, ref in ((1, x1), (2, x2), (3, x3)):
        bv[row(column ^ k), :] = ref[:nx, :]


def floor_kernel(
    g, ce, cw, cn, cz, plane, x1, x2, x3, z1, z2, y1, y2, own, kc, kr, out, ov, fxv, fzv, tcol, trow, bv, sem
):
    nr, cx, width = g.shape
    tiles, wide = cx // SUBL, width // LANES
    step = SUBL
    chunks = nr // BODY
    floor_sides(None, plane, x1, x2, x3, z1, z2, y1, y2, own, kc, kr, tcol, trow, bv)
    rows, lanes = iotas()
    r_first, r_last = rows == 0, rows == SUBL - 1
    l_first, l_last = lanes == 0, lanes == LANES - 1
    fzv[...] = jnp.zeros_like(fzv)
    spans = [slice(j * LANES, (j + 1) * LANES) for j in range(wide)]

    def layer(start, offset):
        z = start + offset
        back = lax.rem(LANES - z, LANES)
        above = z + 1
        if offset == step - 1:
            above = jnp.minimum(above, nr - 1)
            scale = jnp.where(z + 1 < nr, 1.0, 0.0)

        def tile(t):
            rs = slice(t * SUBL, (t + 1) * SUBL)
            gs = [g[z, rs, at] for at in spans]
            return gs, [pltpu.roll(v, SUBL - 1, 0) for v in gs]

        def row_of(s):
            block = trow[s, pl.ds(start, SUBL), :][offset : offset + 1]
            return [jnp.broadcast_to(block[:, at], (SUBL, LANES)) for at in spans]

        low, high = row_of(0), row_of(1)
        gs, ups = tile(0)
        for t in range(tiles):
            rs = slice(t * SUBL, (t + 1) * SUBL)
            if t + 1 < tiles:
                gn, un = tile(t + 1)
            east = [pltpu.roll(v, LANES - 1, 1) for v in gs]
            west = [pltpu.roll(v, 1, 1) for v in gs]
            sides = pltpu.roll(tcol[offset % 2, rs, :], back, 1)
            for j, at in enumerate(spans):
                v = gs[j]
                if t + 1 < tiles:
                    fx = cn[z, rs, at] * (jnp.where(r_last, un[j], ups[j]) - v)
                else:
                    fx = jnp.where(r_last, high[j], cn[z, rs, at] * (ups[j] - v))
                fxv[offset % 4, j, (t + 1) * SUBL : (t + 2) * SUBL, :] = fx
                fxm = fxv[offset % 4, j, (t + 1) * SUBL - 1 : (t + 2) * SUBL - 1, :]
                if t == 0:
                    fxm = jnp.where(r_first, -low[j], fxm)
                yp = jnp.where(l_last, east[j + 1], east[j]) if j + 1 < wide else east[j]
                ym = jnp.where(l_first, west[j - 1], west[j]) if j > 0 else west[j]
                side = ce[z, rs, at] * (yp - v) + cw[z, rs, at] * (ym - v)
                if j == 0:
                    side = side + jnp.where(l_first, sides, 0.0)
                if j + 1 == wide:
                    side = side + jnp.where(l_last, sides, 0.0)
                nxt = g[above, rs, at]
                if offset == step - 1:
                    nxt = scale * nxt
                fz = cz[z, rs, at] * (nxt - v)
                total = v + ((fx - fxm) + side + (fz - fzv[rs, at]))
                fzv[rs, at] = fz
                ov[z, rs, at] = total
            if t + 1 < tiles:
                gs, ups = gn, un

    def store(c):
        at = pl.ds(c * BODY, BODY)
        return pltpu.make_async_copy(ov.at[at], out.at[at], sem.at[c])

    def chunk(c, _):
        for block in range(BODY // step):
            start = pl.multiple_of(c * BODY + block * step, SUBL)
            for offset in range(step):
                layer(start, offset)

        @pl.when(c == 0)
        def _():
            ov[0, :, :] = ov[0] + HR * (bv[...] - g[0])

        store(c).start()
        return 0

    lax.fori_loop(0, chunks, chunk, 0)
    return [store(c) for c in range(chunks)]


def floor_scratch(dims):
    nr, cx, width = dims
    return [
        pltpu.VMEM((cx, width), F32),
        pltpu.VMEM((2, cx, LANES), F32),
        pltpu.VMEM((2, nr, width), F32),
        pltpu.VMEM((cx, width), F32),
        pltpu.SemaphoreType.DMA((3 * nr // SUBL,)),
    ]


def floor_finish(part, g, tcol, trow, bv, out, own, o1, o2):
    nr, cx, width = g.shape
    godd = place()[3]
    rows, lanes = iotas()
    r_first, r_last = rows == 0, rows == SUBL - 1
    l_first, l_last = lanes == 0, lanes == LANES - 1
    tiles, wide = cx // SUBL, width // LANES
    spans = [slice(j * LANES, (j + 1) * LANES) for j in range(wide)]
    step = SUBL
    own[...] = jnp.zeros_like(own)

    zero = jnp.zeros((SUBL, LANES), F32)

    def block(start, first):

        if first is not None:
            touch = jnp.where(first, HR, 0.0)
        ends = [[zero] * wide, [zero] * wide]
        for offset in range(step):
            z = start + offset
            back = lax.rem(LANES - z, LANES)
            for t in range(tiles):
                rs = slice(t * SUBL, (t + 1) * SUBL)
                sides = pltpu.roll(tcol[offset % 2, rs, :], back, 1)
                for j, at in enumerate(spans):
                    v = part[z, rs, at]
                    if offset == 0 and first is not None:
                        v = v + touch * (bv[rs, at] - g[z, rs, at])
                    if j == 0:
                        v = v + jnp.where(l_first, sides, 0.0)
                    if j + 1 == wide:
                        v = v + jnp.where(l_last, sides, 0.0)
                    for s, edge, mask in ((0, 0, r_first), (1, tiles - 1, r_last)):
                        if t == edge:
                            side = trow[s, pl.ds(start, SUBL), at][offset : offset + 1]
                            v = v + jnp.where(mask, jnp.broadcast_to(side, v.shape), 0.0)
                            turned = pltpu.roll(v, offset + s, 0) if (offset + s) % SUBL else v
                            ends[s][j] = jnp.where(rows == offset, turned, ends[s][j])
                    out[z, rs, at] = v
        for t in range(tiles):
            rs = slice(t * SUBL, (t + 1) * SUBL)
            edges = lambda offset: (
                out[start + offset, rs, spans[0]],
                out[start + offset, rs, spans[-1]],
            )
            keep_columns(own, 0, start, step, rs, edges)
        for at, low, high in zip(spans, *ends):
            o1[pl.ds(start, step), at] = jnp.where(godd, low, high)
            o2[pl.ds(start, step), at] = jnp.where(godd, high, low)

    def chunk(c, _):
        for i in range(BODY // step):
            block(pl.multiple_of(c * BODY + i * step, SUBL), None if i else c == 0)
        return 0

    lax.fori_loop(0, nr // BODY, chunk, 0)
    own[1, :, :] = pltpu.roll(own[1], 1, 1)


def fill_rows(padded, e1, e2, start):
    odd = place()[2]
    here = pl.ds(start, SUBL)
    for j in range(padded.shape[1]):
        at = slice(j * LANES, (j + 1) * LANES)
        one, two = e1[here, at], e2[here, at]
        for row, v in (
            (SUBL - 1, jnp.where(odd, one, two)),
            (padded.shape[2] - SUBL, jnp.where(odd, two, one)),
        ):
            for i in range(SUBL):
                padded[start + i, j, row : row + 1, :] = v[i : i + 1, :]


def tin_layer(padded, f, rates, start, offset, store):
    zt, wide, _, _ = padded.shape
    lanes = lax.broadcasted_iota(jnp.int32, (SUBL, LANES), 1)
    l_first, l_last = lanes == 0, lanes == LANES - 1
    tiles = f.shape[1] // SUBL
    zero = jnp.zeros((SUBL, LANES), F32)
    z = start + offset
    sx, sy = (
        jnp.broadcast_to(rates[s, pl.ds(start, SUBL), :][offset : offset + 1], (SUBL, LANES))
        for s in range(2)
    )
    centre = 1.0 - 6.0 * KT - sx - sy
    if offset == 0:
        centre = centre - jnp.where(z == 0, HT, 0.0)
    above, below = jnp.minimum(z + 1, zt - 1), jnp.maximum(z - 1, 0)

    def get(layer, t, j, by=0):
        return padded[layer, j, (t + 1) * SUBL + by : (t + 2) * SUBL + by, :]

    left = [zero] * tiles
    now = [get(z, t, 0) for t in range(tiles)]
    turned = [pltpu.roll(v, LANES - 1, 1) for v in now]
    for j in range(wide):
        at = slice(j * LANES, (j + 1) * LANES)
        if j + 1 < wide:
            nxt = [get(z, t, j + 1) for t in range(tiles)]
            nxt_turned = [pltpu.roll(v, LANES - 1, 1) for v in nxt]
        else:
            nxt, nxt_turned = None, [zero] * tiles
        for t in range(tiles):
            v, xm, xp = now[t], get(z, t, j, -1), get(z, t, j, 1)
            turn = pltpu.roll(v, 1, 1)
            ym = jnp.where(l_first, left[t], turn)
            yp = jnp.where(l_last, nxt_turned[t], turned[t])
            left[t] = turn
            code = f[z, t * SUBL : (t + 1) * SUBL, at]
            xs = jnp.where((code & 1) == 0, xm, xp)
            ys = jnp.where(code < 2, ym, yp)
            spread = (xm + xp) + (ym + yp) + (get(above, t, j) + get(below, t, j))
            store(t, j, (centre * v + KT * spread) + (sx * xs + sy * ys))
        now, turned = nxt, nxt_turned


def flat_store(ref):
    def store(t, j, value):
        ref[t * SUBL : (t + 1) * SUBL, j * LANES : (j + 1) * LANES] = value

    return store


def gather_floor_top(pv, x1, x2, x3, g):
    nx, ny = pv.shape
    width = x2.shape[1]
    column = place()[1]
    lanes_at = lambda other: pl.ds(pl.multiple_of(other * width, LANES), width)
    pv[:, lanes_at(column)] = g[0, pl.ds(pl.multiple_of(column * nx, SUBL), nx), :]
    for k, ref in ((1, x1), (2, x2), (3, x3)):
        pv[:, lanes_at(column ^ k)] = ref[nx : 2 * nx, :]


def tin_edge_kernel(
    padded_in, f, urows, frows, x1, x2, x3, e1, e2, g, rates, padded, o1, o2, plane, pv
):
    zt, nx, ny = f.shape
    odd, lonely = place()[2], alone()
    gather_floor_top(pv, x1, x2, x3, g)
    fill_rows(padded, e1, e2, 0)
    tin_layer(padded, f, rates, 0, 0, flat_store(plane))
    plane[...] = plane[...] + HT * pv[...]
    rows, lanes = iotas()
    r_first, r_last = rows == 0, rows == SUBL - 1
    l_first, l_last = lanes == 0, lanes == LANES - 1
    wide, blocks = ny // LANES, zt // SUBL
    zero = jnp.zeros((SUBL, LANES), F32)

    def block(b, _):
        start = pl.multiple_of(b * SUBL, SUBL)
        here = pl.ds(start, SUBL)
        before = pl.ds(pl.multiple_of(jnp.maximum(start - SUBL, 0), SUBL), SUBL)
        after = pl.ds(pl.multiple_of(jnp.minimum(start + SUBL, zt - SUBL), SUBL), SUBL)
        bottom, top = b == 0, b == blocks - 1
        sx, sy = rates[0, here, :], rates[1, here, :]
        contact = jnp.where(r_first & bottom, HT, 0.0)
        centre = 1.0 - 6.0 * KT - sx - sy - contact
        outs = []
        for s, side in ((0, 0), (1, nx - 1)):
            edge, inner = (3, 2) if s else (0, 1)
            vs = [urows[edge, here, j * LANES : (j + 1) * LANES] for j in range(wide)]
            east = [pltpu.roll(v, LANES - 1, 1) for v in vs] + [zero]
            west = [zero] + [pltpu.roll(v, 1, 1) for v in vs]
            for j in range(wide):
                at = slice(j * LANES, (j + 1) * LANES)
                v, code, inside = vs[j], frows[s, here, at], urows[inner, here, at]
                one, two = e1[here, at], e2[here, at]
                outside = jnp.where(odd, two, one) if s else jnp.where(odd, one, two)
                xm, xp = (inside, outside) if s else (outside, inside)
                ym = jnp.where(l_first, west[j], west[j + 1])
                yp = jnp.where(l_last, east[j + 1], east[j])
                above, below = urows[edge, after, at], urows[edge, before, at]
                above = jnp.where(top, pltpu.roll(v, 1, 0), above)
                below = jnp.where(bottom, pltpu.roll(v, SUBL - 1, 0), below)
                above = jnp.where(r_last, pltpu.roll(above, SUBL - 1, 0), pltpu.roll(v, SUBL - 1, 0))
                below = jnp.where(r_first, pltpu.roll(below, 1, 0), pltpu.roll(v, 1, 0))
                xs = jnp.where((code & 1) == 0, xm, xp)
                ys = jnp.where(code < 2, ym, yp)
                spread = (xm + xp) + (ym + yp) + (above + below)
                new = (centre * v + KT * spread) + (sx * xs + sy * ys)
                new = new + contact * jnp.broadcast_to(pv[side : side + 1, at], (SUBL, LANES))
                outs.append(new)
        for j in range(wide):
            at = slice(j * LANES, (j + 1) * LANES)
            low, high = outs[j], outs[wide + j]
            o1[here, at] = jnp.where(odd, low, high)
            o2[here, at] = jnp.where(lonely, 0.0, jnp.where(odd, high, low))
        return 0

    lax.fori_loop(0, blocks, block, 0)


def tin_edges(*arrays):
    padded, f, _, _, _, _, _, e1, e2, _, _ = arrays
    plane = f.shape[1:]
    return pl.pallas_call(
        tin_edge_kernel,
        out_shape=[shape(padded.shape), shape(e1.shape), shape(e2.shape), shape(plane)],
        in_specs=[VMEM] * 11,
        out_specs=[VMEM] * 4,
        input_output_aliases={0: 0},
        scratch_shapes=[pltpu.VMEM(plane, F32)],
        compiler_params=params(2),
        cost_estimate=cost(0, 4 << 20),
        name="tin_edges",
    )(*in_vmem(*arrays))


def floor_edge_kernel(
    b_plane, plane, x1, x2, x3, g, part, z1, z2, y1, y2, own, halves,
    ox1, ox2, ox3, g_new, own_new, oz1, oz2, kc, kr, tcol, trow, bv
):
    group, column, odd, _ = place()
    floor_sides(halves, b_plane, x1, x2, x3, z1, z2, y1, y2, own, kc, kr, tcol, trow, bv)
    floor_finish(part, g, tcol, trow, bv, g_new, own_new, oz1, oz2)
    put_parts(ox1, ox2, ox3, own_new, plane, g_new.at[0], column, odd)


def floor_edges(*arrays):
    _, _, x1, x2, x3, g, _, _, _, _, _, own, _ = arrays
    nr, cx, width = g.shape
    return pl.pallas_call(
        floor_edge_kernel,
        out_shape=[shape(v.shape) for v in (x1, x2, x3, g, own)]
        + [shape((nr, width))] * 2
        + [shape(own.shape), shape((2, nr, width))],
        in_specs=[VMEM] * 13,
        out_specs=[VMEM] * 9,
        scratch_shapes=floor_scratch(g.shape)[1:-1],
        compiler_params=params(2),
        cost_estimate=cost(0, 10 << 20),
        name="floor_edges",
    )(*in_vmem(*arrays))


def tin_first(padded, f, x1, x2, x3, e1, e2, g, rates):
    zt, wide, _, _ = padded.shape
    nx, step = f.shape[1], SUBL
    tiles = nx // SUBL

    def kernel(padded_in, f, x1, x2, x3, e1, e2, g, rates, padded, out, pv):
        gather_floor_top(pv, x1, x2, x3, g)

        def chunk(c, _):
            for block in range(BODY // step):
                start = pl.multiple_of(c * BODY + block * step, SUBL)
                fill_rows(padded, e1, e2, start)
                for offset in range(step):

                    def store(t, j, value):
                        out[start + offset, j, (t + 1) * SUBL : (t + 2) * SUBL, :] = value

                    tin_layer(padded, f, rates, start, offset, store)
            return 0

        lax.fori_loop(0, zt // BODY, chunk, 0)
        for t in range(tiles):
            rs = slice((t + 1) * SUBL, (t + 2) * SUBL)
            for j in range(wide):
                top = pv[t * SUBL : (t + 1) * SUBL, j * LANES : (j + 1) * LANES]
                out[0, j, rs, :] = out[0, j, rs, :] + HT * top

    return pl.pallas_call(
        kernel,
        out_shape=[shape(padded.shape)] * 2,
        in_specs=[VMEM] * 9,
        out_specs=[VMEM] * 2,
        input_output_aliases={0: 0},
        scratch_shapes=[pltpu.VMEM((nx, wide * LANES), F32)],
        compiler_params=params(2),
        cost_estimate=cost(0, 20 << 20),
        name="tin_first",
    )(*in_vmem(padded, f, x1, x2, x3, e1, e2, g, rates))[1]


def tin_last(padded, f, e1, e2, pv, rates, out, ov, sem):
    zt, step = padded.shape[0], SUBL

    def store(c):
        at = pl.ds(c * BODY, BODY)
        return pltpu.make_async_copy(ov.at[at], out.at[at], sem.at[c])

    def chunk(c, _):
        for block in range(BODY // step):
            start = pl.multiple_of(c * BODY + block * step, SUBL)
            fill_rows(padded, e1, e2, start)
            for offset in range(step):
                tin_layer(padded, f, rates, start, offset, flat_store(ov.at[start + offset]))

        @pl.when(c == 0)
        def _():
            ov[0, :, :] = ov[0] + HT * pv[...]

        store(c).start()
        return 0

    lax.fori_loop(0, zt // BODY, chunk, 0)
    return [store(c) for c in range(zt // BODY)]


def last_sweep(padded, f, plane, x1, x2, x3, e1, e2, g, rates, coefs, z1, z2, y1, y2, own, kc, kr):
    zt, wide, _, _ = padded.shape

    def kernel(
        padded_in, f, plane, x1, x2, x3, e1, e2, g, ce, cw, cn, cz, z1, z2, y1, y2, own, kc, kr, rates,
        padded, u_out, g_out, uv, gv, pv, sem, *scratch
    ):
        stores = floor_kernel(
            g, ce, cw, cn, cz, plane, x1, x2, x3, z1, z2, y1, y2, own, kc, kr, g_out, gv, *scratch
        )
        gather_floor_top(pv, x1, x2, x3, g)
        stores += tin_last(padded, f, e1, e2, pv, rates, u_out, uv, sem)
        for copy in stores:
            copy.wait()

    return pl.pallas_call(
        kernel,
        out_shape=[shape(padded.shape), far(f.shape), far(g.shape)],
        in_specs=[VMEM] * 21,
        out_specs=[VMEM, ANY, ANY],
        input_output_aliases={0: 0},
        scratch_shapes=[
            pltpu.VMEM(f.shape, F32),
            pltpu.VMEM(g.shape, F32),
            pltpu.VMEM(plane.shape, F32),
            pltpu.SemaphoreType.DMA((zt // SUBL,)),
            pltpu.VMEM((4, g.shape[2] // LANES, g.shape[1] + SUBL, LANES), F32),
        ]
        + floor_scratch(g.shape),
        compiler_params=params(10),
        cost_estimate=cost(0, 36 << 20),
        name="last_sweep",
    )(*in_vmem(padded, f, plane, x1, x2, x3, e1, e2, g, *coefs, z1, z2, y1, y2, own, kc, kr, rates))[1:]


def local(tin_temp, flow_code, speeds, floor_temp, material, conductivity):
    u, f, g, m = tin_temp, flow_code, floor_temp[0], material[0]
    zt, nx, ny = u.shape
    nr, cx, width = g.shape
    e1, e2, z1, z2 = pl.pallas_call(
        pack_rows_kernel,
        out_shape=[shape((zt, ny))] * 2 + [shape((2 * nr, width))] * 2,
        in_specs=[ANY] * 3,
        out_specs=[VMEM] * 4,
        scratch_shapes=[pltpu.VMEM((2, nr, width), jnp.int32), pltpu.SemaphoreType.DMA((6,))],
        compiler_params=params(2),
        cost_estimate=cost(0, 6 << 20),
        name="pack_rows",
    )(*in_hbm(u, floor_temp, material))
    e2, e1 = swap(e2, "e2"), swap(e1, "e1")
    y1, y2 = swap(z1, "z1"), swap(z2, "z2")
    x1, x2, x3, own, rates, halves, b_plane = pl.pallas_call(
        pack_columns_kernel,
        out_shape=[
            shape((cx, 2 * LANES)),
            shape((2 * nx, width)),
            shape((cx, 2 * LANES)),
            shape((2, cx, LANES)),
            shape((2, zt, LANES)),
            shape((conductivity.shape[0], SUBL, LANES)),
            shape((nx, ny)),
        ],
        in_specs=[VMEM] * 2 + [ANY] * 3,
        out_specs=[VMEM] * 7,
        scratch_shapes=[
            pltpu.VMEM((2, cx, LANES), jnp.int32),
            pltpu.VMEM(speeds.shape, F32),
            pltpu.VMEM((1, conductivity.shape[0]), F32),
            pltpu.SemaphoreType.DMA((3,)),
        ],
        compiler_params=params(2),
        cost_estimate=cost(0, 12 << 20),
        name="pack_columns",
    )(*in_vmem(g, m), *in_hbm(u, speeds, conductivity[None]))
    x1 = swap(x1, "e1")
    e1, x3 = lax.optimization_barrier((e1, x3))
    x1, x2 = lax.optimization_barrier((x1, x2))
    x2, x3 = swap(x2, "x2"), swap(x3, "x3")
    part, *coefs, urows, frows, padded = pl.pallas_call(
        inner_kernel,
        out_shape=[shape(g.shape)] * 5
        + [
            shape((4, zt, ny)),
            shape((2, zt, ny), jnp.int32),
            shape((zt, ny // LANES, nx + 2 * SUBL, LANES)),
        ],
        in_specs=[VMEM] * 3 + [ANY] * 2,
        out_specs=[VMEM] * 8,
        scratch_shapes=[
            pltpu.VMEM((2, width // LANES, cx + SUBL, LANES), F32),
            pltpu.VMEM((cx, width), F32),
            pltpu.VMEM((4, width // LANES, cx + SUBL, LANES), F32),
            pltpu.SemaphoreType.DMA((6 + ny // LANES,)),
        ],
        compiler_params=params(2),
        cost_estimate=cost(0, 24 << 20),
        name="inner",
    )(*in_vmem(m, g, halves), *in_hbm(u, f))
    rates, y1, y2 = lax.optimization_barrier((rates, y1, y2))
    padded, d1, d2, plane = tin_edges(
        padded, f, urows, frows, x1, x2, x3, e1, e2, g, rates
    )
    d1, d2 = swap(d1, "e1"), swap(d2, "e2")
    w1, w2, w3, g1, own1, z1, z2, kc, kr = floor_edges(
        b_plane, plane, x1, x2, x3, g, part, z1, z2, y1, y2, own, halves
    )
    w1 = swap(w1, "e1")
    d1, w3 = lax.optimization_barrier((d1, w3))
    w1, z2 = lax.optimization_barrier((w1, z2))
    w2, w3 = swap(w2, "x2"), swap(w3, "x3")
    y1, y2 = swap(z1, "z1"), swap(z2, "z2")
    u1 = tin_first(padded, f, x1, x2, x3, e1, e2, g, rates)
    u2, g2 = last_sweep(
        u1, f, plane, w1, w2, w3, d1, d2, g1, rates, coefs, z1, z2, y1, y2, own1, kc, kr
    )
    return u2, g2[None]


def solution(mesh):
    placed = (
        P(None, ("grp", "len"), None),
        P(None, ("grp", "len"), None),
        P(),
        P(("grp", "len"), None, None, None),
        P(("grp", "len"), None, None, None),
        P(),
    )
    return jax.shard_map(
        local,
        mesh=mesh,
        in_specs=placed,
        out_specs=(P(None, ("grp", "len"), None), P(("grp", "len"), None, None, None)),
        check_vma=False,
    )
```

```python
import functools

import jax
import jax.numpy as jnp
from jax import lax
from jax.experimental import pallas as pl
from jax.experimental.pallas import tpu as pltpu
from jax.sharding import PartitionSpec as P

TILE_Y = 4
KT = 0.1
HT = 0.2
HR = 0.2
LANES = 128
SUBL = 8
BODY = 16
F32 = jnp.float32
ANY = pl.BlockSpec(memory_space=pl.ANY)
VMEM = pl.BlockSpec(memory_space=pltpu.VMEM)


def params(mib):
    return pltpu.CompilerParams(vmem_limit_bytes=mib * 1024 * 1024)


def shape(dims, dtype=F32):
    return pltpu.VMEM(dims, dtype)


def far(dims, dtype=F32):
    return pltpu.HBM(dims, dtype)


def in_hbm(*arrays):
    return [pltpu.with_memory_space_constraint(a, pltpu.HBM) for a in arrays]


def in_vmem(*arrays):
    return [pltpu.with_memory_space_constraint(a, pltpu.VMEM) for a in arrays]


def cost(flops, nbytes):
    return pl.CostEstimate(flops=flops, bytes_accessed=nbytes, transcendentals=0)


def place():
    pos = lax.axis_index("len")
    group, column = pos // TILE_Y, pos % TILE_Y
    return group, column, pos % 2 == 1, group % 2 == 1


def alone():
    pos = lax.axis_index("len")
    return (pos == 0) | (pos == lax.axis_size("len") - 1)


def iotas():
    rows = lax.broadcasted_iota(jnp.int32, (SUBL, LANES), 0)
    lanes = lax.broadcasted_iota(jnp.int32, (SUBL, LANES), 1)
    return rows, lanes


def partner(kind, pos):
    return {
        "e1": lambda: pos ^ 1,
        "e2": lambda: pos + 1 if pos % 2 else pos - 1,
        "x2": lambda: pos ^ 2,
        "x3": lambda: pos ^ 3,
        "z1": lambda: pos ^ TILE_Y,
        "z2": lambda: pos + TILE_Y if (pos // TILE_Y) % 2 else pos - TILE_Y,
    }[kind]()


def swap(value, kind):
    count, parts = lax.axis_size("len"), lax.axis_size("grp")
    pairs = []
    for part in range(parts):
        for pos in range(count):
            to, other = part, partner(kind, pos)
            if not 0 <= other < count:
                to, other = (part ^ 1, pos) if kind == "e2" else (part, pos ^ 1)
            if 0 <= to < parts:
                pairs.append((part * count + pos, to * count + other))
    return lax.ppermute(value, ("grp", "len"), pairs)


def select_copy(cond, first, second, sem):
    @pl.when(cond)
    def _():
        pltpu.make_async_copy(*first, sem).start()

    @pl.when(jnp.logical_not(cond))
    def _():
        pltpu.make_async_copy(*second, sem).start()


def half_coded(codes, halves):
    value = jnp.zeros(codes.shape, F32)
    for i in range(halves.shape[0]):
        value = jnp.where(codes == i + 1.0, halves[i, 0:1, 0:1], value)
    return value


def wait_bytes(src, dst, sem):
    pltpu.make_async_copy(src, dst, sem).wait()


def put_columns(aux, cols):
    half = cols.shape[0] // 2
    aux[half:, :LANES] = cols[:half]
    aux[half:, LANES:] = cols[half:]


def get_columns(aux):
    half = aux.shape[0] // 2
    return jnp.concatenate([aux[half:, :LANES], aux[half:, LANES:]], 0)


def put_planes(dst, b_plane, p_plane, other):
    nx, width = b_plane.shape[0], p_plane.shape[1]
    lane = pl.multiple_of(other * width, LANES)
    row = pl.multiple_of(other * nx, SUBL)
    dst[:nx, :] = b_plane[:, pl.ds(lane, width)]
    dst[nx : 2 * nx, :] = p_plane[pl.ds(row, nx), :]


def keep_columns(own, slots, start, step, rs, edges):
    lanes = lax.broadcasted_iota(jnp.int32, (SUBL, LANES), 1)
    left, right = own[0, rs, :], own[1, rs, :]
    for offset in range(step):
        z = start + offset + slots
        first, last = edges(offset)
        both = pltpu.roll(jnp.where(lanes == 0, first, last), z, 1)
        left = jnp.where(lanes == z, both, left)
        right = jnp.where(lanes == lax.rem(z + LANES - 1, LANES), both, right)
    own[0, rs, :] = left
    own[1, rs, :] = right


def put_parts(x1, x2, x3, own, b_plane, p_plane, column, odd):
    nx = b_plane.shape[0]
    left, right = own[0], own[1]
    put_columns(x1, jnp.where(odd, left, right))
    put_planes(x1, b_plane, p_plane, column ^ 1)
    put_planes(x2, b_plane, p_plane, column ^ 2)
    inner = (column > 0) & (column < TILE_Y - 1)
    put_columns(x3, jnp.where(inner, jnp.where(odd, right, left), 0.0))
    put_planes(x3, b_plane, p_plane, column ^ 3)


def pack_rows_kernel(u, floor, ids, e1, e2, z1, z2, mrow, sem):
    g, m = floor.at[0], ids.at[0]
    group, column, odd, godd = place()
    nx = u.shape[1]
    nr, cx, width = g.shape
    low, high = g.at[:, 0, :], g.at[:, cx - 1, :]
    mrows = [
        pltpu.make_async_copy(m.at[:, r, :], mrow.at[s], sem.at[s]) for r, s in ((0, 0), (cx - 1, 1))
    ]
    for copy in mrows:
        copy.start()
    select_copy(odd, (u.at[:, nx - 1, :], e2), (u.at[:, 0, :], e2), sem.at[4])
    select_copy(godd, (low, z1.at[:nr]), (high, z1.at[:nr]), sem.at[2])
    select_copy(godd, (high, z2.at[:nr]), (low, z2.at[:nr]), sem.at[3])
    select_copy(odd, (u.at[:, 0, :], e1), (u.at[:, nx - 1, :], e1), sem.at[5])
    for copy in mrows:
        copy.wait()
    m_low, m_high = mrow[0].astype(F32) + 1.0, mrow[1].astype(F32) + 1.0
    z1[nr:, :] = jnp.where(godd, m_low, m_high)
    z2[nr:, :] = jnp.where(godd, m_high, m_low)
    wait_bytes(low, z1.at[:nr], sem.at[2])
    wait_bytes(low, z2.at[:nr], sem.at[3])
    wait_bytes(u.at[:, 0, :], e2, sem.at[4])

    @pl.when(alone())
    def _():
        e2[...] = jnp.zeros_like(e2)

    wait_bytes(u.at[:, 0, :], e1, sem.at[5])


def pack_columns_kernel(
    g, m, u, speeds, cond, x1, x2, x3, own, rates, halves, b_plane, own_m, speeds_v, cond_v, sem
):
    group, column, odd, godd = place()
    nr, cx, width = g.shape
    step = SUBL
    shift = LANES // 2
    small = (
        pltpu.make_async_copy(u.at[0], b_plane, sem.at[0]),
        pltpu.make_async_copy(speeds, speeds_v, sem.at[1]),
        pltpu.make_async_copy(cond, cond_v, sem.at[2]),
    )
    for copy in small:
        copy.start()
    own[...] = jnp.zeros_like(own)
    own_m[...] = jnp.zeros_like(own_m)

    def chunk(c, _):
        for block in range(BODY // step):
            start = c * BODY + block * step
            for t in range(cx // SUBL):
                rs = slice(t * SUBL, (t + 1) * SUBL)

                def edges(ref):
                    return lambda offset: (
                        ref[start + offset, rs, :LANES],
                        ref[start + offset, rs, width - LANES :],
                    )

                keep_columns(own, 0, start, step, rs, edges(g))
                keep_columns(own_m, shift, start, step, rs, edges(m))
        return 0

    lax.fori_loop(0, nr // BODY, chunk, 0)
    is_k = lax.broadcasted_iota(jnp.int32, (cx, LANES), 1) >= shift
    for s in range(2):
        codes = pltpu.roll(own_m[s], s, 1)
        own[s, :, :] = jnp.where(is_k, codes.astype(F32) + 1.0, pltpu.roll(own[s], s, 1))
    for copy in small:
        copy.wait()
    put_parts(x1, x2, x3, own, b_plane, g.at[0], column, odd)
    zt = u.shape[0]
    diagonal = lax.broadcasted_iota(jnp.int32, (zt, zt), 0) == lax.broadcasted_iota(
        jnp.int32, (zt, zt), 1
    )
    for s in range(2):
        spread = jnp.where(diagonal, jnp.broadcast_to(speeds_v[s : s + 1, :], (zt, zt)), 0.0)
        along = jnp.sum(spread, axis=1, keepdims=True)
        rates[s, :, :] = jnp.broadcast_to(along, (zt, LANES))
    for i in range(halves.shape[0]):
        halves[i, :, :] = jnp.broadcast_to(0.5 * cond_v[0:1, i : i + 1], (SUBL, LANES))


def inner_kernel(m, g, halves, u, f, out, ce, cw, cn, cz, urows, frows, padded, kv, fzv, fxv, sem):
    nr, cx, width = m.shape
    nx = u.shape[1]
    picks = [
        (u.at[:, :, j * LANES : (j + 1) * LANES], padded.at[:, j, SUBL : SUBL + nx, :])
        for j in range(padded.shape[1])
    ]
    picks += [(u.at[:, r, :], urows.at[i]) for i, r in enumerate((0, 1, nx - 2, nx - 1))]
    picks += [(f.at[:, r, :], frows.at[i]) for i, r in enumerate((0, nx - 1))]
    picks = [pltpu.make_async_copy(a, b, sem.at[i]) for i, (a, b) in enumerate(picks)]
    for copy in picks:
        copy.start()
    rows, lanes = iotas()
    r_first, r_last = rows == 0, rows == SUBL - 1
    l_first, l_last = lanes == 0, lanes == LANES - 1
    tiles, wide = cx // SUBL, width // LANES
    spans = [slice(j * LANES, (j + 1) * LANES) for j in range(wide)]
    step = SUBL
    values = [halves[i] for i in range(halves.shape[0])]
    zero = jnp.zeros((SUBL, LANES), F32)

    def lookup(ids):
        value = values[0]
        for i in range(1, len(values)):
            value = jnp.where(ids == i, values[i], value)
        return value

    kv[...] = jnp.zeros_like(kv)
    fxv[...] = jnp.zeros_like(fxv)
    for t in range(tiles):
        rs = slice(t * SUBL, (t + 1) * SUBL)
        for j, at in enumerate(spans):
            kv[0, j, rs, :] = lookup(m[0, rs, at])
    fzv[...] = jnp.zeros_like(fzv)
    turn = lambda vs, by, axis: [pltpu.roll(v, by, axis) for v in vs]

    def layer(start, offset):
        z = start + offset
        above, here, there = z + 1, offset % 2, (offset + 1) % 2
        last = offset == step - 1
        if last:
            above = jnp.minimum(above, nr - 1)
            scale = jnp.where(z + 1 < nr, 1.0, 0.0)

        def tile(t):
            rs = slice(t * SUBL, (t + 1) * SUBL)
            gs = [g[z, rs, at] for at in spans]
            ks = [kv[here, j, rs, :] for j in range(wide)]
            return gs, ks, turn(gs, SUBL - 1, 0)

        now = tile(0)
        for t in range(tiles):
            rs = slice(t * SUBL, (t + 1) * SUBL)
            gs, ks, g_up = now
            if t + 1 < tiles:
                now = tile(t + 1)
            ge, gw = turn(gs, LANES - 1, 1), turn(gs, 1, 1)
            ke, kw = turn(ks, LANES - 1, 1), turn(ks, 1, 1)
            for j, at in enumerate(spans):
                v, k = gs[j], ks[j]
                k_next, v_next = lookup(m[above, rs, at]), g[above, rs, at]
                if last:
                    k_next, v_next = scale * k_next, scale * v_next
                kv[there, j, rs, :] = k_next
                below = k + k_next
                north = k + kv[here, j, t * SUBL + 1 : (t + 1) * SUBL + 1, :]
                if t + 1 < tiles:
                    xp = jnp.where(r_last, now[2][j], g_up[j])
                else:
                    north, xp = jnp.where(r_last, 0.0, north), g_up[j]
                if j + 1 < wide:
                    east = k + jnp.where(l_last, ke[j + 1], ke[j])
                    yp = jnp.where(l_last, ge[j + 1], ge[j])
                else:
                    east, yp = jnp.where(l_last, 0.0, k + ke[j]), ge[j]
                if j > 0:
                    west = k + jnp.where(l_first, kw[j - 1], kw[j])
                    ym = jnp.where(l_first, gw[j - 1], gw[j])
                else:
                    west, ym = jnp.where(l_first, 0.0, k + kw[j]), gw[j]
                ce[z, rs, at], cw[z, rs, at] = east, west
                cn[z, rs, at], cz[z, rs, at] = north, below
                fx = north * (xp - v)
                fxv[offset % 4, j, (t + 1) * SUBL : (t + 2) * SUBL, :] = fx
                fxm = fxv[offset % 4, j, (t + 1) * SUBL - 1 : (t + 2) * SUBL - 1, :]
                fz = below * (v_next - v)
                side = east * (yp - v) + west * (ym - v)
                out[z, rs, at] = v + ((fx - fxm) + side + (fz - fzv[rs, at]))
                fzv[rs, at] = fz

    def chunk(c, _):
        for block in range(BODY // step):
            start = pl.multiple_of(c * BODY + block * step, SUBL)
            for offset in range(step):
                layer(start, offset)
        return 0

    lax.fori_loop(0, nr // BODY, chunk, 0)
    for copy in picks:
        copy.wait()


def floor_sides(halves, plane, x1, x2, x3, z1, z2, y1, y2, own, kc, kr, tcol, trow, bv):
    nr = kr.shape[1]
    nx, ny = plane.shape
    width = bv.shape[1]
    group, column, odd, godd = place()
    shift = LANES // 2
    groups = lax.axis_size("len") // TILE_Y
    known = (group ^ 1) < groups, jnp.where(godd, group + 1 < groups, group > 0)
    sides = []
    one, three = get_columns(x1), get_columns(x3)
    for s, halo in ((0, jnp.where(odd, one, three)), (1, jnp.where(odd, three, one))):
        if halves is not None:
            both = half_coded(own[s], halves) + half_coded(halo, halves)
            kc[s, :, :] = pltpu.roll(both, shift, 1)
        sides.append(kc[s] * (halo - own[s]))
    west, east = sides[0], pltpu.roll(sides[1], LANES - 1, 1)
    even = lax.broadcasted_iota(jnp.int32, west.shape, 1) % 2 == 0
    tcol[0, :, :], tcol[1, :, :] = jnp.where(even, west, east), jnp.where(even, east, west)
    for s, (mine, halo) in enumerate(((z1, y1), (z2, y2))):
        halo = jnp.where(known[s], halo[...], 0.0)
        if halves is not None:
            kr[s, :, :] = half_coded(mine[nr:, :], halves) + half_coded(halo[nr:, :], halves)
        side = kr[s] * (halo[:nr, :] - mine[:nr, :])
        trow[jnp.where(godd, s, 1 - s), :, :] = side
    row = lambda other: pl.ds(pl.multiple_of(other * nx, SUBL), nx)
    bv[row(column), :] = plane[:, pl.ds(pl.multiple_of(column * width, LANES), width)]
    for k, ref in ((1, x1), (2, x2), (3, x3)):
        bv[row(column ^ k), :] = ref[:nx, :]


def floor_kernel(
    g, ce, cw, cn, cz, plane, x1, x2, x3, z1, z2, y1, y2, own, kc, kr, out, ov, fxv, fzv, tcol, trow, bv, sem
):
    nr, cx, width = g.shape
    tiles, wide = cx // SUBL, width // LANES
    step = SUBL
    chunks = nr // BODY
    floor_sides(None, plane, x1, x2, x3, z1, z2, y1, y2, own, kc, kr, tcol, trow, bv)
    rows, lanes = iotas()
    r_first, r_last = rows == 0, rows == SUBL - 1
    l_first, l_last = lanes == 0, lanes == LANES - 1
    fzv[...] = jnp.zeros_like(fzv)
    spans = [slice(j * LANES, (j + 1) * LANES) for j in range(wide)]

    def layer(start, offset):
        z = start + offset
        back = lax.rem(LANES - z, LANES)
        above = z + 1
        if offset == step - 1:
            above = jnp.minimum(above, nr - 1)
            scale = jnp.where(z + 1 < nr, 1.0, 0.0)

        def tile(t):
            rs = slice(t * SUBL, (t + 1) * SUBL)
            gs = [g[z, rs, at] for at in spans]
            return gs, [pltpu.roll(v, SUBL - 1, 0) for v in gs]

        def row_of(s):
            block = trow[s, pl.ds(start, SUBL), :][offset : offset + 1]
            return [jnp.broadcast_to(block[:, at], (SUBL, LANES)) for at in spans]

        low, high = row_of(0), row_of(1)
        gs, ups = tile(0)
        for t in range(tiles):
            rs = slice(t * SUBL, (t + 1) * SUBL)
            if t + 1 < tiles:
                gn, un = tile(t + 1)
            east = [pltpu.roll(v, LANES - 1, 1) for v in gs]
            west = [pltpu.roll(v, 1, 1) for v in gs]
            sides = pltpu.roll(tcol[offset % 2, rs, :], back, 1)
            for j, at in enumerate(spans):
                v = gs[j]
                if t + 1 < tiles:
                    fx = cn[z, rs, at] * (jnp.where(r_last, un[j], ups[j]) - v)
                else:
                    fx = jnp.where(r_last, high[j], cn[z, rs, at] * (ups[j] - v))
                fxv[offset % 4, j, (t + 1) * SUBL : (t + 2) * SUBL, :] = fx
                fxm = fxv[offset % 4, j, (t + 1) * SUBL - 1 : (t + 2) * SUBL - 1, :]
                if t == 0:
                    fxm = jnp.where(r_first, -low[j], fxm)
                yp = jnp.where(l_last, east[j + 1], east[j]) if j + 1 < wide else east[j]
                ym = jnp.where(l_first, west[j - 1], west[j]) if j > 0 else west[j]
                side = ce[z, rs, at] * (yp - v) + cw[z, rs, at] * (ym - v)
                if j == 0:
                    side = side + jnp.where(l_first, sides, 0.0)
                if j + 1 == wide:
                    side = side + jnp.where(l_last, sides, 0.0)
                nxt = g[above, rs, at]
                if offset == step - 1:
                    nxt = scale * nxt
                fz = cz[z, rs, at] * (nxt - v)
                total = v + ((fx - fxm) + side + (fz - fzv[rs, at]))
                fzv[rs, at] = fz
                ov[z, rs, at] = total
            if t + 1 < tiles:
                gs, ups = gn, un

    def store(c):
        at = pl.ds(c * BODY, BODY)
        return pltpu.make_async_copy(ov.at[at], out.at[at], sem.at[c])

    def chunk(c, _):
        for block in range(BODY // step):
            start = pl.multiple_of(c * BODY + block * step, SUBL)
            for offset in range(step):
                layer(start, offset)

        @pl.when(c == 0)
        def _():
            ov[0, :, :] = ov[0] + HR * (bv[...] - g[0])

        store(c).start()
        return 0

    lax.fori_loop(0, chunks, chunk, 0)
    return [store(c) for c in range(chunks)]


def floor_scratch(dims):
    nr, cx, width = dims
    return [
        pltpu.VMEM((cx, width), F32),
        pltpu.VMEM((2, cx, LANES), F32),
        pltpu.VMEM((2, nr, width), F32),
        pltpu.VMEM((cx, width), F32),
        pltpu.SemaphoreType.DMA((3 * nr // SUBL,)),
    ]


def floor_finish(part, g, tcol, trow, bv, out, own, o1, o2):
    nr, cx, width = g.shape
    godd = place()[3]
    rows, lanes = iotas()
    r_first, r_last = rows == 0, rows == SUBL - 1
    l_first, l_last = lanes == 0, lanes == LANES - 1
    tiles, wide = cx // SUBL, width // LANES
    spans = [slice(j * LANES, (j + 1) * LANES) for j in range(wide)]
    step = SUBL
    own[...] = jnp.zeros_like(own)

    zero = jnp.zeros((SUBL, LANES), F32)

    def block(start, first):

        if first is not None:
            touch = jnp.where(first, HR, 0.0)
        ends = [[zero] * wide, [zero] * wide]
        for offset in range(step):
            z = start + offset
            back = lax.rem(LANES - z, LANES)
            for t in range(tiles):
                rs = slice(t * SUBL, (t + 1) * SUBL)
                sides = pltpu.roll(tcol[offset % 2, rs, :], back, 1)
                for j, at in enumerate(spans):
                    v = part[z, rs, at]
                    if offset == 0 and first is not None:
                        v = v + touch * (bv[rs, at] - g[z, rs, at])
                    if j == 0:
                        v = v + jnp.where(l_first, sides, 0.0)
                    if j + 1 == wide:
                        v = v + jnp.where(l_last, sides, 0.0)
                    for s, edge, mask in ((0, 0, r_first), (1, tiles - 1, r_last)):
                        if t == edge:
                            side = trow[s, pl.ds(start, SUBL), at][offset : offset + 1]
                            v = v + jnp.where(mask, jnp.broadcast_to(side, v.shape), 0.0)
                            turned = pltpu.roll(v, offset + s, 0) if (offset + s) % SUBL else v
                            ends[s][j] = jnp.where(rows == offset, turned, ends[s][j])
                    out[z, rs, at] = v
        for t in range(tiles):
            rs = slice(t * SUBL, (t + 1) * SUBL)
            edges = lambda offset: (
                out[start + offset, rs, spans[0]],
                out[start + offset, rs, spans[-1]],
            )
            keep_columns(own, 0, start, step, rs, edges)
        for at, low, high in zip(spans, *ends):
            o1[pl.ds(start, step), at] = jnp.where(godd, low, high)
            o2[pl.ds(start, step), at] = jnp.where(godd, high, low)

    def chunk(c, _):
        for i in range(BODY // step):
            block(pl.multiple_of(c * BODY + i * step, SUBL), None if i else c == 0)
        return 0

    lax.fori_loop(0, nr // BODY, chunk, 0)
    own[1, :, :] = pltpu.roll(own[1], 1, 1)


def fill_rows(padded, e1, e2, start):
    odd = place()[2]
    here = pl.ds(start, SUBL)
    for j in range(padded.shape[1]):
        at = slice(j * LANES, (j + 1) * LANES)
        one, two = e1[here, at], e2[here, at]
        for row, v in (
            (SUBL - 1, jnp.where(odd, one, two)),
            (padded.shape[2] - SUBL, jnp.where(odd, two, one)),
        ):
            for i in range(SUBL):
                padded[start + i, j, row : row + 1, :] = v[i : i + 1, :]


def tin_layer(padded, f, rates, start, offset, store):
    zt, wide, _, _ = padded.shape
    lanes = lax.broadcasted_iota(jnp.int32, (SUBL, LANES), 1)
    l_first, l_last = lanes == 0, lanes == LANES - 1
    tiles = f.shape[1] // SUBL
    zero = jnp.zeros((SUBL, LANES), F32)
    z = start + offset
    sx, sy = (
        jnp.broadcast_to(rates[s, pl.ds(start, SUBL), :][offset : offset + 1], (SUBL, LANES))
        for s in range(2)
    )
    centre = 1.0 - 6.0 * KT - sx - sy
    if offset == 0:
        centre = centre - jnp.where(z == 0, HT, 0.0)
    above, below = jnp.minimum(z + 1, zt - 1), jnp.maximum(z - 1, 0)

    def get(layer, t, j, by=0):
        return padded[layer, j, (t + 1) * SUBL + by : (t + 2) * SUBL + by, :]

    left = [zero] * tiles
    now = [get(z, t, 0) for t in range(tiles)]
    turned = [pltpu.roll(v, LANES - 1, 1) for v in now]
    for j in range(wide):
        at = slice(j * LANES, (j + 1) * LANES)
        if j + 1 < wide:
            nxt = [get(z, t, j + 1) for t in range(tiles)]
            nxt_turned = [pltpu.roll(v, LANES - 1, 1) for v in nxt]
        else:
            nxt, nxt_turned = None, [zero] * tiles
        for t in range(tiles):
            v, xm, xp = now[t], get(z, t, j, -1), get(z, t, j, 1)
            turn = pltpu.roll(v, 1, 1)
            ym = jnp.where(l_first, left[t], turn)
            yp = jnp.where(l_last, nxt_turned[t], turned[t])
            left[t] = turn
            code = f[z, t * SUBL : (t + 1) * SUBL, at]
            xs = jnp.where((code & 1) == 0, xm, xp)
            ys = jnp.where(code < 2, ym, yp)
            spread = (xm + xp) + (ym + yp) + (get(above, t, j) + get(below, t, j))
            store(t, j, (centre * v + KT * spread) + (sx * xs + sy * ys))
        now, turned = nxt, nxt_turned


def flat_store(ref):
    def store(t, j, value):
        ref[t * SUBL : (t + 1) * SUBL, j * LANES : (j + 1) * LANES] = value

    return store


def gather_floor_top(pv, x1, x2, x3, g):
    nx, ny = pv.shape
    width = x2.shape[1]
    column = place()[1]
    lanes_at = lambda other: pl.ds(pl.multiple_of(other * width, LANES), width)
    pv[:, lanes_at(column)] = g[0, pl.ds(pl.multiple_of(column * nx, SUBL), nx), :]
    for k, ref in ((1, x1), (2, x2), (3, x3)):
        pv[:, lanes_at(column ^ k)] = ref[nx : 2 * nx, :]


def tin_edge_kernel(
    padded_in, f, urows, frows, x1, x2, x3, e1, e2, g, rates, padded, o1, o2, plane, pv
):
    zt, nx, ny = f.shape
    odd, lonely = place()[2], alone()
    gather_floor_top(pv, x1, x2, x3, g)
    fill_rows(padded, e1, e2, 0)
    tin_layer(padded, f, rates, 0, 0, flat_store(plane))
    plane[...] = plane[...] + HT * pv[...]
    rows, lanes = iotas()
    r_first, r_last = rows == 0, rows == SUBL - 1
    l_first, l_last = lanes == 0, lanes == LANES - 1
    wide, blocks = ny // LANES, zt // SUBL
    zero = jnp.zeros((SUBL, LANES), F32)

    def block(b, _):
        start = pl.multiple_of(b * SUBL, SUBL)
        here = pl.ds(start, SUBL)
        before = pl.ds(pl.multiple_of(jnp.maximum(start - SUBL, 0), SUBL), SUBL)
        after = pl.ds(pl.multiple_of(jnp.minimum(start + SUBL, zt - SUBL), SUBL), SUBL)
        bottom, top = b == 0, b == blocks - 1
        sx, sy = rates[0, here, :], rates[1, here, :]
        contact = jnp.where(r_first & bottom, HT, 0.0)
        centre = 1.0 - 6.0 * KT - sx - sy - contact
        outs = []
        for s, side in ((0, 0), (1, nx - 1)):
            edge, inner = (3, 2) if s else (0, 1)
            vs = [urows[edge, here, j * LANES : (j + 1) * LANES] for j in range(wide)]
            east = [pltpu.roll(v, LANES - 1, 1) for v in vs] + [zero]
            west = [zero] + [pltpu.roll(v, 1, 1) for v in vs]
            for j in range(wide):
                at = slice(j * LANES, (j + 1) * LANES)
                v, code, inside = vs[j], frows[s, here, at], urows[inner, here, at]
                one, two = e1[here, at], e2[here, at]
                outside = jnp.where(odd, two, one) if s else jnp.where(odd, one, two)
                xm, xp = (inside, outside) if s else (outside, inside)
                ym = jnp.where(l_first, west[j], west[j + 1])
                yp = jnp.where(l_last, east[j + 1], east[j])
                above, below = urows[edge, after, at], urows[edge, before, at]
                above = jnp.where(top, pltpu.roll(v, 1, 0), above)
                below = jnp.where(bottom, pltpu.roll(v, SUBL - 1, 0), below)
                above = jnp.where(r_last, pltpu.roll(above, SUBL - 1, 0), pltpu.roll(v, SUBL - 1, 0))
                below = jnp.where(r_first, pltpu.roll(below, 1, 0), pltpu.roll(v, 1, 0))
                xs = jnp.where((code & 1) == 0, xm, xp)
                ys = jnp.where(code < 2, ym, yp)
                spread = (xm + xp) + (ym + yp) + (above + below)
                new = (centre * v + KT * spread) + (sx * xs + sy * ys)
                new = new + contact * jnp.broadcast_to(pv[side : side + 1, at], (SUBL, LANES))
                outs.append(new)
        for j in range(wide):
            at = slice(j * LANES, (j + 1) * LANES)
            low, high = outs[j], outs[wide + j]
            o1[here, at] = jnp.where(odd, low, high)
            o2[here, at] = jnp.where(lonely, 0.0, jnp.where(odd, high, low))
        return 0

    def pair(i, _):
        return block(2 * i + 1, block(2 * i, 0))

    lax.fori_loop(0, blocks // 2, pair, 0)


def tin_edges(*arrays):
    padded, f, _, _, _, _, _, e1, e2, _, _ = arrays
    plane = f.shape[1:]
    return pl.pallas_call(
        tin_edge_kernel,
        out_shape=[shape(padded.shape), shape(e1.shape), shape(e2.shape), shape(plane)],
        in_specs=[VMEM] * 11,
        out_specs=[VMEM] * 4,
        input_output_aliases={0: 0},
        scratch_shapes=[pltpu.VMEM(plane, F32)],
        compiler_params=params(2),
        cost_estimate=cost(0, 4 << 20),
        name="tin_edges",
    )(*in_vmem(*arrays))


def floor_edge_kernel(
    b_plane, plane, x1, x2, x3, g, part, z1, z2, y1, y2, own, halves,
    ox1, ox2, ox3, g_new, own_new, oz1, oz2, kc, kr, tcol, trow, bv
):
    group, column, odd, _ = place()
    floor_sides(halves, b_plane, x1, x2, x3, z1, z2, y1, y2, own, kc, kr, tcol, trow, bv)
    floor_finish(part, g, tcol, trow, bv, g_new, own_new, oz1, oz2)
    put_parts(ox1, ox2, ox3, own_new, plane, g_new.at[0], column, odd)


def floor_edges(*arrays):
    _, _, x1, x2, x3, g, _, _, _, _, _, own, _ = arrays
    nr, cx, width = g.shape
    return pl.pallas_call(
        floor_edge_kernel,
        out_shape=[shape(v.shape) for v in (x1, x2, x3, g, own)]
        + [shape((nr, width))] * 2
        + [shape(own.shape), shape((2, nr, width))],
        in_specs=[VMEM] * 13,
        out_specs=[VMEM] * 9,
        scratch_shapes=floor_scratch(g.shape)[1:-1],
        compiler_params=params(2),
        cost_estimate=cost(0, 10 << 20),
        name="floor_edges",
    )(*in_vmem(*arrays))


def tin_first(padded, f, x1, x2, x3, e1, e2, g, rates):
    zt, wide, _, _ = padded.shape
    nx, step = f.shape[1], SUBL
    tiles = nx // SUBL

    def kernel(padded_in, f, x1, x2, x3, e1, e2, g, rates, padded, out, pv):
        gather_floor_top(pv, x1, x2, x3, g)

        def chunk(c, _):
            for block in range(BODY // step):
                start = pl.multiple_of(c * BODY + block * step, SUBL)
                fill_rows(padded, e1, e2, start)
                for offset in range(step):

                    def store(t, j, value):
                        out[start + offset, j, (t + 1) * SUBL : (t + 2) * SUBL, :] = value

                    tin_layer(padded, f, rates, start, offset, store)
            return 0

        lax.fori_loop(0, zt // BODY, chunk, 0)
        for t in range(tiles):
            rs = slice((t + 1) * SUBL, (t + 2) * SUBL)
            for j in range(wide):
                top = pv[t * SUBL : (t + 1) * SUBL, j * LANES : (j + 1) * LANES]
                out[0, j, rs, :] = out[0, j, rs, :] + HT * top

    return pl.pallas_call(
        kernel,
        out_shape=[shape(padded.shape)] * 2,
        in_specs=[VMEM] * 9,
        out_specs=[VMEM] * 2,
        input_output_aliases={0: 0},
        scratch_shapes=[pltpu.VMEM((nx, wide * LANES), F32)],
        compiler_params=params(2),
        cost_estimate=cost(0, 20 << 20),
        name="tin_first",
    )(*in_vmem(padded, f, x1, x2, x3, e1, e2, g, rates))[1]


def tin_last(padded, f, e1, e2, pv, rates, out, ov, sem):
    zt, step = padded.shape[0], SUBL

    def store(c):
        at = pl.ds(c * BODY, BODY)
        return pltpu.make_async_copy(ov.at[at], out.at[at], sem.at[c])

    def chunk(c, _):
        for block in range(BODY // step):
            start = pl.multiple_of(c * BODY + block * step, SUBL)
            fill_rows(padded, e1, e2, start)
            for offset in range(step):
                tin_layer(padded, f, rates, start, offset, flat_store(ov.at[start + offset]))

        @pl.when(c == 0)
        def _():
            ov[0, :, :] = ov[0] + HT * pv[...]

        store(c).start()
        return 0

    lax.fori_loop(0, zt // BODY, chunk, 0)
    return [store(c) for c in range(zt // BODY)]


def last_sweep(padded, f, plane, x1, x2, x3, e1, e2, g, rates, coefs, z1, z2, y1, y2, own, kc, kr):
    zt, wide, _, _ = padded.shape

    def kernel(
        padded_in, f, plane, x1, x2, x3, e1, e2, g, ce, cw, cn, cz, z1, z2, y1, y2, own, kc, kr, rates,
        padded, u_out, g_out, uv, gv, pv, sem, *scratch
    ):
        stores = floor_kernel(
            g, ce, cw, cn, cz, plane, x1, x2, x3, z1, z2, y1, y2, own, kc, kr, g_out, gv, *scratch
        )
        gather_floor_top(pv, x1, x2, x3, g)
        stores += tin_last(padded, f, e1, e2, pv, rates, u_out, uv, sem)
        for copy in stores:
            copy.wait()

    return pl.pallas_call(
        kernel,
        out_shape=[shape(padded.shape), far(f.shape), far(g.shape)],
        in_specs=[VMEM] * 21,
        out_specs=[VMEM, ANY, ANY],
        input_output_aliases={0: 0},
        scratch_shapes=[
            pltpu.VMEM(f.shape, F32),
            pltpu.VMEM(g.shape, F32),
            pltpu.VMEM(plane.shape, F32),
            pltpu.SemaphoreType.DMA((zt // SUBL,)),
            pltpu.VMEM((4, g.shape[2] // LANES, g.shape[1] + SUBL, LANES), F32),
        ]
        + floor_scratch(g.shape),
        compiler_params=params(10),
        cost_estimate=cost(0, 36 << 20),
        name="last_sweep",
    )(*in_vmem(padded, f, plane, x1, x2, x3, e1, e2, g, *coefs, z1, z2, y1, y2, own, kc, kr, rates))[1:]


def local(tin_temp, flow_code, speeds, floor_temp, material, conductivity):
    u, f, g, m = tin_temp, flow_code, floor_temp[0], material[0]
    zt, nx, ny = u.shape
    nr, cx, width = g.shape
    e1, e2, z1, z2 = pl.pallas_call(
        pack_rows_kernel,
        out_shape=[shape((zt, ny))] * 2 + [shape((2 * nr, width))] * 2,
        in_specs=[ANY] * 3,
        out_specs=[VMEM] * 4,
        scratch_shapes=[pltpu.VMEM((2, nr, width), jnp.int32), pltpu.SemaphoreType.DMA((6,))],
        compiler_params=params(2),
        cost_estimate=cost(0, 6 << 20),
        name="pack_rows",
    )(*in_hbm(u, floor_temp, material))
    e2, e1 = swap(e2, "e2"), swap(e1, "e1")
    y1, y2 = swap(z1, "z1"), swap(z2, "z2")
    x1, x2, x3, own, rates, halves, b_plane = pl.pallas_call(
        pack_columns_kernel,
        out_shape=[
            shape((cx, 2 * LANES)),
            shape((2 * nx, width)),
            shape((cx, 2 * LANES)),
            shape((2, cx, LANES)),
            shape((2, zt, LANES)),
            shape((conductivity.shape[0], SUBL, LANES)),
            shape((nx, ny)),
        ],
        in_specs=[VMEM] * 2 + [ANY] * 3,
        out_specs=[VMEM] * 7,
        scratch_shapes=[
            pltpu.VMEM((2, cx, LANES), jnp.int32),
            pltpu.VMEM(speeds.shape, F32),
            pltpu.VMEM((1, conductivity.shape[0]), F32),
            pltpu.SemaphoreType.DMA((3,)),
        ],
        compiler_params=params(2),
        cost_estimate=cost(0, 12 << 20),
        name="pack_columns",
    )(*in_vmem(g, m), *in_hbm(u, speeds, conductivity[None]))
    x1 = swap(x1, "e1")
    e1, x3 = lax.optimization_barrier((e1, x3))
    x1, x2 = lax.optimization_barrier((x1, x2))
    x2, x3 = swap(x2, "x2"), swap(x3, "x3")
    part, *coefs, urows, frows, padded = pl.pallas_call(
        inner_kernel,
        out_shape=[shape(g.shape)] * 5
        + [
            shape((4, zt, ny)),
            shape((2, zt, ny), jnp.int32),
            shape((zt, ny // LANES, nx + 2 * SUBL, LANES)),
        ],
        in_specs=[VMEM] * 3 + [ANY] * 2,
        out_specs=[VMEM] * 8,
        scratch_shapes=[
            pltpu.VMEM((2, width // LANES, cx + SUBL, LANES), F32),
            pltpu.VMEM((cx, width), F32),
            pltpu.VMEM((4, width // LANES, cx + SUBL, LANES), F32),
            pltpu.SemaphoreType.DMA((6 + ny // LANES,)),
        ],
        compiler_params=params(2),
        cost_estimate=cost(0, 24 << 20),
        name="inner",
    )(*in_vmem(m, g, halves), *in_hbm(u, f))
    rates, y1, y2 = lax.optimization_barrier((rates, y1, y2))
    padded, d1, d2, plane = tin_edges(
        padded, f, urows, frows, x1, x2, x3, e1, e2, g, rates
    )
    d1, d2 = swap(d1, "e1"), swap(d2, "e2")
    w1, w2, w3, g1, own1, z1, z2, kc, kr = floor_edges(
        b_plane, plane, x1, x2, x3, g, part, z1, z2, y1, y2, own, halves
    )
    w1 = swap(w1, "e1")
    d1, w3 = lax.optimization_barrier((d1, w3))
    w1, z1, z2 = lax.optimization_barrier((w1, z1, z2))
    w2, w3 = swap(w2, "x2"), swap(w3, "x3")
    y1, y2 = swap(z1, "z1"), swap(z2, "z2")
    u1 = tin_first(padded, f, x1, x2, x3, e1, e2, g, rates)
    u2, g2 = last_sweep(
        u1, f, plane, w1, w2, w3, d1, d2, g1, rates, coefs, z1, z2, y1, y2, own1, kc, kr
    )
    return u2, g2[None]


def solution(mesh):
    placed = (
        P(None, ("grp", "len"), None),
        P(None, ("grp", "len"), None),
        P(),
        P(("grp", "len"), None, None, None),
        P(("grp", "len"), None, None, None),
        P(),
    )
    return jax.shard_map(
        local,
        mesh=mesh,
        in_specs=placed,
        out_specs=(P(None, ("grp", "len"), None), P(("grp", "len"), None, None, None)),
        check_vma=False,
    )
```
